128 devices in a mesh: fsdp: 32 (over y, z_lo, x), ctx: 2 (over core), tp: 2 (over z_hi).
Axes of the slice: x: 4, y: 4, z: 4 (z_hi: 2, z_lo: 2; z = z_hi * 2 + z_lo), core: 2. Of those that a mesh axis runs over, the one named last changes fastest.
Arguments:
- tokens: bfloat16 [8192, 768], P(('fsdp', 'ctx')), may hold values from -6 to 6
- cotangent: bfloat16 [8192, 768], P(('fsdp', 'ctx')), may hold values from -16 to 16
- doc_lens: int32 [32, 4], P('fsdp'), may hold values from 1 to 192, as said below
- block_pos: int32 [32, 4], P('fsdp'), may hold values from 0 to 3, each once within a row
- w_qkv: bfloat16 [2, 768, 2304], P(None, 'fsdp', 'tp'), may hold values from -0.21875 to 0.21875
- w_out: bfloat16 [2, 768, 768], P(None, 'tp', 'fsdp'), may hold values from -1.75 to 1.75
- w_up: bfloat16 [2, 768, 3072], P(None, 'fsdp', 'tp'), may hold values from -0.21875 to 0.21875
- w_down: bfloat16 [2, 3072, 768], P(None, 'tp', 'fsdp'), may hold values from -0.109375 to 0.109375
- b_qkv: bfloat16 [2, 2304], P(None, ('tp', 'fsdp')), may hold values from -1.796875 to 1.796875
- b_up: bfloat16 [2, 3072], P(None, ('tp', 'fsdp')), may hold values from -1.796875 to 1.796875
- out_bias: bfloat16 [2, 2, 768], P(None, None, 'fsdp'), may hold values from -1.796875 to 1.796875
- norm_gain: bfloat16 [2, 2, 768], P(None, None, 'fsdp'), may hold values from 0.25 to 1.75
- norm_bias: bfloat16 [2, 2, 768], P(None, None, 'fsdp'), may hold values from -1.796875 to 1.796875
Outputs:
- output: bfloat16 [8192, 768], P(('fsdp', 'ctx'))
- grad_tokens: bfloat16 [8192, 768], P(('fsdp', 'ctx'))
- grad_w_qkv: float32 [2, 768, 2304], P(None, 'fsdp', 'tp')
- grad_w_out: float32 [2, 768, 768], P(None, 'tp', 'fsdp')
- grad_w_up: float32 [2, 768, 3072], P(None, 'fsdp', 'tp')
- grad_w_down: float32 [2, 3072, 768], P(None, 'tp', 'fsdp')
- grad_b_qkv: float32 [2, 2304], P(None, ('tp', 'fsdp'))
- grad_b_up: float32 [2, 3072], P(None, ('tp', 'fsdp'))
- grad_out_bias: float32 [2, 2, 768], P(None, None, 'fsdp')
- grad_norm_gain: float32 [2, 2, 768], P(None, None, 'fsdp')
- grad_norm_bias: float32 [2, 2, 768], P(None, None, 'fsdp')
The draws below stay inside these ranges and needn't reach their ends.
Inputs may be any that keep to these rules, and one draw needn't show every extreme that they name: `doc_lens`: in each group's row one entry, at a place drawn from the seed, is exactly 192; every entry is at least 1, and the row sums to at most 256. `block_pos`: each group's row is a permutation of the 4 position blocks.
All inputs are finite; a program needn't handle non-finite values.
Results may differ from the reference program's by a relative error of at most 0.019.
Values may be sent and summed in bfloat16 or wider, within the bound.
No kernel may reach another device: no remote copies, remote signals or barrier semaphores. Data moves between devices by JAX's collectives and lax.ppermute only.
A program may use at most 192 MiB of HBM per device.

```python
import jax
import jax.numpy as jnp
from jax import lax

D = 768
H = 12
HS = 64
ROT = 16
FF = 3072
LAYERS = 2
NDOC = 4
TOK_DEV = 128
GROUPS = 32
TOKENS = 8192
NBLK = 4
N_FSDP = 32
N_CTX = 2


def draw_doc_lens(key, part):
    key = jax.random.fold_in(key, 7)
    first_key, second_key = jax.random.split(key)
    group_rows = TOK_DEV * N_CTX
    longest = 3 * (group_rows // 4)
    spare = (group_rows - longest) // (NDOC - 1)
    others = jax.random.randint(first_key, (N_FSDP, NDOC), 1, spare + 1)
    chosen = jax.random.randint(second_key, (N_FSDP, 1), 0, NDOC)
    lengths = jnp.where(jnp.arange(NDOC)[None, :] == chosen, longest, others)
    return lengths.astype(jnp.int32)


def spiked(values, key, source, target, blocks, factor):
    owner, partner = [(jnp.arange(values.shape[position]) // (values.shape[position] // blocks)).reshape([-1 if axis == position else 1 for axis in range(values.ndim)]) for position in (source, target)]
    chosen = jax.random.permutation(key, blocks)[partner]
    strong = (owner == chosen) | (owner == (partner + blocks // 2) % blocks)
    return jnp.where(strong, factor * values, values)


def levels(own_key, shape, shards, low, high):
    level = 1.0
    for axis_at, shards_of in shards:
        heights = jax.random.uniform(jax.random.fold_in(jax.random.fold_in(own_key, 6), axis_at), (shards_of,), jnp.float32, low / len(shards), high / len(shards))
        level = level * jnp.repeat(jnp.exp(heights), shape[axis_at] // shards_of).reshape((-1,) + (1,) * (len(shape) - 1 - axis_at))
    return level


def gaussian(own_key, extent, spread, reach, shards=(), held_as=jnp.bfloat16):
    values = jax.random.normal(own_key, extent, jnp.float32) * spread
    if len(shards) > 0:
        values = levels(own_key, extent, shards, -0.22, 0.18) * values
    return jnp.clip(values, min=-reach, max=reach).astype(held_as)


def noise_with(key, dims, deviation, most, pieces, heavy, held_as=jnp.bfloat16):
    values = deviation * jax.random.normal(key, dims, jnp.float32)
    if pieces:
        values = values * levels(key, dims, pieces, -0.22, 0.18)
    return jnp.clip(spiked(values, jax.random.fold_in(key, 3), *heavy), -most, most).astype(held_as)


def setup_inputs(seed: int = 0) -> dict:
    seeds = jax.random.split(jax.random.key(seed), 14)
    return {
        "tokens": gaussian(seeds[0], (TOKENS, D), 1.0, 6.0, ((0, 64),)),
        "cotangent": noise_with(seeds[1], (TOKENS, D), 1.0, 16.0, ((0, 64),), (0, 1, 64, 4.0)),
        "doc_lens": draw_doc_lens(jax.random.fold_in(seeds[13], 71), 0),
        "block_pos": jax.vmap(lambda own: jax.random.permutation(own, NBLK))(jax.random.split(seeds[3], GROUPS)).reshape((GROUPS, NBLK)).astype(jnp.int32),
        "w_qkv": gaussian(seeds[4], (LAYERS, D, 3 * D), D ** -0.5, 0.21875, ((1, 32), (2, 2))),
        "w_out": gaussian(seeds[5], (LAYERS, D, D), (D // 64) ** -0.5, 1.75, ((1, 2), (2, 32))),
        "w_up": gaussian(seeds[6], (LAYERS, D, FF), D ** -0.5, 0.21875, ((1, 32), (2, 2))),
        "w_down": gaussian(seeds[7], (LAYERS, FF, D), FF ** -0.5, 0.109375, ((1, 2), (2, 32))),
        "b_qkv": gaussian(seeds[8], (LAYERS, 3 * D), 0.3, 1.796875, ((1, 64),)),
        "b_up": gaussian(seeds[9], (LAYERS, FF), 0.3, 1.796875, ((1, 64),)),
        "out_bias": gaussian(seeds[10], (LAYERS, 2, D), 0.3, 1.796875, ((2, 32),)),
        "norm_gain": jnp.clip(1.0 + 0.15 * jax.random.normal(seeds[11], (LAYERS, 2, D), jnp.float32), 0.25, 1.75).astype(jnp.bfloat16),
        "norm_bias": gaussian(seeds[12], (LAYERS, 2, D), 0.3, 1.796875, ((2, 32),)),
    }


EPSILON = 1e-05
MASKED = -1e+30
HIGHEST = lax.Precision.HIGHEST

@jax.custom_vjp
def low(v):
    return lax.optimization_barrier(v.astype(jnp.bfloat16)).astype(jnp.float32)

@jax.custom_vjp
def low_back(v):
    return v

def low_keep(v):
    return (low(v), None)

def low_pass(kept, grad):
    return (grad,)

def back_keep(v):
    return (v, None)

def back_low(kept, grad):
    return (low(grad),)
low.defvjp(low_keep, low_pass)
low_back.defvjp(back_keep, back_low)

def angles(positions):
    exponents = jnp.arange(ROT // 2, dtype=jnp.float32) * (2.0 / ROT)
    inverse = jnp.power(10000.0, -exponents)
    phase = positions.astype(jnp.float32)[:, None] * inverse[None, :]
    return (jnp.cos(phase), jnp.sin(phase))

def rotate(values, cos_table, sin_table):
    half_rot = ROT // 2
    first_half = values[..., :half_rot]
    second_half = values[..., half_rot:ROT]
    cos_wide = cos_table[:, None, :]
    sin_wide = sin_table[:, None, :]
    return jnp.concatenate([first_half * cos_wide - second_half * sin_wide, second_half * cos_wide + first_half * sin_wide, values[..., ROT:]], axis=-1)

def normalize(values, gain_row, shift_row):
    row_mean = lax.optimization_barrier(jnp.mean(values, axis=-1, keepdims=True))
    centered = values - row_mean
    inv_std = lax.rsqrt(lax.optimization_barrier(jnp.mean(centered * centered, axis=-1, keepdims=True)) + EPSILON)
    return centered * inv_std * gain_row + shift_row

def product(left, right):
    return jnp.dot(left, right, precision=HIGHEST)

def layer_ref(hidden, weights, allowed, cos_table, sin_table):
    w_qkv, w_out, w_up, w_down, b_qkv, b_up, b_out, norm_gain, norm_bias = weights
    row_count = hidden.shape[0]
    attn_in = low(normalize(hidden, norm_gain[0], norm_bias[0]))
    projected = low_back(product(attn_in, w_qkv) + b_qkv).reshape(row_count, H, 3, HS)
    queries = low(rotate(projected[:, :, 0], cos_table, sin_table))
    key_rows = low(rotate(projected[:, :, 1], cos_table, sin_table))
    values = low(projected[:, :, 2])
    scores = low_back(jnp.einsum('qhd,khd->hqk', queries, key_rows, precision=HIGHEST) * HS ** (-0.5))
    scores = jnp.where(allowed[None], scores, MASKED)
    attention = low(jax.nn.softmax(scores, axis=-1))
    attended = jnp.einsum('hqk,khd->qhd', attention, values, precision=HIGHEST).reshape(row_count, D)
    attn_out = low(low_back(attended))
    mlp_in = low(normalize(hidden, norm_gain[1], norm_bias[1]))
    up_value = low_back(product(mlp_in, w_up) + b_up)
    activated = low(jax.nn.gelu(up_value, approximate=False))
    branch = low_back(product(attn_out, w_out) + product(activated, w_down))
    return hidden + branch + b_out[0] + b_out[1]

def token_layout(lens_row, block_row):
    block_rows = TOK_DEV // 2
    offsets = jnp.arange(block_rows, dtype=jnp.int32)
    positions = (block_row.astype(jnp.int32)[:, None] * block_rows + offsets[None, :]).reshape(-1).astype(jnp.int32)
    doc_ends = jnp.cumsum(lens_row).astype(jnp.int32)
    documents = lax.optimization_barrier(jnp.sum((positions[:, None] >= doc_ends[None, :]).astype(jnp.int32), axis=1)).astype(jnp.int32)
    return (positions, documents)

def reference(tokens, cotangent, doc_lens, block_pos, w_qkv, w_out, w_up, w_down, b_qkv, b_up, out_bias, norm_gain, norm_bias):
    params = tuple((array.astype(jnp.float32) for array in (w_qkv, w_out, w_up, w_down, b_qkv, b_up, out_bias, norm_gain, norm_bias)))
    group_rows = TOK_DEV * N_CTX
    inputs = tokens.astype(jnp.float32).reshape(N_FSDP, group_rows, D)
    cotangents = cotangent.astype(jnp.float32).reshape(N_FSDP, group_rows, D)

    def one_group(totals, group_items):
        group_input, group_cotangent, lens_row, block_row = group_items
        positions, documents = token_layout(lens_row, block_row)
        allowed = (documents[:, None] == documents[None, :]) & (positions[None, :] <= positions[:, None])
        cos_table, sin_table = angles(positions)

        def forward(start, weights_all):
            hidden = start
            for layer_index in range(LAYERS):
                hidden = layer_ref(hidden, tuple((array[layer_index] for array in weights_all)), allowed, cos_table, sin_table)
            return hidden
        result, backward = jax.vjp(forward, group_input, params)
        grad_input, grad_params = backward(group_cotangent)
        totals = tuple((total_sum + piece for total_sum, piece in zip(totals, grad_params)))
        return (totals, (result, grad_input))
    zeros = tuple((jnp.zeros_like(array) for array in params))
    totals, (results, grad_inputs) = lax.scan(one_group, zeros, (inputs, cotangents, doc_lens, block_pos))
    return (results.reshape(TOKENS, D).astype(jnp.bfloat16), grad_inputs.reshape(TOKENS, D).astype(jnp.bfloat16), totals[0], totals[1], totals[2], totals[3], totals[4], totals[5], totals[6], totals[7], totals[8])
```

```python
import jax
import jax.numpy as jnp
from jax import lax
from jax.sharding import PartitionSpec as P

HS = 64
ROT = 16
EPSILON = 1e-05
MASKED = -1e30
F32 = jnp.float32
BF = jnp.bfloat16
SWAP = [(0, 1), (1, 0)]


def other_core(values):
    return lax.ppermute(values, "ctx", SWAP)


def other_half(values):
    return lax.ppermute(values, "tp", SWAP)


def to_all(block):
    count = lax.axis_size("fsdp")
    return lax.all_to_all(
        jnp.broadcast_to(block[None], (count, *block.shape)), "fsdp", 0, 0, tiled=True
    )


def summed(blocks):
    got = lax.all_to_all(blocks, "fsdp", 0, 0, tiled=True)
    return jnp.sum(got.astype(F32), axis=0)


def own_rows_summed(part):
    half = part.shape[0] // 2
    mine = part[:half] + other_core(part[half:].astype(BF)).astype(F32)
    mine = mine.astype(BF)
    return mine.astype(F32) + other_half(mine).astype(F32)


def with_other_rows(total):
    return jnp.concatenate([total, other_core(total.astype(BF)).astype(F32)], axis=0)


def rows_by_rows(left, right):
    return lax.dot_general(
        left, right, (((0,), (0,)), ((), ())), preferred_element_type=F32
    )


def cols_by_cols(left, right):
    return lax.dot_general(
        left, right, (((1,), (1,)), ((), ())), preferred_element_type=F32
    )


def product(left, right):
    return jnp.dot(left, right, preferred_element_type=F32)


def gelu_exact(values):
    return jax.nn.gelu(values, approximate=False)


def angles(positions):
    exponents = jnp.arange(ROT // 2, dtype=F32) * (2.0 / ROT)
    inverse = jnp.power(10000.0, -exponents)
    phase = positions.astype(F32)[:, None] * inverse[None, :]
    return (jnp.cos(phase), jnp.sin(phase))


def rotate(values, cos_table, sin_table):
    half_rot = ROT // 2
    first_half = values[..., :half_rot]
    second_half = values[..., half_rot:ROT]
    cos_wide = cos_table[:, None, :]
    sin_wide = sin_table[:, None, :]
    return jnp.concatenate(
        [
            first_half * cos_wide - second_half * sin_wide,
            second_half * cos_wide + first_half * sin_wide,
            values[..., ROT:],
        ],
        axis=-1,
    )


def standardize(values):
    centered = values - jnp.mean(values, axis=-1, keepdims=True)
    inv_std = lax.rsqrt(jnp.mean(centered * centered, axis=-1, keepdims=True) + EPSILON)
    return (centered * inv_std, inv_std)


def layer_forward(hidden, weights, allowed, cos_table, sin_table):
    w_qkv, w_out_t, w_up, w_down_t, b_qkv, b_up, b_out, gains, shifts = weights
    rows = hidden.shape[0]
    heads = w_qkv.shape[1] // (3 * HS)
    normed, inv_std = standardize(hidden)
    attn_in = (normed * gains[0] + shifts[0]).astype(BF)
    mlp_in = (normed * gains[1] + shifts[1]).astype(BF)
    projected = (product(attn_in, w_qkv) + b_qkv).reshape(rows, heads, 3, HS)
    queries = rotate(projected[:, :, 0], cos_table, sin_table).astype(BF)
    keys = rotate(projected[:, :, 1], cos_table, sin_table).astype(BF)
    values = projected[:, :, 2].astype(BF)
    scores = jnp.einsum("qhd,khd->hqk", queries, keys, preferred_element_type=F32)
    scores = jnp.where(allowed[None], scores * HS ** (-0.5), MASKED)
    exponent = jnp.exp(scores - jnp.max(scores, axis=2, keepdims=True))
    attention = exponent / jnp.sum(exponent, axis=2, keepdims=True)
    attended = jnp.einsum(
        "hqk,khd->qhd", attention.astype(BF), values, preferred_element_type=F32
    )
    attn_out = attended.astype(BF).reshape(rows, heads * HS)
    up_value = product(mlp_in, w_up) + b_up
    activated = gelu_exact(up_value).astype(BF)
    part = cols_by_cols(attn_out, w_out_t) + cols_by_cols(activated, w_down_t)
    state = (normed, inv_std, attn_in, mlp_in, queries, keys, values, attention, attn_out)
    return (part, (*state, up_value, activated))


def layer_backward(grad_next, state, weights, cos_table, sin_table):
    w_qkv, w_out_t, w_up, w_down_t, b_qkv, b_up, b_out, gains, shifts = weights
    normed, inv_std, attn_in, mlp_in, queries, keys, values, attention, attn_out = state[:9]
    up_value, activated = state[9:]
    rows = grad_next.shape[0]
    heads = queries.shape[1]
    scale = HS ** (-0.5)
    low_grad = grad_next.astype(BF)
    grad_w_out = rows_by_rows(low_grad, attn_out)
    grad_w_down = rows_by_rows(low_grad, activated)
    grad_attended = product(low_grad, w_out_t).astype(BF).reshape(rows, heads, HS)
    grad_activated = product(low_grad, w_down_t)
    unused_value, gelu_back = jax.vjp(gelu_exact, up_value)
    low_grad_up = gelu_back(grad_activated)[0].astype(BF)
    grad_w_up = rows_by_rows(mlp_in, low_grad_up)
    grad_b_up = jnp.sum(low_grad_up.astype(F32), axis=0)
    part_mlp = cols_by_cols(low_grad_up, w_up)
    grad_attention = jnp.einsum("qhd,khd->hqk", grad_attended, values, preferred_element_type=F32)
    grad_values = jnp.einsum(
        "hqk,qhd->khd", attention.astype(BF), grad_attended, preferred_element_type=F32
    )
    row_dot = jnp.sum(attention * grad_attention, axis=2, keepdims=True)
    low_scores = (attention * (grad_attention - row_dot)).astype(BF)
    grad_queries = scale * jnp.einsum(
        "hqk,khd->qhd", low_scores, keys, preferred_element_type=F32
    )
    grad_keys = scale * jnp.einsum(
        "hqk,qhd->khd", low_scores, queries, preferred_element_type=F32
    )
    grad_queries = rotate(grad_queries, cos_table, -sin_table)
    grad_keys = rotate(grad_keys, cos_table, -sin_table)
    low_grad_qkv = (
        jnp.stack([grad_queries, grad_keys, grad_values], axis=2)
        .astype(BF)
        .reshape(rows, heads * 3 * HS)
    )
    grad_w_qkv = rows_by_rows(attn_in, low_grad_qkv)
    grad_b_qkv = jnp.sum(low_grad_qkv.astype(F32), axis=0)
    part_attn = cols_by_cols(low_grad_qkv, w_qkv)
    part = part_attn * gains[0] + part_mlp * gains[1]
    slab = jnp.concatenate([grad_w_qkv, grad_w_out, grad_w_up, grad_w_down], axis=1).astype(BF)
    sums = (
        jnp.sum(grad_next, axis=0) * 0.25,
        jnp.sum(part_attn * normed, axis=0),
        jnp.sum(part_mlp * normed, axis=0),
        jnp.sum(part_attn, axis=0),
        jnp.sum(part_mlp, axis=0),
    )
    return (part, slab, sums, grad_b_qkv, grad_b_up)


def norm_back(total, normed, inv_std):
    return inv_std * (
        total
        - jnp.mean(total, axis=-1, keepdims=True)
        - normed * jnp.mean(total * normed, axis=-1, keepdims=True)
    )


def per_device(
    tokens,
    cotangent,
    doc_lens,
    block_pos,
    w_qkv,
    w_out,
    w_up,
    w_down,
    b_qkv,
    b_up,
    out_bias,
    norm_gain,
    norm_bias,
):
    row_count = tokens.shape[0]
    block_rows = row_count // 2
    core = lax.axis_index("ctx")
    owners = lax.axis_size("fsdp")
    layers, depth, width_qkv = w_qkv.shape
    width_qkv, width_out, width_up = (n // 2 for n in (width_qkv, w_out.shape[1], w_up.shape[2]))

    def mine(array, axis, width):
        return lax.dynamic_slice_in_dim(array, core * width, width, axis)

    slabs = jnp.concatenate(
        [
            mine(w_qkv, 2, width_qkv),
            mine(w_out, 1, width_out).transpose(0, 2, 1),
            mine(w_up, 2, width_up),
            mine(w_down, 1, width_up).transpose(0, 2, 1),
        ],
        axis=2,
    )
    vectors = jnp.concatenate([out_bias, norm_gain, norm_bias], axis=1).reshape(-1, depth)
    bias_qkv = jnp.pad(b_qkv, ((0, 0), (0, 2 * depth - b_qkv.shape[1]))).reshape(-1, depth)
    bias_up = b_up.reshape(-1, depth)
    small = jnp.concatenate([vectors, bias_qkv, bias_up], axis=0)
    small = jnp.pad(small, ((0, 128 - small.shape[0]), (0, 0))).T
    first = to_all(jnp.concatenate([slabs[0], small], axis=1)).reshape(owners * depth, -1)
    later = to_all(slabs[1]).reshape(owners * depth, -1)
    width = slabs.shape[2]
    small = first[:, width:].T.reshape(128, owners, depth)[: 10 * layers].astype(F32)
    vectors = small[: 6 * layers].reshape(layers, 3, 2, owners * depth)
    bias_qkv, bias_up = (
        small[at * layers : (at + 2) * layers]
        .reshape(layers, 2, owners, depth)
        .transpose(0, 2, 1, 3)
        .reshape(layers, owners, 2 * depth)
        for at in (6, 8)
    )
    bias_qkv = mine(bias_qkv[:, :, : b_qkv.shape[1]].reshape(layers, -1), 1, width_qkv)
    bias_up = mine(bias_up.reshape(layers, -1), 1, width_up)

    cuts = (0, width_qkv, width_qkv + width_out, width_qkv + width_out + width_up, width)
    weights = []
    for layer, slab in enumerate((first, later)):
        matrices = (slab[:, a:b] for a, b in zip(cuts[:-1], cuts[1:]))
        weights.append((*matrices, bias_qkv[layer], bias_up[layer], *vectors[layer]))

    both = jnp.stack([tokens, cotangent])
    hidden, grad = jnp.concatenate([both, other_core(both)], axis=1).astype(F32)
    offsets = jnp.arange(block_rows, dtype=jnp.int32)
    positions = (block_pos[0][:, None] * block_rows + offsets[None, :]).reshape(2, row_count)
    positions = jnp.where(core == 0, positions, positions[::-1]).reshape(-1)
    doc_ends = jnp.cumsum(doc_lens[0])
    docs = jnp.sum((positions[:, None] >= doc_ends[None, :]).astype(jnp.int32), axis=1)
    allowed = (docs[:, None] == docs[None, :]) & (positions[None, :] <= positions[:, None])
    cos_table, sin_table = angles(positions)

    states = []
    for layer in range(layers):
        part, state = layer_forward(hidden, weights[layer], allowed, cos_table, sin_table)
        states.append(state)
        total = own_rows_summed(part)
        b_out = weights[layer][6]
        if layer + 1 < layers:
            hidden = hidden + with_other_rows(total) + b_out[0] + b_out[1]
        else:
            result = (hidden[:row_count] + total + b_out[0] + b_out[1]).astype(BF)

    all_sums, pieces = [None] * layers, [None] * layers
    for layer in reversed(range(layers)):
        state = states[layer]
        part, slab, sums, grad_b_qkv, grad_b_up = layer_backward(
            grad, state, weights[layer], cos_table, sin_table
        )
        bias_grads = []
        for vector, whole in ((grad_b_qkv, 2 * depth), (grad_b_up, 2 * depth)):
            empty = jnp.zeros_like(vector)
            spread = jnp.where(
                core == 0, jnp.concatenate([vector, empty]), jnp.concatenate([empty, vector])
            ).reshape(owners, -1)
            spread = jnp.pad(spread, ((0, 0), (0, whole - spread.shape[1])))
            bias_grads.append(spread.reshape(owners, 2, depth).transpose(1, 0, 2).reshape(2, -1))
        all_sums[layer] = jnp.concatenate([jnp.stack(sums), *bias_grads], axis=0)
        if layer == 0:
            rows = jnp.concatenate(all_sums, axis=0)
            rows = jnp.pad(rows, ((0, 128 - rows.shape[0]), (0, 0))).astype(BF)
            slab = jnp.concatenate([slab, rows.T], axis=1)
        pieces[layer] = summed(slab.reshape(owners, depth, -1))
        total = own_rows_summed(part)
        if layer > 0:
            total = with_other_rows(total)
            grad = grad + norm_back(total, state[0], state[1])
        else:
            normed, inv_std = state[0][:row_count], state[1][:row_count]
            grad_tokens = (grad[:row_count] + norm_back(total, normed, inv_std)).astype(BF)

    small = pieces[0][:, width:].T[: 9 * layers].astype(BF).astype(F32)
    small = small + other_half(small)
    own_small = pieces[0][:, width:].T[: 9 * layers].astype(BF).astype(F32)
    small = small.reshape(layers, 9, depth)
    own_small = own_small.reshape(layers, 9, depth)
    small = jnp.concatenate([small[:, :5], own_small[:, 5:]], axis=1)
    small = small + other_core(small)
    matrices = jnp.stack([pieces[0][:, :width], pieces[1]]).astype(BF)
    theirs = other_core(matrices)
    low = jnp.where(core == 0, matrices, theirs).astype(F32)
    high = jnp.where(core == 0, theirs, matrices).astype(F32)
    joined = []
    for k, (a, b) in enumerate(zip(cuts[:-1], cuts[1:])):
        joined.append(jnp.concatenate([low[:, :, a:b], high[:, :, a:b]], axis=2))
    grad_qkv, grad_out, grad_up, grad_down = joined
    return (
        result,
        grad_tokens,
        grad_qkv,
        grad_out.transpose(0, 2, 1),
        grad_up,
        grad_down.transpose(0, 2, 1),
        small[:, 5:7].reshape(layers, -1)[:, : b_qkv.shape[1]],
        small[:, 7:9].reshape(layers, -1),
        jnp.stack([small[:, 0], small[:, 0]], axis=1),
        small[:, 1:3],
        small[:, 3:5],
    )


def solution(mesh):
    in_specs = (
        P(("fsdp", "ctx"), None),
        P(("fsdp", "ctx"), None),
        P("fsdp", None),
        P("fsdp", None),
        P(None, "fsdp", "tp"),
        P(None, "tp", "fsdp"),
        P(None, "fsdp", "tp"),
        P(None, "tp", "fsdp"),
        P(None, ("tp", "fsdp")),
        P(None, ("tp", "fsdp")),
        P(None, None, "fsdp"),
        P(None, None, "fsdp"),
        P(None, None, "fsdp"),
    )
    out_specs = (P(("fsdp", "ctx"), None), P(("fsdp", "ctx"), None), *in_specs[4:])
    return jax.shard_map(
        per_device, mesh=mesh, in_specs=in_specs, out_specs=out_specs, check_vma=False
    )
```

```python
import functools

import jax
import jax.numpy as jnp
from jax import lax
from jax.experimental import pallas as pl
from jax.experimental.pallas import tpu as pltpu
from jax.sharding import PartitionSpec as P

HS = 64
ROT = 16
EPSILON = 1e-05
MASKED = -1e30
F32 = jnp.float32
BF = jnp.bfloat16
SWAP = [(0, 1), (1, 0)]
LANES = 128
CHUNK = 32
HEAD = 4 * HS
SCALE = HS ** (-0.5)
VMEM_BYTES = 50 * 1024 * 1024
GAIN_A, GAIN_B, SHIFT_A, SHIFT_B, BIAS_QKV, BIAS_UP, BIAS_OUT = range(7)
VECTORS = 8
SUM_OUT, SUM_GAIN_A, SUM_GAIN_B, SUM_SHIFT_A, SUM_SHIFT_B, SUM_QKV, SUM_UP = range(7)


def other_core(values):
    return lax.ppermute(values, "ctx", SWAP)


def other_half(values):
    return lax.ppermute(values, "tp", SWAP)


def to_all(block):
    count = lax.axis_size("fsdp")
    return lax.all_to_all(
        jnp.broadcast_to(block[None], (count, *block.shape)), "fsdp", 0, 0, tiled=True
    )


def summed(blocks):
    got = lax.all_to_all(blocks, "fsdp", 0, 0, tiled=True)
    return jnp.sum(got.astype(F32), axis=0)


def dot(left, right, along=(1, 0)):
    dims = (((along[0],), (along[1],)), ((), ()))
    return lax.dot_general(left, right, dims, preferred_element_type=F32)


def over_rows(rows, step, carry=None, start=0):
    def body(at, kept):
        return step(pl.ds(pl.multiple_of(at * CHUNK, CHUNK), CHUNK), kept)

    return lax.fori_loop(start // CHUNK, rows // CHUNK, body, carry)


def by_eights(values):
    return values.reshape(-1, 8, values.shape[-1]).sum(axis=0)


def whole_sum(eights):
    return jnp.sum(eights, axis=0, keepdims=True)


def turned(tile, cos, left, right):
    return (
        tile * cos
        + pltpu.roll(tile, LANES - ROT // 2, 1) * left
        + pltpu.roll(tile, ROT // 2, 1) * right
    )


def row_norm(values):
    centered = values - jnp.mean(values, axis=-1, keepdims=True)
    inv_std = lax.rsqrt(jnp.mean(centered * centered, axis=-1, keepdims=True) + EPSILON)
    return centered * inv_std, inv_std


def row_norm_back(total, normed, inv_std):
    return inv_std * (
        total
        - jnp.mean(total, axis=-1, keepdims=True)
        - normed * jnp.mean(total * normed, axis=-1, keepdims=True)
    )


def one_hot(place_ref, at, width):
    rows = lax.broadcasted_iota(jnp.int32, (width, place_ref.shape[1]), 0)
    return (rows == place_ref[at : at + 1, :]).astype(F32).astype(BF)


class State:
    names = ("normed", "inv_std", "a", "m", "qk", "v", "p", "o", "gl", "slope")

    def __init__(self, refs):
        for name, ref in zip(self.names, refs, strict=True):
            setattr(self, name, ref)

    @staticmethod
    def shapes(rows, depth, heads, hidden):
        return (
            jax.ShapeDtypeStruct((rows, depth), F32),
            jax.ShapeDtypeStruct((rows, 1), F32),
            jax.ShapeDtypeStruct((rows, depth), BF),
            jax.ShapeDtypeStruct((rows, depth), BF),
            jax.ShapeDtypeStruct((rows, heads * 2 * HS), BF),
            jax.ShapeDtypeStruct((rows, heads * HS), BF),
            jax.ShapeDtypeStruct((heads, rows, rows), F32),
            jax.ShapeDtypeStruct((rows, heads * HEAD), BF),
            jax.ShapeDtypeStruct((rows, hidden), BF),
            jax.ShapeDtypeStruct((rows, hidden), F32),
        )


def forward(state, vec_ref, w_ref, table_ref, mask_ref, part_ref, wide_ref):
    rows, depth = state.normed.shape
    heads = state.v.shape[1] // HS
    attn, hidden = heads * HEAD, state.gl.shape[1]

    def affine(at, _):
        normed = state.normed[at, :]
        state.a[at, :] = (
            normed * vec_ref[GAIN_A : GAIN_A + 1, :] + vec_ref[SHIFT_A : SHIFT_A + 1, :]
        ).astype(BF)
        state.m[at, :] = (
            normed * vec_ref[GAIN_B : GAIN_B + 1, :] + vec_ref[SHIFT_B : SHIFT_B + 1, :]
        ).astype(BF)

    over_rows(rows, affine)
    wide_ref[...] = dot(state.a[...], w_ref[:, :attn])
    state.o[...] = jnp.zeros_like(state.o)
    for head in range(heads):
        at = head * HEAD
        bias = vec_ref[BIAS_QKV : BIAS_QKV + 1, at : at + HEAD]
        tile = wide_ref[:, at : at + LANES] + bias[:, :LANES]
        tile = turned(tile, table_ref[0], table_ref[1], table_ref[2]).astype(BF)
        value = wide_ref[:, at + 2 * HS : at + 3 * HS] + bias[:, 2 * HS : 3 * HS]
        value = value.astype(BF)
        state.qk[:, head * LANES : (head + 1) * LANES] = tile
        state.v[:, head * HS : (head + 1) * HS] = value
        half = rows // 2
        for top in (0, half):
            scores = dot(tile[top : top + half, :HS], tile[:, HS:], (1, 1))
            scores = scores * SCALE + mask_ref[top : top + half, :]
            exponent = jnp.exp(scores - jnp.max(scores, axis=1, keepdims=True))
            share = exponent * (1.0 / jnp.sum(exponent, axis=1, keepdims=True))
            state.p[head, top : top + half, :] = share
            state.o[top : top + half, at + 3 * HS : at + HEAD] = dot(
                share.astype(BF), value
            ).astype(BF)
    wide_ref[:, :hidden] = dot(state.m[...], w_ref[:, attn : attn + hidden])

    def gelu(at, _):
        up = wide_ref[at, :hidden] + vec_ref[BIAS_UP : BIAS_UP + 1, :hidden]
        below = 0.5 + 0.5 * lax.erf(up * (0.5**0.5))
        state.gl[at, :] = (up * below).astype(BF)
        state.slope[at, :] = below + up * (jnp.exp(-0.5 * up * up) * 0.3989422804014327)

    over_rows(rows, gelu)
    part = dot(state.o[...], w_ref[:, :attn], (1, 1))
    part = part + dot(state.gl[...], w_ref[:, attn + hidden : attn + 2 * hidden], (1, 1))
    part_ref[...] = part.astype(BF)


def backward(
    state, grad_ref, vec_ref, w_ref, table_ref, part_ref, slab_ref, sums_ref, scratch
):
    low_ref, up_ref, qkv_ref, wide_ref, deep_ref = scratch
    rows, depth = state.normed.shape
    heads = state.v.shape[1] // HS
    attn, hidden = heads * HEAD, state.gl.shape[1]

    def lower(at, total):
        grad = grad_ref[at, :].astype(F32)
        low_ref[at, :] = grad.astype(BF)
        return total + by_eights(grad)

    total = over_rows(rows, lower, jnp.zeros((8, depth), F32))
    sums_ref[SUM_OUT : SUM_OUT + 1, :] = whole_sum(total) * 0.25
    low = low_ref[...]
    wide_ref[:, :hidden] = dot(low, w_ref[:, attn + hidden : attn + 2 * hidden])

    def through_gelu(at, total):
        up = (wide_ref[at, :hidden] * state.slope[at, :]).astype(BF)
        up_ref[at, :] = up
        return total + by_eights(up.astype(F32))

    total = over_rows(rows, through_gelu, jnp.zeros((8, hidden), F32))
    sums_ref[SUM_UP : SUM_UP + 1, :hidden] = whole_sum(total)
    wide_ref[...] = dot(low, w_ref[:, :attn])
    for head in range(heads):
        at = head * HEAD
        tile = state.qk[:, head * LANES : (head + 1) * LANES]
        query, key = tile[:, :HS], tile[:, HS:]
        value = state.v[:, head * HS : (head + 1) * HS]
        out = wide_ref[:, at + 3 * HS : at + HEAD].astype(BF)
        half = rows // 2
        grad_value, grad_key, grad_query = 0.0, 0.0, []
        for top in (0, half):
            share = state.p[head, top : top + half, :]
            grad = dot(out[top : top + half], value, (1, 1))
            delta = jnp.sum(share * grad, axis=1, keepdims=True)
            low_scores = (share * (grad - delta)).astype(BF)
            grad_value = grad_value + dot(share.astype(BF), out[top : top + half], (0, 0))
            grad_query.append(dot(low_scores, key))
            grad_key = grad_key + dot(low_scores, query[top : top + half], (0, 0))
        both = jnp.concatenate([jnp.concatenate(grad_query, axis=0), grad_key], axis=1) * SCALE
        both = turned(both, table_ref[0], -table_ref[1], -table_ref[2])
        qkv_ref[:, at : at + LANES] = both.astype(BF)
        qkv_ref[:, at + LANES : at + HEAD] = jnp.concatenate(
            [grad_value, jnp.zeros_like(grad_value)], axis=1
        ).astype(BF)

    def count_qkv(at, total):
        return total + by_eights(qkv_ref[at, :].astype(F32))

    total = over_rows(rows, count_qkv, jnp.zeros((8, attn), F32))
    sums_ref[SUM_QKV : SUM_QKV + 1, :] = whole_sum(total)
    wide_ref[...] = dot(qkv_ref[...], w_ref[:, :attn], (1, 1))
    deep_ref[...] = dot(up_ref[...], w_ref[:, attn : attn + hidden], (1, 1))

    def through_norm(at, totals):
        first, second, normed = wide_ref[at, :], deep_ref[at, :], state.normed[at, :]
        part_ref[at, :] = (
            first * vec_ref[GAIN_A : GAIN_A + 1, :] + second * vec_ref[GAIN_B : GAIN_B + 1, :]
        ).astype(BF)
        new = (first * normed, second * normed, first, second)
        return tuple(old + by_eights(term) for old, term in zip(totals, new, strict=True))

    totals = over_rows(rows, through_norm, (jnp.zeros((8, depth), F32),) * 4)
    for row, total in enumerate(totals):
        sums_ref[SUM_GAIN_A + row : SUM_GAIN_A + row + 1, :] = whole_sum(total)
    slab = dot(state.a[...], qkv_ref[...], (0, 0)) + dot(low, state.o[...], (0, 0))
    slab_ref[:, :attn] = slab.astype(BF)
    slab_ref[:, attn : attn + hidden] = dot(state.m[...], up_ref[...], (0, 0)).astype(BF)
    slab_ref[:, attn + hidden : attn + 2 * hidden] = dot(low, state.gl[...], (0, 0)).astype(BF)


def first_kernel(layers, tokens_ref, w_ref, place_ref, table_ref, mask_ref, *rest):
    part_ref, vec_ref, *state, wide_ref = rest
    state = State(state)
    attn = state.o.shape[1]
    hidden = state.gl.shape[1]
    small = jnp.transpose(w_ref[:, attn + 2 * hidden :].astype(F32))
    at = 6 * layers
    biases = small[at : at + 4 * layers].astype(BF)
    bias_qkv = dot(biases[:layers], one_hot(place_ref, 0, attn), (1, 1)) + dot(
        biases[layers : 2 * layers], one_hot(place_ref, 1, attn), (1, 1)
    )
    bias_up = dot(biases[2 * layers : 3 * layers], one_hot(place_ref, 2, attn), (1, 1)) + dot(
        biases[3 * layers :], one_hot(place_ref, 3, attn), (1, 1)
    )
    for layer in range(layers):
        rows = small[6 * layer : 6 * layer + 6]
        vec_ref[layer, GAIN_A : SHIFT_B + 1, :] = rows[2:]
        vec_ref[layer, BIAS_QKV : BIAS_QKV + 1, :] = bias_qkv[layer : layer + 1]
        vec_ref[layer, BIAS_UP : BIAS_UP + 1, :] = bias_up[layer : layer + 1]
        vec_ref[layer, BIAS_OUT : BIAS_OUT + 1, :] = rows[0:1] + rows[1:2]
        vec_ref[layer, BIAS_OUT + 1 : VECTORS, :] = rows[0:1]

    def enter(at, _):
        normed, inv_std = row_norm(tokens_ref[at, :].astype(F32))
        state.normed[at, :] = normed
        state.inv_std[at, :] = inv_std

    over_rows(tokens_ref.shape[0], enter)
    forward(state, vec_ref.at[0], w_ref, table_ref, mask_ref, part_ref, wide_ref)


def last_kernel(
    tokens_ref, mine_ref, theirs_ref, other_ref, grad_ref, vec_ref, w_ref, table_ref, mask_ref, *rest
):
    ahead_ref, part_ref, slab_ref, sums_ref, hidden_ref, normed_ref, inv_std_ref, *rest = rest
    state, scratch = State([normed_ref, inv_std_ref, *rest[:8]]), rest[8:]
    own = mine_ref.shape[0]
    bias = vec_ref[0, BIAS_OUT : BIAS_OUT + 1, :]

    def keep(at, values):
        normed, inv_std = row_norm(values)
        normed_ref[at, :] = normed
        inv_std_ref[at, :] = inv_std

    def enter_own(at, _):
        total = mine_ref[at, :].astype(F32) + theirs_ref[at, :].astype(F32)
        values = tokens_ref[at, :].astype(F32) + total + bias
        hidden_ref[at, :] = values + vec_ref[1, BIAS_OUT : BIAS_OUT + 1, :]
        keep(at, values)

    def enter_other(at, _):
        there = pl.ds(pl.multiple_of(at.start + own, CHUNK), CHUNK)
        keep(there, tokens_ref[there, :].astype(F32) + other_ref[at, :].astype(F32) + bias)

    over_rows(own, enter_own)
    over_rows(own, enter_other)
    forward(state, vec_ref.at[1], w_ref, table_ref, mask_ref, ahead_ref, scratch[3])
    backward(
        state, grad_ref, vec_ref.at[1], w_ref, table_ref, part_ref, slab_ref, sums_ref, scratch
    )


def back_kernel(
    layers, grad_ref, mine_ref, theirs_ref, other_ref, normed_ref, inv_std_ref, later_ref, *rest
):
    vec_ref, w_ref, place_ref, table_ref, *rest = rest
    state, rest = State(rest[:10]), rest[10:]
    part_ref, slab_ref, kept_ref, sums_ref, below_ref, *scratch = rest
    own = mine_ref.shape[0]
    attn, hidden = state.o.shape[1], state.gl.shape[1]

    def enter_own(at, _):
        total = mine_ref[at, :].astype(F32) + theirs_ref[at, :].astype(F32)
        grad = row_norm_back(total, normed_ref[at, :], inv_std_ref[at, :])
        grad = grad + grad_ref[at, :].astype(F32)
        kept_ref[at, :] = grad
        below_ref[at, :] = grad

    def enter_other(at, _):
        there = pl.ds(pl.multiple_of(at.start + own, CHUNK), CHUNK)
        total = other_ref[at, :].astype(F32)
        grad = row_norm_back(total, normed_ref[there, :], inv_std_ref[there, :])
        below_ref[there, :] = grad + grad_ref[there, :].astype(F32)

    over_rows(own, enter_own)
    over_rows(own, enter_other)
    backward(
        state, below_ref, vec_ref.at[0], w_ref, table_ref, part_ref, slab_ref, sums_ref, scratch
    )
    both = [sums_ref, later_ref]
    pad = jnp.zeros((8 - layers, attn), F32)
    qkv = jnp.concatenate([ref[SUM_QKV : SUM_QKV + 1, :] for ref in both] + [pad], axis=0)
    up = jnp.concatenate([ref[SUM_UP : SUM_UP + 1, :] for ref in both] + [pad], axis=0)
    spread = [
        dot(values.astype(BF), one_hot(place_ref, at, attn))[:layers]
        for values, at in ((qkv, 0), (qkv, 1), (up, 2), (up, 3))
    ]
    small = [ref[: SUM_SHIFT_B + 1, :] for ref in both] + spread
    used = 9 * layers
    small = jnp.concatenate(small + [jnp.zeros((LANES - used, attn), F32)], axis=0)
    slab_ref[:, attn + 2 * hidden :] = jnp.transpose(small).astype(BF)


def call(kernel, outs, scratch, flops, *args):
    return pl.pallas_call(
        kernel,
        out_shape=outs,
        in_specs=[pl.BlockSpec(memory_space=pltpu.VMEM)] * len(args),
        out_specs=jax.tree.map(lambda _: pl.BlockSpec(memory_space=pltpu.VMEM), outs),
        scratch_shapes=scratch,
        compiler_params=pltpu.CompilerParams(vmem_limit_bytes=VMEM_BYTES),
        cost_estimate=pl.CostEstimate(flops=flops, bytes_accessed=8_000_000, transcendentals=0),
    )(*args)


def own_rows_summed(part):
    half = part.shape[0] // 2
    mine = part[:half].astype(F32) + other_core(part[half:]).astype(F32)
    mine = mine.astype(BF)
    return mine, other_half(mine)


def other_rows(mine, theirs):
    return other_core((mine.astype(F32) + theirs.astype(F32)).astype(BF))


def rotation(positions):
    exponents = jnp.arange(ROT // 2, dtype=F32) * (2.0 / ROT)
    inverse = jnp.power(10000.0, -exponents)
    phase = positions.astype(F32)[:, None] * inverse[None, :]
    cos, sin = jnp.cos(phase), jnp.sin(phase)
    none = jnp.zeros_like(sin)
    rest = jnp.zeros((positions.shape[0], HS - ROT), F32)
    tables = [[cos, cos, rest + 1.0], [-sin, none, rest], [none, sin, rest]]
    return jnp.stack([jnp.concatenate(t + t, axis=1) for t in tables])


def bias_places(core, owners, depth, width_qkv, width_up, shard_qkv, shard_up):
    owner = jnp.arange(owners * depth, dtype=jnp.int32) // depth
    inner = jnp.arange(owners * depth, dtype=jnp.int32) % depth
    rows = []
    for width, shard, head in ((width_qkv, shard_qkv, 3 * HS), (width_up, shard_up, None)):
        for first in (0, depth):
            at = owner * shard + inner + first - core * width
            fits = (inner + first < shard) & (at >= 0) & (at < width)
            if head is not None:
                at = at // head * HEAD + at % head
            rows.append(jnp.where(fits, at, -1))
    return jnp.stack(rows + rows)


def per_device(
    tokens,
    cotangent,
    doc_lens,
    block_pos,
    w_qkv,
    w_out,
    w_up,
    w_down,
    b_qkv,
    b_up,
    out_bias,
    norm_gain,
    norm_bias,
):
    row_count = tokens.shape[0]
    block_rows = row_count // 2
    core = lax.axis_index("ctx")
    owners = lax.axis_size("fsdp")
    layers, depth, width_qkv = w_qkv.shape
    width_qkv, width_out, hidden = (n // 2 for n in (width_qkv, w_out.shape[1], w_up.shape[2]))
    heads = width_out // HS
    attn = heads * HEAD
    width = attn + 2 * hidden
    wide = owners * depth
    rows = 2 * row_count

    def mine_of(array, axis, size):
        return lax.dynamic_slice_in_dim(array, core * size, size, axis)

    qkv = mine_of(w_qkv, 2, width_qkv).reshape(layers, depth, heads, 3 * HS)
    out = mine_of(w_out, 1, width_out).transpose(0, 2, 1).reshape(layers, depth, heads, HS)
    slabs = jnp.concatenate(
        [
            jnp.concatenate([qkv, out], axis=3).reshape(layers, depth, attn),
            mine_of(w_up, 2, hidden),
            mine_of(w_down, 1, hidden).transpose(0, 2, 1),
        ],
        axis=2,
    )
    vectors = jnp.concatenate([out_bias, norm_gain, norm_bias], axis=1).reshape(-1, depth)
    bias_qkv = jnp.pad(b_qkv, ((0, 0), (0, 2 * depth - b_qkv.shape[1])))
    biases = [b[:, at : at + depth] for b in (bias_qkv, b_up) for at in (0, depth)]
    small = jnp.concatenate([vectors, *biases], axis=0)
    small = jnp.pad(small, ((0, LANES - small.shape[0]), (0, 0))).T
    first = to_all(jnp.concatenate([slabs[0], small], axis=1)).reshape(wide, -1)
    second = to_all(slabs[1]).reshape(wide, -1)

    both = jnp.stack([tokens, cotangent])
    start, grad = jnp.concatenate([both, other_core(both)], axis=1)
    offsets = jnp.arange(block_rows, dtype=jnp.int32)
    positions = (block_pos[0][:, None] * block_rows + offsets[None, :]).reshape(2, row_count)
    positions = jnp.where(core == 0, positions, positions[::-1]).reshape(-1)
    doc_ends = jnp.cumsum(doc_lens[0])
    docs = jnp.sum((positions[:, None] >= doc_ends[None, :]).astype(jnp.int32), axis=1)
    allowed = (docs[:, None] == docs[None, :]) & (positions[None, :] <= positions[:, None])
    mask = jnp.where(allowed, 0.0, MASKED).astype(F32)
    table = rotation(positions)
    place = bias_places(core, owners, depth, width_qkv, hidden, b_qkv.shape[1], b_up.shape[1])

    sds = jax.ShapeDtypeStruct
    flops = 2 * rows * wide * width
    part, vec, *state = call(
        functools.partial(first_kernel, layers),
        (sds((rows, wide), BF), sds((layers, VECTORS, wide), F32), *State.shapes(rows, wide, heads, hidden)),
        [pltpu.VMEM((rows, wide), F32)],
        flops,
        start,
        first,
        place,
        table,
        mask,
    )
    mine, theirs = own_rows_summed(part)
    kept = State.shapes(rows, wide, heads, hidden)
    scratch = [
        pltpu.VMEM((rows, wide), BF),
        pltpu.VMEM((rows, hidden), BF),
        pltpu.VMEM((rows, attn), BF),
        pltpu.VMEM((rows, wide), F32),
        pltpu.VMEM((rows, wide), F32),
    ]
    ahead, part, slab, later_sums, result, normed, inv_std = call(
        last_kernel,
        (
            sds((rows, wide), BF),
            sds((rows, wide), BF),
            sds((wide, width), BF),
            sds((8, wide), F32),
            sds((row_count, wide), F32),
            *kept[:2],
        ),
        [pltpu.VMEM(s.shape, s.dtype) for s in kept[2:]] + scratch,
        3 * flops,
        start,
        mine,
        theirs,
        other_rows(mine, theirs),
        grad,
        vec,
        second,
        table,
        mask,
    )
    pieces = [None, summed(slab.reshape(owners, depth, -1))]
    mine, theirs = own_rows_summed(part)
    part, slab, grad_below = call(
        functools.partial(back_kernel, layers),
        (sds((rows, wide), BF), sds((wide, width + LANES), BF), sds((row_count, wide), F32)),
        [pltpu.VMEM((8, wide), F32), pltpu.VMEM((rows, wide), F32)] + scratch,
        2 * flops,
        grad,
        mine,
        theirs,
        other_rows(mine, theirs),
        normed,
        inv_std,
        later_sums,
        vec,
        first,
        place,
        table,
        *state,
    )
    pieces[0] = summed(slab.reshape(owners, depth, -1))
    mine, theirs = own_rows_summed(ahead)
    result = (result + mine.astype(F32) + theirs.astype(F32)).astype(BF)
    mine, theirs = own_rows_summed(part)
    total = mine.astype(F32) + theirs.astype(F32)
    total = row_norm_back(total, state[0][:row_count], state[1][:row_count])
    grad_tokens = (grad_below + total).astype(BF)

    small = pieces[0][:, width:].T[: 9 * layers].astype(BF).astype(F32)
    vectors = small[: 5 * layers]
    vectors = vectors + other_half(vectors)
    small = jnp.concatenate([vectors, small[5 * layers :]], axis=0)
    small = small + other_core(small)
    vectors = small[: 5 * layers].reshape(layers, 5, depth)
    low, high, up_low, up_high = (small[at * layers : (at + 1) * layers] for at in (5, 6, 7, 8))
    matrices = jnp.stack([pieces[0][:, :width], pieces[1]]).astype(BF)
    theirs = other_core(matrices)
    low_half = jnp.where(core == 0, matrices, theirs).astype(F32)
    high_half = jnp.where(core == 0, theirs, matrices).astype(F32)
    halves = (low_half, high_half)
    heads_of = [h[:, :, :attn].reshape(layers, depth, heads, HEAD) for h in halves]
    grad_qkv = jnp.concatenate(
        [h[..., : 3 * HS].reshape(layers, depth, width_qkv) for h in heads_of], axis=2
    )
    grad_out = jnp.concatenate(
        [h[..., 3 * HS :].reshape(layers, depth, width_out) for h in heads_of], axis=2
    )
    grad_up = jnp.concatenate([h[:, :, attn : attn + hidden] for h in halves], axis=2)
    grad_down = jnp.concatenate([h[:, :, attn + hidden :] for h in halves], axis=2)
    return (
        result,
        grad_tokens,
        grad_qkv,
        grad_out.transpose(0, 2, 1),
        grad_up,
        grad_down.transpose(0, 2, 1),
        jnp.concatenate([low, high], axis=1)[:, : b_qkv.shape[1]],
        jnp.concatenate([up_low, up_high], axis=1),
        jnp.stack([vectors[:, 0], vectors[:, 0]], axis=1),
        vectors[:, 1:3],
        vectors[:, 3:5],
    )


def solution(mesh):
    in_specs = (
        P(("fsdp", "ctx"), None),
        P(("fsdp", "ctx"), None),
        P("fsdp", None),
        P("fsdp", None),
        P(None, "fsdp", "tp"),
        P(None, "tp", "fsdp"),
        P(None, "fsdp", "tp"),
        P(None, "tp", "fsdp"),
        P(None, ("tp", "fsdp")),
        P(None, ("tp", "fsdp")),
        P(None, None, "fsdp"),
        P(None, None, "fsdp"),
        P(None, None, "fsdp"),
    )
    out_specs = (P(("fsdp", "ctx"), None), P(("fsdp", "ctx"), None), *in_specs[4:])
    return jax.shard_map(
        per_device, mesh=mesh, in_specs=in_specs, out_specs=out_specs, check_vma=False
    )
```

```python
import functools

import jax
import jax.numpy as jnp
from jax import lax
from jax.experimental import pallas as pl
from jax.experimental.pallas import tpu as pltpu
from jax.sharding import PartitionSpec as P

HS = 64
ROT = 16
EPSILON = 1e-05
MASKED = -1e30
F32 = jnp.float32
BF = jnp.bfloat16
SWAP = [(0, 1), (1, 0)]
NEAR = 4
LANES = 128
CHUNK = 128
HEAD = 4 * HS
SCALE = HS ** (-0.5)
VMEM_BYTES = 62 * 1024 * 1024
GAIN_A, GAIN_B, SHIFT_A, SHIFT_B, BIAS_QKV, BIAS_UP, BIAS_OUT = range(7)
VECTORS = 8
SUM_OUT, SUM_GAIN_A, SUM_GAIN_B, SUM_SHIFT_A, SUM_SHIFT_B, SUM_QKV, SUM_UP = range(7)


def other_core(values):
    return lax.ppermute(values, "ctx", SWAP)


def other_half(values):
    return lax.ppermute(values, "tp", SWAP)


def other_core_and_half(values):
    return lax.ppermute(values, ("ctx", "tp"), [(0, 3), (1, 2), (2, 1), (3, 0)])


def near_group(values):
    owners = lax.axis_size("fsdp")
    return lax.ppermute(values, "fsdp", [(f, f ^ NEAR) for f in range(owners)])


def near_other_half(values):
    owners = lax.axis_size("fsdp")
    pairs = [(2 * f + t, 2 * (f ^ NEAR) + 1 - t) for f in range(owners) for t in (0, 1)]
    return lax.ppermute(values, ("fsdp", "tp"), pairs)


def exchanged(blocks):
    return lax.all_to_all(blocks, "fsdp", 0, 0, tiled=True)


def dot(left, right, along=(1, 0)):
    dims = (((along[0],), (along[1],)), ((), ()))
    return lax.dot_general(left, right, dims, preferred_element_type=F32)


def over_rows(rows, step, carry=None, start=0):
    def body(at, kept):
        return step(pl.ds(pl.multiple_of(at * CHUNK, CHUNK), CHUNK), kept)

    return lax.fori_loop(start // CHUNK, rows // CHUNK, body, carry)


def by_eights(values):
    return values.reshape(-1, 8, values.shape[-1]).sum(axis=0)


def whole_sum(eights):
    return jnp.sum(eights, axis=0, keepdims=True)


def turned(tile, cos, left, right):
    return (
        tile * cos
        + pltpu.roll(tile, LANES - ROT // 2, 1) * left
        + pltpu.roll(tile, ROT // 2, 1) * right
    )


def row_norm(values):
    centered = values - jnp.mean(values, axis=-1, keepdims=True)
    inv_std = lax.rsqrt(jnp.mean(centered * centered, axis=-1, keepdims=True) + EPSILON)
    return centered * inv_std, inv_std


def row_norm_back(total, normed, inv_std):
    return inv_std * (
        total
        - jnp.mean(total, axis=-1, keepdims=True)
        - normed * jnp.mean(total * normed, axis=-1, keepdims=True)
    )


def one_hot(place_ref, at, width):
    rows = lax.broadcasted_iota(jnp.int32, (width, place_ref.shape[1]), 0)
    return (rows == place_ref[at : at + 1, :]).astype(F32).astype(BF)


class Slab:
    def __init__(self, far_ref, heads_ref, w_ref, arrived):
        attn, width = heads_ref.shape[1], heads_ref.shape[1] + w_ref.shape[1]
        self.heads_ref, self.w_ref = heads_ref, w_ref
        self.copies = [
            pltpu.make_async_copy(far_ref.at[:, :attn], heads_ref, arrived.at[0]),
            pltpu.make_async_copy(far_ref.at[:, attn:width], w_ref, arrived.at[1]),
        ]
        for copy in self.copies:
            copy.start()

    def wait(self):
        for copy in self.copies:
            copy.wait()
        return self.heads_ref, self.w_ref

    def give(self, far_ref, sent):
        attn, width = self.heads_ref.shape[1], self.heads_ref.shape[1] + self.w_ref.shape[1]
        copies = [
            pltpu.make_async_copy(self.heads_ref, far_ref.at[:, :attn], sent.at[0]),
            pltpu.make_async_copy(self.w_ref, far_ref.at[:, attn:width], sent.at[1]),
        ]
        for copy in copies:
            copy.start()
        for copy in copies:
            copy.wait()


class Copies:
    def __init__(self, semaphores):
        self.semaphores, self.started = semaphores, []

    def start(self, src, dst):
        copy = pltpu.make_async_copy(src, dst, self.semaphores.at[len(self.started)])
        copy.start()
        self.started.append(copy)

    def wait(self, begin=0, end=None):
        for copy in self.started[begin:end]:
            copy.wait()


class State:
    names = ("normed", "inv_std", "a", "m", "qk", "v", "p", "o", "gl", "slope")

    def __init__(self, refs, copies=None, far=()):
        for name, ref in zip(self.names, refs, strict=True):
            setattr(self, name, ref)
        self.copies, self.far = copies, dict(zip(self.names, far))

    def ready(self, *names):
        for name in names:
            if name in self.far:
                self.copies.start(getattr(self, name), self.far[name])

    @staticmethod
    def shapes(rows, depth, heads, hidden):
        group = rows // 2
        return (
            jax.ShapeDtypeStruct((rows, depth), F32),
            jax.ShapeDtypeStruct((rows, 1), F32),
            jax.ShapeDtypeStruct((group, depth), BF),
            jax.ShapeDtypeStruct((rows, depth), BF),
            jax.ShapeDtypeStruct((group, heads * 2 * HS), BF),
            jax.ShapeDtypeStruct((group, heads * HS), BF),
            jax.ShapeDtypeStruct((heads, group, group), F32),
            jax.ShapeDtypeStruct((group, heads * HEAD), BF),
            jax.ShapeDtypeStruct((rows, hidden), BF),
            jax.ShapeDtypeStruct((rows, hidden), F32),
        )


def places(rows):
    quarter = rows // 4
    return [(0, 0, 0), (quarter, 1, 0), (2 * quarter, 0, quarter), (3 * quarter, 1, quarter)]


def forward(state, vec_ref, slab, near_copies, table_ref, mask_ref, parts, wide_ref):
    rows, depth = state.normed.shape
    group = rows // 2
    heads = state.v.shape[1] // HS
    hidden = state.gl.shape[1]

    def affine_a(at, _):
        state.a[at, :] = (
            state.normed[at, :] * vec_ref[GAIN_A : GAIN_A + 1, :]
            + vec_ref[SHIFT_A : SHIFT_A + 1, :]
        ).astype(BF)

    def affine_b(at, _):
        state.m[at, :] = (
            state.normed[at, :] * vec_ref[GAIN_B : GAIN_B + 1, :]
            + vec_ref[SHIFT_B : SHIFT_B + 1, :]
        ).astype(BF)

    state.ready("normed", "inv_std")
    over_rows(group, affine_a)
    over_rows(rows, affine_b)
    state.ready("a", "m")
    heads_ref, w_ref = slab.wait()
    near_copies.wait()
    wide_ref[:group, :] = dot(state.a[...], heads_ref[...])
    state.o[...] = jnp.zeros_like(state.o)
    for head in range(heads):
        at = head * HEAD
        bias = vec_ref[BIAS_QKV : BIAS_QKV + 1, at : at + HEAD]
        tile = wide_ref[:group, at : at + LANES] + bias[:, :LANES]
        tile = turned(tile, table_ref[0], table_ref[1], table_ref[2]).astype(BF)
        value = wide_ref[:group, at + 2 * HS : at + 3 * HS] + bias[:, 2 * HS : 3 * HS]
        value = value.astype(BF)
        state.qk[:, head * LANES : (head + 1) * LANES] = tile
        state.v[:, head * HS : (head + 1) * HS] = value
        half = group // 2
        for top in (0, half):
            scores = dot(tile[top : top + half, :HS], tile[:, HS:], (1, 1))
            scores = scores * SCALE + mask_ref[top : top + half, :]
            exponent = jnp.exp(scores - jnp.max(scores, axis=1, keepdims=True))
            share = exponent * (1.0 / jnp.sum(exponent, axis=1, keepdims=True))
            state.p[head, top : top + half, :] = share
            state.o[top : top + half, at + 3 * HS : at + HEAD] = dot(
                share.astype(BF), value
            ).astype(BF)
    state.ready("qk", "v", "p", "o")
    wide_ref[:, :hidden] = dot(state.m[...], w_ref[:, :hidden])

    def gelu(at, _):
        up = wide_ref[at, :hidden] + vec_ref[BIAS_UP : BIAS_UP + 1, :hidden]
        below = 0.5 + 0.5 * lax.erf(up * (0.5**0.5))
        state.gl[at, :] = (up * below).astype(BF)
        state.slope[at, :] = below + up * (jnp.exp(-0.5 * up * up) * 0.3989422804014327)

    over_rows(rows, gelu)
    state.ready("gl", "slope")
    down = w_ref[:, hidden : 2 * hidden]
    part = dot(state.o[...], heads_ref[...], (1, 1))
    half = group // 2
    part = (part + dot(state.gl[:group, :], down, (1, 1))).astype(BF)
    near = dot(state.gl[group:, :], down, (1, 1)).astype(BF)
    for core, part_ref in enumerate(parts):
        at = core * half
        part_ref[:half, :] = part[at : at + half]
        part_ref[half:, :] = near[at : at + half]


def backward(
    state, grad_ref, vec_ref, slab, table_ref, parts, sums_ref, scratch, put, far_parts
):
    low_ref, up_ref, qkv_ref, wide_ref, deep_ref = scratch
    heads_ref, w_ref = slab.heads_ref, slab.w_ref
    rows, depth = state.normed.shape
    group = rows // 2
    heads = state.v.shape[1] // HS
    attn, hidden = heads * HEAD, state.gl.shape[1]

    def lower(at, total):
        grad = grad_ref[at, :].astype(F32)
        low_ref[at, :] = grad.astype(BF)
        return total + by_eights(grad)

    total = over_rows(rows, lower, jnp.zeros((8, depth), F32))
    sums_ref[SUM_OUT : SUM_OUT + 1, :] = whole_sum(total) * 0.125
    low = low_ref[...]
    wide_ref[:, :hidden] = dot(low, w_ref[:, hidden : 2 * hidden])

    def through_gelu(at, total):
        up = (wide_ref[at, :hidden] * state.slope[at, :]).astype(BF)
        up_ref[at, :] = up
        return total + by_eights(up.astype(F32))

    total = over_rows(rows, through_gelu, jnp.zeros((8, hidden), F32))
    sums_ref[SUM_UP : SUM_UP + 1, :hidden] = whole_sum(total)
    wide_ref[:group, :] = dot(low_ref[:group, :], heads_ref[...])
    for head in range(heads):
        at = head * HEAD
        tile = state.qk[:, head * LANES : (head + 1) * LANES]
        query, key = tile[:, :HS], tile[:, HS:]
        value = state.v[:, head * HS : (head + 1) * HS]
        out = wide_ref[:group, at + 3 * HS : at + HEAD].astype(BF)
        half = group // 2
        grad_value, grad_key, grad_query = 0.0, 0.0, []
        for top in (0, half):
            share = state.p[head, top : top + half, :]
            grad = dot(out[top : top + half], value, (1, 1))
            delta = jnp.sum(share * grad, axis=1, keepdims=True)
            low_scores = (share * (grad - delta)).astype(BF)
            grad_value = grad_value + dot(share.astype(BF), out[top : top + half], (0, 0))
            grad_query.append(dot(low_scores, key))
            grad_key = grad_key + dot(low_scores, query[top : top + half], (0, 0))
        both = jnp.concatenate([jnp.concatenate(grad_query, axis=0), grad_key], axis=1) * SCALE
        both = turned(both, table_ref[0], -table_ref[1], -table_ref[2])
        qkv_ref[:, at : at + LANES] = both.astype(BF)
        qkv_ref[:, at + LANES : at + HEAD] = jnp.concatenate(
            [grad_value, jnp.zeros_like(grad_value)], axis=1
        ).astype(BF)

    def count_qkv(at, total):
        return total + by_eights(qkv_ref[at, :].astype(F32))

    total = over_rows(group, count_qkv, jnp.zeros((8, attn), F32))
    sums_ref[SUM_QKV : SUM_QKV + 1, :] = whole_sum(total)
    wide_ref[:group, :] = dot(qkv_ref[...], heads_ref[...], (1, 1))
    deep_ref[...] = dot(up_ref[...], w_ref[:, :hidden], (1, 1))

    def through_norms(with_first, part_ref, begin, to):
        def step(at, totals):
            there, at = moved(at, to), moved(at, begin)
            second, normed = deep_ref[at, :], state.normed[at, :]
            total, new = second * vec_ref[GAIN_B : GAIN_B + 1, :], (second * normed, second)
            if with_first:
                first = wide_ref[at, :]
                total = total + first * vec_ref[GAIN_A : GAIN_A + 1, :]
                new = (*new, first * normed, first)
            part_ref[there, :] = total.astype(BF)
            return tuple(old + by_eights(term) for old, term in zip(totals, new, strict=True))

        return step

    totals = (jnp.zeros((8, depth), F32),) * 4
    for begin, core, to in places(rows):
        count = 4 if begin < group else 2
        step = through_norms(begin < group, parts[core], begin, to)
        totals = (*over_rows(rows // 4, step, totals[:count]), *totals[count:])
    for row, total in zip((SUM_GAIN_B, SUM_SHIFT_B, SUM_GAIN_A, SUM_SHIFT_A), totals, strict=True):
        sums_ref[row : row + 1, :] = whole_sum(total)
    for ref, far_part_ref in zip(parts, far_parts, strict=True):
        put.start(ref, far_part_ref)
    heads_grad = dot(state.a[...], qkv_ref[...], (0, 0))
    heads_grad = heads_grad + dot(low_ref[:group, :], state.o[...], (0, 0))
    heads_ref[...] = heads_grad.astype(BF)
    w_ref[:, :hidden] = dot(state.m[...], up_ref[...], (0, 0)).astype(BF)
    w_ref[:, hidden : 2 * hidden] = dot(low, state.gl[...], (0, 0)).astype(BF)


def first_kernel(layers, *refs):
    inputs, (far_ref, place_ref, far_table_ref, far_mask_ref, *rest) = refs[:4], refs[4:]
    far_parts, vec_ref, far_state, rest = rest[:2], rest[2], rest[3:13], rest[13:]
    parts, (table_ref, mask_ref, get, put), rest = rest[:2], rest[2:6], rest[6:]
    wide_ref, small_ref, heads_ref, w_ref, arrived, *state = rest
    get, put = Copies(get), Copies(put)
    state = State(state, put, far_state)
    attn = state.o.shape[1]
    hidden = state.gl.shape[1]
    columns = attn + 2 * hidden
    copy = pltpu.make_async_copy(far_ref.at[:, columns:], small_ref, arrived.at[2])
    copy.start()
    slab = Slab(far_ref, heads_ref, w_ref, arrived)
    get.start(far_table_ref, table_ref)
    get.start(far_mask_ref, mask_ref)
    copy.wait()
    small = jnp.transpose(small_ref[...].astype(F32))
    at = 6 * layers
    biases = small[at : at + 4 * layers].astype(BF)
    bias_qkv = dot(biases[:layers], one_hot(place_ref, 0, attn), (1, 1)) + dot(
        biases[layers : 2 * layers], one_hot(place_ref, 1, attn), (1, 1)
    )
    bias_up = dot(biases[2 * layers : 3 * layers], one_hot(place_ref, 2, hidden), (1, 1)) + dot(
        biases[3 * layers :], one_hot(place_ref, 3, hidden), (1, 1)
    )
    for layer in range(layers):
        rows = small[6 * layer : 6 * layer + 6]
        vec_ref[layer, GAIN_A : SHIFT_B + 1, :] = rows[2:]
        vec_ref[layer, BIAS_QKV : BIAS_QKV + 1, :] = bias_qkv[layer : layer + 1]
        vec_ref[layer, BIAS_UP : BIAS_UP + 1, :hidden] = bias_up[layer : layer + 1]
        vec_ref[layer, BIAS_OUT : BIAS_OUT + 1, :] = rows[0:1] + rows[1:2]
        vec_ref[layer, BIAS_OUT + 1 : VECTORS, :] = rows[0:1]

    for quarter, ref in enumerate(inputs):

        def enter(at, _, ref=ref, begin=quarter * ref.shape[0]):
            normed, inv_std = row_norm(ref[at, :].astype(F32))
            state.normed[moved(at, begin), :] = normed
            state.inv_std[moved(at, begin), :] = inv_std

        over_rows(ref.shape[0], enter)
    forward(state, vec_ref.at[0], slab, get, table_ref, mask_ref, parts, wide_ref)
    for ref, far_part_ref in zip(parts, far_parts, strict=True):
        put.start(ref, far_part_ref)
    put.wait()


def summed_rows(parts, at, there):
    mine, half, near, near_half = parts
    first = mine[at, :].astype(F32) + half[at, :].astype(F32)
    return first + (near[there, :].astype(F32) + near_half[there, :].astype(F32))


def moved(at, by):
    return pl.ds(pl.multiple_of(at.start + by, CHUNK), CHUNK)


def over_totals(parts, other_ref, inputs, take):
    own = parts[0].shape[0] // 2

    def own_core(at, _):
        take(at, summed_rows(parts, at, moved(at, own)), inputs[0][at, :])

    def near_own_core(at, _):
        total = summed_rows(parts, moved(at, own), at)
        take(moved(at, 2 * own), total, inputs[2][at, :])

    def other(at, _):
        take(moved(at, own), other_ref[at, :].astype(F32), inputs[1][at, :])

    def near_other(at, _):
        total = other_ref[moved(at, own), :].astype(F32)
        take(moved(at, 3 * own), total, inputs[3][at, :])

    for step in (own_core, near_own_core, other, near_other):
        over_rows(own, step)


def last_kernel(*refs):
    inputs, far_ends, parts, refs = refs[:4], refs[4:8], refs[8:12], refs[12:]
    other_ref, vec_ref, far_ref, far_table_ref, far_mask_ref, *rest = refs
    far_parts, rest = rest[:4], rest[4:]
    slab_ref, sums_ref, far_hidden_ref, far_normed_ref, far_inv_std_ref, *rest = rest
    (table_ref, mask_ref, hidden_ref, get, put), rest = rest[:5], rest[5:]
    ahead, back, rest = rest[:2], rest[2:4], rest[4:]
    get, put = Copies(get), Copies(put)
    state, rest = State(rest[:10], put, (far_normed_ref, far_inv_std_ref)), rest[10:]
    grad_ref, heads_ref, w_ref, arrived, *scratch = rest
    slab = Slab(far_ref, heads_ref, w_ref, arrived)
    get.start(far_table_ref, table_ref)
    get.start(far_mask_ref, mask_ref)
    own = hidden_ref.shape[0]
    for quarter, ref in enumerate(far_ends):
        get.start(ref, grad_ref.at[quarter * own : (quarter + 1) * own, :])
    bias = vec_ref[0, BIAS_OUT : BIAS_OUT + 1, :]

    def enter(at, total, tokens):
        values = tokens.astype(F32) + total + bias
        scratch[3][at, :] = values
        normed, inv_std = row_norm(values)
        state.normed[at, :] = normed
        state.inv_std[at, :] = inv_std

    over_totals(parts, other_ref, inputs, enter)
    hidden_ref[...] = scratch[3][:own, :] + vec_ref[1, BIAS_OUT : BIAS_OUT + 1, :]
    put.start(hidden_ref, far_hidden_ref)
    forward(state, vec_ref.at[1], slab, get, table_ref, mask_ref, ahead, scratch[3])
    for ref, far_part_ref in zip(ahead, far_parts[:2], strict=True):
        put.start(ref, far_part_ref)
    backward(state, grad_ref, vec_ref.at[1], slab, table_ref, back, sums_ref, scratch, put, far_parts[2:])
    slab.give(slab_ref, arrived)
    put.wait()


def back_kernel(layers, *refs):
    inputs, parts, refs = refs[:4], refs[4:8], refs[8:]
    other_ref, normed_ref, inv_std_ref, later_ref, vec_ref, far_ref, place_ref, far_table_ref, *rest = refs
    far_state, rest = rest[:10], rest[10:]
    far_back, (slab_ref, kept_ref, table_ref, get, put, *rest) = rest[:2], rest[2:]
    back, state, rest = rest[:2], State(rest[2:12]), rest[12:]
    sums_ref, below_ref, small_ref, heads_ref, w_ref, arrived, *scratch = rest
    get, put = Copies(get), Copies(put)
    slab = Slab(far_ref, heads_ref, w_ref, arrived)
    get.start(far_table_ref, table_ref)
    for name, ref in zip(State.names, far_state, strict=True):
        get.start(ref, getattr(state, name))
    attn, hidden = state.o.shape[1], state.gl.shape[1]

    def enter(at, total, cotangent):
        grad = row_norm_back(total, normed_ref[at, :], inv_std_ref[at, :])
        below_ref[at, :] = grad + cotangent.astype(F32)

    over_totals(parts, other_ref, inputs, enter)
    kept_ref[...] = below_ref[: kept_ref.shape[0], :]
    slab.wait()
    get.wait()
    backward(state, below_ref, vec_ref.at[0], slab, table_ref, back, sums_ref, scratch, put, far_back)
    both = [sums_ref, later_ref]
    pad = jnp.zeros((8 - layers, attn), F32)
    qkv = jnp.concatenate([ref[SUM_QKV : SUM_QKV + 1, :] for ref in both] + [pad], axis=0)
    up = [ref[SUM_UP : SUM_UP + 1, :hidden] for ref in both] + [pad[:, :hidden]]
    up = jnp.concatenate(up, axis=0)
    spread = [
        dot(values.astype(BF), one_hot(place_ref, at, values.shape[1]))[:layers]
        for values, at in ((qkv, 0), (qkv, 1), (up, 2), (up, 3))
    ]
    small = [ref[: SUM_SHIFT_B + 1, :] for ref in both] + spread
    used = 9 * layers
    small = jnp.concatenate(small + [jnp.zeros((LANES - used, attn), F32)], axis=0)
    small_ref[...] = jnp.transpose(small).astype(BF)
    columns = attn + 2 * hidden
    copy = pltpu.make_async_copy(small_ref, slab_ref.at[:, columns:], arrived.at[2])
    copy.start()
    slab.give(slab_ref, arrived)
    copy.wait()
    put.wait()


def slabs_kernel(layers, core_ref, *refs):
    far, sends, refs = refs[:9], refs[9 : 9 + layers], refs[9 + layers :]
    local, (rows_ref, bias_ref, arrived) = refs[:9], refs[9:]
    copies = [
        pltpu.make_async_copy(src, dst, arrived.at[i])
        for i, (src, dst) in enumerate(zip(far, local, strict=True))
    ]
    for copy in copies:
        copy.start()
    for copy in copies:
        copy.wait()
    (qkv_ref, out_ref, up_ref, down_ref), vectors, biases = local[:4], local[4:7], local[7:9]
    depth, width_out = qkv_ref.shape[1], out_ref.shape[2] // 2
    hidden = up_ref.shape[2] // 4
    low = core_ref[0] == 0

    def half(values):
        width = values.shape[1] // 2
        return jnp.where(low, values[:, :width], values[:, width:])

    rows_ref[...] = jnp.zeros_like(rows_ref)
    at = 0
    for layer in range(layers):
        for ref in vectors:
            rows_ref[at : at + 2, :depth] = ref[layer].astype(F32)
            at += 2
    lanes = lax.broadcasted_iota(jnp.int32, bias_ref.shape, 1)
    for ref in biases:
        bias_ref[...] = jnp.zeros_like(bias_ref)
        bias_ref[:layers, : ref.shape[1]] = ref[...].astype(F32)
        for values in (bias_ref[...], pltpu.roll(bias_ref[...], LANES - depth, 1)):
            rows_ref[at : at + layers, :] = jnp.where(lanes < depth, values, 0.0)[:layers]
            at += layers
    small = jnp.transpose(rows_ref[...])[:depth].astype(BF)
    for layer, send_ref in enumerate(sends):
        qkv, out = half(qkv_ref[layer]), half(out_ref[layer])
        up, down = half(up_ref[layer]), half(down_ref[layer])
        attn = []
        for head in range(width_out // HS):
            at = head * 3 * HS
            attn += [qkv[:, at : at + 3 * HS], out[:, head * HS : (head + 1) * HS]]
        attn = jnp.concatenate(attn, axis=1)
        for z in (0, 1):
            at = slice(z * hidden, (z + 1) * hidden)
            block = [attn, up[:, at], down[:, at]] + ([small] if layer == 0 else [])
            block = jnp.concatenate(block, axis=1)
            for owner in range(send_ref.shape[0]):
                if owner // NEAR % 2 == z:
                    send_ref[owner] = block


def gather_kernel(layers, *refs):
    got, (all_ref, small_ref, pad_ref) = refs[:layers], refs[layers:]
    owners, depth, width = got[1].shape
    hidden = (all_ref.shape[2] - width) // 2
    attn = width - 2 * hidden

    def sums_of(got_ref, columns):
        sums = []
        for z in (0, 1):
            senders = [owner for owner in range(owners) if owner // NEAR % 2 == z]
            total = got_ref[senders[0], :, columns].astype(F32)
            for owner in senders[1:]:
                total = total + got_ref[owner, :, columns].astype(F32)
            sums.append(total)
        return sums

    for layer in range(layers):
        first, second = sums_of(got[layer], slice(0, attn))
        all_ref[layer, :, :attn] = (first + second).astype(BF)
        for kind in (0, 1):
            begin = attn + kind * hidden
            first, second = sums_of(got[layer], slice(begin, begin + hidden))
            begin = attn + 2 * kind * hidden
            all_ref[layer, :, begin : begin + hidden] = first.astype(BF)
            all_ref[layer, :, begin + hidden : begin + 2 * hidden] = second.astype(BF)
    first, second = sums_of(got[0], slice(width, width + LANES))
    pad_ref[...] = jnp.zeros_like(pad_ref)
    pad_ref[:depth, :] = first + second
    small_ref[...] = jnp.transpose(pad_ref[...])[: small_ref.shape[0]]


def finish_kernel(layers, core_ref, mine_ref, theirs_ref, *rest):
    smalls, (qkv_ref, out_ref, up_ref, down_ref, *vectors) = rest[:4], rest[4:]
    bias_qkv_ref, bias_up_ref, bias_out_ref, gain_ref, shift_ref = vectors
    width_qkv, width_out, width_up = (r.shape[2] // 2 for r in (qkv_ref, out_ref, up_ref))
    depth, heads = qkv_ref.shape[1], width_out // HS
    attn = heads * HEAD
    low = core_ref[0] == 0
    for layer in range(layers):
        mine, theirs = mine_ref[layer].astype(F32), theirs_ref[layer].astype(F32)
        sides = (jnp.where(low, mine, theirs), jnp.where(low, theirs, mine))
        for side, values in enumerate(sides):
            at = side * width_up
            up_ref[layer, :, at : at + width_up] = values[:, attn : attn + width_up]
            down_ref[layer, :, at : at + width_up] = values[:, attn + width_up :]
        starts = [(values, head * HEAD) for values in sides for head in range(heads)]
        qkv_ref[layer] = jnp.concatenate([v[:, at : at + 3 * HS] for v, at in starts], axis=1)
        out_ref[layer] = jnp.concatenate([v[:, at + 3 * HS : at + HEAD] for v, at in starts], axis=1)
    mine, core, half, core_half = (ref[...] for ref in smalls)
    vectors = (mine + half) + (core + core_half)
    for layer in range(layers):
        rows = vectors[5 * layer : 5 * layer + 5, :depth]
        bias_out_ref[layer, 0:1, :] = rows[:1]
        bias_out_ref[layer, 1:2, :] = rows[:1]
        gain_ref[layer] = rows[1:3]
        shift_ref[layer] = rows[3:5]
    biases = mine + core
    at = 5 * layers
    for ref in (bias_qkv_ref, bias_up_ref):
        first, second = biases[at : at + layers], biases[at + layers : at + 2 * layers]
        lanes = lax.broadcasted_iota(jnp.int32, first.shape, 1)
        both = jnp.where(lanes < depth, first, pltpu.roll(second, depth, 1))
        ref[...] = both[:, : ref.shape[1]]
        at += 2 * layers


def call(kernel, outs, scratch, flops, *args, far=(), far_outs=(), limit=VMEM_BYTES, **more):
    def space(at, arg, far):
        if at in far:
            return pltpu.HBM
        return pltpu.SMEM if arg.shape == (1,) else pltpu.VMEM

    return pl.pallas_call(
        kernel,
        out_shape=outs,
        in_specs=[pl.BlockSpec(memory_space=space(at, arg, far)) for at, arg in enumerate(args)],
        out_specs=[
            pl.BlockSpec(memory_space=space(at, out, far_outs)) for at, out in enumerate(outs)
        ],
        scratch_shapes=scratch,
        compiler_params=pltpu.CompilerParams(vmem_limit_bytes=limit),
        cost_estimate=pl.CostEstimate(flops=flops, bytes_accessed=8_000_000, transcendentals=0),
        **more,
    )(*args)


def core_rows_summed(kept, sent):
    return (kept.astype(F32) + other_core(sent).astype(F32)).astype(BF)


def parts_of_sum(mine):
    return mine, other_half(mine), near_group(mine), near_other_half(mine)


def other_rows(parts):
    mine, half, near, near_half = (p.astype(F32).reshape(2, -1, p.shape[1]) for p in parts)
    total = (mine + half) + (near[::-1] + near_half[::-1])
    return other_core(total.astype(BF).reshape(parts[0].shape))


def own_parts(kept, sent):
    mine = core_rows_summed(kept, sent)
    own = mine.shape[0] // 2
    return mine[:own], other_half(mine[:own]), near_group(mine[own:]), near_other_half(mine[own:])


def total_of(parts):
    mine, half, near, near_half = (part.astype(F32) for part in parts)
    return (mine + half) + (near + near_half)


def rotation(positions):
    exponents = jnp.arange(ROT // 2, dtype=F32) * (2.0 / ROT)
    inverse = jnp.power(10000.0, -exponents)
    phase = positions.astype(F32)[:, None] * inverse[None, :]
    cos, sin = jnp.cos(phase), jnp.sin(phase)
    none = jnp.zeros_like(sin)
    rest = jnp.zeros((positions.shape[0], HS - ROT), F32)
    tables = [[cos, cos, rest + 1.0], [-sin, none, rest], [none, sin, rest]]
    return jnp.stack([jnp.concatenate(t + t, axis=1) for t in tables])


def bias_places(owners, depth, starts, widths, shards):
    owner = jnp.arange(owners * depth, dtype=jnp.int32) // depth
    inner = jnp.arange(owners * depth, dtype=jnp.int32) % depth
    rows = []
    for start, width, shard, head in zip(starts, widths, shards, (3 * HS, None), strict=True):
        for first in (0, depth):
            at = owner * shard + inner + first - start
            fits = (inner + first < shard) & (at >= 0) & (at < width)
            if head is not None:
                at = at // head * HEAD + at % head
            rows.append(jnp.where(fits, at, -1))
    return jnp.stack(rows + rows)


def per_device(
    tokens,
    cotangent,
    doc_lens,
    block_pos,
    w_qkv,
    w_out,
    w_up,
    w_down,
    b_qkv,
    b_up,
    out_bias,
    norm_gain,
    norm_bias,
):
    row_count = tokens.shape[0]
    block_rows = row_count // 2
    core = lax.axis_index("ctx")
    owners = lax.axis_size("fsdp")
    layers, depth, width_qkv = w_qkv.shape
    width_qkv, width_out, hidden = width_qkv // 2, w_out.shape[1] // 2, w_up.shape[2] // 4
    place_z = lax.axis_index("fsdp") // NEAR % 2
    heads = width_out // HS
    attn = heads * HEAD
    width = attn + 2 * hidden
    wide = owners * depth
    rows = 4 * row_count

    core_at = core.astype(jnp.int32).reshape(1)
    sds = jax.ShapeDtypeStruct
    raw = (
        w_qkv,
        w_out.transpose(0, 2, 1),
        w_up,
        w_down.transpose(0, 2, 1),
        out_bias,
        norm_gain,
        norm_bias,
        b_qkv,
        b_up,
    )
    sends = call(
        functools.partial(slabs_kernel, layers),
        (
            sds((owners, depth, width + LANES), BF),
            sds((owners, depth, width), BF),
        ),
        [pltpu.VMEM(a.shape, a.dtype) for a in raw]
        + [pltpu.VMEM((LANES, LANES), F32), pltpu.VMEM((8, LANES), F32)]
        + [pltpu.SemaphoreType.DMA((len(raw),))],
        1000,
        core_at,
        *raw,
        far=range(1, 1 + len(raw)),
    )
    first, second = (exchanged(blocks).reshape(wide, -1) for blocks in sends)
    starts, ends = ((own, near_other_half(own)) for own in (tokens, cotangent))
    starts, ends = ((o, other_core(o), n, other_core(n)) for o, n in (starts, ends))
    offsets = jnp.arange(block_rows, dtype=jnp.int32)
    positions = (block_pos[0][:, None] * block_rows + offsets[None, :]).reshape(2, row_count)
    positions = jnp.where(core == 0, positions, positions[::-1]).reshape(-1)
    doc_ends = jnp.cumsum(doc_lens[0])
    docs = jnp.sum((positions[:, None] >= doc_ends[None, :]).astype(jnp.int32), axis=1)
    allowed = (docs[:, None] == docs[None, :]) & (positions[None, :] <= positions[:, None])
    mask = jnp.where(allowed, 0.0, MASKED).astype(F32)
    table = rotation(positions)
    place = bias_places(
        owners,
        depth,
        (core * width_qkv, (2 * core + place_z) * hidden),
        (width_qkv, hidden),
        (b_qkv.shape[1], b_up.shape[1]),
    )

    flops = 2 * rows * wide * width
    part = sds((rows // 2, wide), BF)
    kept = State.shapes(rows, wide, heads, hidden)

    def vmem(*arrays):
        return [pltpu.VMEM(array.shape, array.dtype) for array in arrays]

    def copies(*counts):
        return [pltpu.SemaphoreType.DMA((count,)) for count in counts]

    slab_scratch = [
        pltpu.VMEM((wide, attn), BF),
        pltpu.VMEM((wide, 2 * hidden), BF),
        pltpu.SemaphoreType.DMA((3,)),
    ]
    kept_part, sent_part, vec, *state = call(
        functools.partial(first_kernel, layers),
        (part, part, sds((layers, VECTORS, wide), F32), *State.shapes(rows, wide, heads, hidden)),
        [
            *vmem(part, part, table, mask),
            *copies(2, 12),
            pltpu.VMEM((rows, wide), F32),
            pltpu.VMEM((wide, LANES), BF),
            *slab_scratch,
            *vmem(*kept),
        ],
        flops,
        *starts,
        first,
        place,
        table,
        mask,
        far=(4, 6, 7),
        far_outs=(0, 1, *range(3, 13)),
    )
    parts = parts_of_sum(core_rows_summed(kept_part, sent_part))
    scratch = [
        pltpu.VMEM((rows, wide), BF),
        pltpu.VMEM((rows, hidden), BF),
        pltpu.VMEM((rows // 2, attn), BF),
        pltpu.VMEM((rows, wide), F32),
        pltpu.VMEM((rows, wide), F32),
    ]
    *sums, slab, later_sums, result, normed, inv_std = call(
        last_kernel,
        (
            *(part,) * 4,
            sds((wide, width), BF),
            sds((8, wide), F32),
            sds((row_count, wide), F32),
            *kept[:2],
        ),
        [
            *vmem(table, mask, sds((row_count, wide), F32)),
            *copies(6, 7),
            *vmem(part, part, part, part, *kept, sds((rows, wide), BF)),
            *slab_scratch,
            *scratch,
        ],
        3 * flops,
        *starts,
        *ends,
        *parts,
        other_rows(parts),
        vec,
        second,
        table,
        mask,
        far=(4, 5, 6, 7, 14, 15, 16),
        far_outs=(0, 1, 2, 3, 4, 6, 7, 8),
    )
    parts = parts_of_sum(core_rows_summed(*sums[2:]))
    slab, *sums = lax.optimization_barrier((slab, *sums[:2], *parts))
    ahead, parts = own_parts(*sums[:2]), sums[2:]
    later = exchanged(slab.reshape(owners, depth, -1))
    kept_part, sent_part, slab, grad_below = call(
        functools.partial(back_kernel, layers),
        (part, part, sds((wide, width + LANES), BF), sds((row_count, wide), F32)),
        [
            *vmem(table),
            *copies(11, 2),
            *vmem(part, part, *kept, later_sums, sds((rows, wide), F32), sds((wide, LANES), BF)),
            *slab_scratch,
            *scratch,
        ],
        2 * flops,
        *ends,
        *parts,
        other_rows(parts),
        normed,
        inv_std,
        later_sums,
        vec,
        first,
        place,
        table,
        *state,
        far=(13, *range(15, 26)),
        far_outs=(0, 1, 2),
    )
    earlier = exchanged(slab.reshape(owners, depth, -1))
    below = own_parts(kept_part, sent_part)

    mine, small = call(
        functools.partial(gather_kernel, layers),
        (sds((layers, depth, width + 2 * hidden), BF), sds((24, LANES), F32)),
        [pltpu.VMEM((LANES, LANES), F32)],
        1000,
        earlier,
        later,
    )
    result = (result + total_of(ahead)).astype(BF)
    mine, small, below = lax.optimization_barrier((mine, small, below))
    total = row_norm_back(total_of(below), state[0][:row_count], state[1][:row_count])
    grad_tokens = (grad_below + total).astype(BF)
    grad_qkv, grad_out, grad_up, grad_down, *vectors = call(
        functools.partial(finish_kernel, layers),
        tuple(
            sds(shape, F32)
            for shape in (
                w_qkv.shape,
                (layers, depth, w_out.shape[1]),
                w_up.shape,
                (layers, depth, w_down.shape[1]),
                b_qkv.shape,
                b_up.shape,
                out_bias.shape,
                norm_gain.shape,
                norm_bias.shape,
            )
        ),
        [],
        1000,
        core_at,
        mine,
        other_core(mine),
        small,
        other_core(small),
        other_half(small),
        other_core_and_half(small),
    )
    return (
        result,
        grad_tokens,
        grad_qkv,
        grad_out.transpose(0, 2, 1),
        grad_up,
        grad_down.transpose(0, 2, 1),
        *vectors,
    )


def solution(mesh):
    in_specs = (
        P(("fsdp", "ctx"), None),
        P(("fsdp", "ctx"), None),
        P("fsdp", None),
        P("fsdp", None),
        P(None, "fsdp", "tp"),
        P(None, "tp", "fsdp"),
        P(None, "fsdp", "tp"),
        P(None, "tp", "fsdp"),
        P(None, ("tp", "fsdp")),
        P(None, ("tp", "fsdp")),
        P(None, None, "fsdp"),
        P(None, None, "fsdp"),
        P(None, None, "fsdp"),
    )
    out_specs = (P(("fsdp", "ctx"), None), P(("fsdp", "ctx"), None), *in_specs[4:])
    return jax.shard_map(
        per_device, mesh=mesh, in_specs=in_specs, out_specs=out_specs, check_vma=False
    )
```

```python
import functools

import jax
import jax.numpy as jnp
from jax import lax
from jax.experimental import pallas as pl
from jax.experimental.pallas import tpu as pltpu
from jax.sharding import PartitionSpec as P

HS = 64
ROT = 16
EPSILON = 1e-05
MASKED = -1e30
F32 = jnp.float32
BF = jnp.bfloat16
SWAP = [(0, 1), (1, 0)]
NEAR = 4
LANES = 128
CHUNK = 128
HEAD = 4 * HS
SCALE = HS ** (-0.5)
VMEM_BYTES = 62 * 1024 * 1024
GAIN_A, GAIN_B, SHIFT_A, SHIFT_B, BIAS_QKV, BIAS_UP, BIAS_OUT = range(7)
VECTORS = 8
SUM_OUT, SUM_GAIN_A, SUM_GAIN_B, SUM_SHIFT_A, SUM_SHIFT_B, SUM_QKV, SUM_UP = range(7)


def other_core(values):
    return lax.ppermute(values, "ctx", SWAP)


def other_half(values):
    return lax.ppermute(values, "tp", SWAP)


def other_core_and_half(values):
    return lax.ppermute(values, ("ctx", "tp"), [(0, 3), (1, 2), (2, 1), (3, 0)])


def near_group(values):
    owners = lax.axis_size("fsdp")
    return lax.ppermute(values, "fsdp", [(f, f ^ NEAR) for f in range(owners)])


def near_other_half(values):
    owners = lax.axis_size("fsdp")
    pairs = [(2 * f + t, 2 * (f ^ NEAR) + 1 - t) for f in range(owners) for t in (0, 1)]
    return lax.ppermute(values, ("fsdp", "tp"), pairs)


def exchanged(blocks):
    return lax.all_to_all(blocks, "fsdp", 0, 0, tiled=True)


def dot(left, right, along=(1, 0)):
    dims = (((along[0],), (along[1],)), ((), ()))
    return lax.dot_general(left, right, dims, preferred_element_type=F32)


def over_rows(rows, step, carry=None, start=0):
    def body(at, kept):
        return step(pl.ds(pl.multiple_of(at * CHUNK, CHUNK), CHUNK), kept)

    return lax.fori_loop(start // CHUNK, rows // CHUNK, body, carry)


def by_eights(values):
    return values.reshape(-1, 8, values.shape[-1]).sum(axis=0)


def whole_sum(eights):
    return jnp.sum(eights, axis=0, keepdims=True)


def turned(tile, cos, left, right):
    return (
        tile * cos
        + pltpu.roll(tile, LANES - ROT // 2, 1) * left
        + pltpu.roll(tile, ROT // 2, 1) * right
    )


def row_norm(values):
    centered = values - jnp.mean(values, axis=-1, keepdims=True)
    inv_std = lax.rsqrt(jnp.mean(centered * centered, axis=-1, keepdims=True) + EPSILON)
    return centered * inv_std, inv_std


def row_norm_back(total, normed, inv_std):
    return inv_std * (
        total
        - jnp.mean(total, axis=-1, keepdims=True)
        - normed * jnp.mean(total * normed, axis=-1, keepdims=True)
    )


def one_hot(place_ref, at, width):
    rows = lax.broadcasted_iota(jnp.int32, (width, place_ref.shape[1]), 0)
    return (rows == place_ref[at : at + 1, :]).astype(F32).astype(BF)


class Slab:
    def __init__(self, far_heads_ref, far_ref, heads_ref, w_ref, arrived):
        self.heads_ref, self.w_ref = heads_ref, w_ref
        self.copies = [
            pltpu.make_async_copy(far_heads_ref, heads_ref, arrived.at[0]),
            pltpu.make_async_copy(far_ref, w_ref, arrived.at[1]),
        ]
        for copy in self.copies:
            copy.start()

    def wait(self):
        for copy in self.copies:
            copy.wait()
        return self.heads_ref, self.w_ref

    def give(self, far_heads_ref, far_ref, sent):
        copies = [
            pltpu.make_async_copy(self.heads_ref, far_heads_ref, sent.at[0]),
            pltpu.make_async_copy(self.w_ref, far_ref, sent.at[1]),
        ]
        for copy in copies:
            copy.start()
        for copy in copies:
            copy.wait()


class Copies:
    def __init__(self, semaphores):
        self.semaphores, self.started = semaphores, []

    def start(self, src, dst):
        copy = pltpu.make_async_copy(src, dst, self.semaphores.at[len(self.started)])
        copy.start()
        self.started.append(copy)

    def wait(self, begin=0, end=None):
        for copy in self.started[begin:end]:
            copy.wait()


class State:
    names = ("normed", "inv_std", "a", "m", "qk", "v", "p", "o", "gl", "slope")

    def __init__(self, refs, copies=None, far=()):
        for name, ref in zip(self.names, refs, strict=True):
            setattr(self, name, ref)
        self.copies, self.far = copies, dict(zip(self.names, far))

    def ready(self, *names):
        for name in names:
            if name in self.far:
                self.copies.start(getattr(self, name), self.far[name])

    @staticmethod
    def shapes(rows, depth, heads, hidden):
        group = rows // 2
        return (
            jax.ShapeDtypeStruct((rows, depth), F32),
            jax.ShapeDtypeStruct((rows, 1), F32),
            jax.ShapeDtypeStruct((group, depth), BF),
            jax.ShapeDtypeStruct((rows, depth), BF),
            jax.ShapeDtypeStruct((group, heads * 2 * HS), BF),
            jax.ShapeDtypeStruct((group, heads * HS), BF),
            jax.ShapeDtypeStruct((heads, group, group), F32),
            jax.ShapeDtypeStruct((group, heads * HEAD), BF),
            jax.ShapeDtypeStruct((rows, hidden), BF),
            jax.ShapeDtypeStruct((rows, hidden), F32),
        )


def places(rows):
    quarter = rows // 4
    return [(0, 0, 0), (quarter, 1, 0), (2 * quarter, 0, quarter), (3 * quarter, 1, quarter)]


def forward(state, vec_ref, slab, near_copies, table_ref, mask_ref, parts, wide_ref):
    rows, depth = state.normed.shape
    group = rows // 2
    heads = state.v.shape[1] // HS
    hidden = state.gl.shape[1]

    def affine_a(at, _):
        state.a[at, :] = (
            state.normed[at, :] * vec_ref[GAIN_A : GAIN_A + 1, :]
            + vec_ref[SHIFT_A : SHIFT_A + 1, :]
        ).astype(BF)

    def affine_b(at, _):
        state.m[at, :] = (
            state.normed[at, :] * vec_ref[GAIN_B : GAIN_B + 1, :]
            + vec_ref[SHIFT_B : SHIFT_B + 1, :]
        ).astype(BF)

    state.ready("normed", "inv_std")
    over_rows(group, affine_a)
    over_rows(rows, affine_b)
    state.ready("a", "m")
    heads_ref, w_ref = slab.wait()
    near_copies.wait()
    wide_ref[:group, :] = dot(state.a[...], heads_ref[...])
    state.o[...] = jnp.zeros_like(state.o)
    for head in range(heads):
        at = head * HEAD
        bias = vec_ref[BIAS_QKV : BIAS_QKV + 1, at : at + HEAD]
        tile = wide_ref[:group, at : at + LANES] + bias[:, :LANES]
        tile = turned(tile, table_ref[0], table_ref[1], table_ref[2]).astype(BF)
        value = wide_ref[:group, at + 2 * HS : at + 3 * HS] + bias[:, 2 * HS : 3 * HS]
        value = value.astype(BF)
        state.qk[:, head * LANES : (head + 1) * LANES] = tile
        state.v[:, head * HS : (head + 1) * HS] = value
        half = group // 2
        for top in (0, half):
            scores = dot(tile[top : top + half, :HS], tile[:, HS:], (1, 1))
            scores = scores * SCALE + mask_ref[top : top + half, :]
            exponent = jnp.exp(scores - jnp.max(scores, axis=1, keepdims=True))
            share = exponent * (1.0 / jnp.sum(exponent, axis=1, keepdims=True))
            state.p[head, top : top + half, :] = share
            state.o[top : top + half, at + 3 * HS : at + HEAD] = dot(
                share.astype(BF), value
            ).astype(BF)
    state.ready("qk", "v", "p", "o")
    wide_ref[:, :hidden] = dot(state.m[...], w_ref[:, :hidden])

    def gelu(at, _):
        up = wide_ref[at, :hidden] + vec_ref[BIAS_UP : BIAS_UP + 1, :hidden]
        below = 0.5 + 0.5 * lax.erf(up * (0.5**0.5))
        state.gl[at, :] = (up * below).astype(BF)
        state.slope[at, :] = below + up * (jnp.exp(-0.5 * up * up) * 0.3989422804014327)

    over_rows(rows, gelu)
    state.ready("gl", "slope")
    down = w_ref[:, hidden : 2 * hidden]
    part = dot(state.o[...], heads_ref[...], (1, 1))
    half = group // 2
    part = (part + dot(state.gl[:group, :], down, (1, 1))).astype(BF)
    near = dot(state.gl[group:, :], down, (1, 1)).astype(BF)
    for core, part_ref in enumerate(parts):
        at = core * half
        part_ref[:half, :] = part[at : at + half]
        part_ref[half:, :] = near[at : at + half]


def backward(
    state, grad_ref, vec_ref, slab, table_ref, parts, sums_ref, scratch, put, far_parts
):
    low_ref, up_ref, qkv_ref, wide_ref, deep_ref = scratch
    heads_ref, w_ref = slab.heads_ref, slab.w_ref
    rows, depth = state.normed.shape
    group = rows // 2
    heads = state.v.shape[1] // HS
    attn, hidden = heads * HEAD, state.gl.shape[1]

    def lower(at, total):
        grad = grad_ref[at, :].astype(F32)
        low_ref[at, :] = grad.astype(BF)
        return total + by_eights(grad)

    total = over_rows(rows, lower, jnp.zeros((8, depth), F32))
    sums_ref[SUM_OUT : SUM_OUT + 1, :] = whole_sum(total) * 0.125
    low = low_ref[...]
    wide_ref[:, :hidden] = dot(low, w_ref[:, hidden : 2 * hidden])

    def through_gelu(at, total):
        up = (wide_ref[at, :hidden] * state.slope[at, :]).astype(BF)
        up_ref[at, :] = up
        return total + by_eights(up.astype(F32))

    total = over_rows(rows, through_gelu, jnp.zeros((8, hidden), F32))
    sums_ref[SUM_UP : SUM_UP + 1, :hidden] = whole_sum(total)
    wide_ref[:group, :] = dot(low_ref[:group, :], heads_ref[...])
    for head in range(heads):
        at = head * HEAD
        tile = state.qk[:, head * LANES : (head + 1) * LANES]
        query, key = tile[:, :HS], tile[:, HS:]
        value = state.v[:, head * HS : (head + 1) * HS]
        out = wide_ref[:group, at + 3 * HS : at + HEAD].astype(BF)
        half = group // 2
        grad_value, grad_key, grad_query = 0.0, 0.0, []
        for top in (0, half):
            share = state.p[head, top : top + half, :]
            grad = dot(out[top : top + half], value, (1, 1))
            delta = jnp.sum(share * grad, axis=1, keepdims=True)
            low_scores = (share * (grad - delta)).astype(BF)
            grad_value = grad_value + dot(share.astype(BF), out[top : top + half], (0, 0))
            grad_query.append(dot(low_scores, key))
            grad_key = grad_key + dot(low_scores, query[top : top + half], (0, 0))
        both = jnp.concatenate([jnp.concatenate(grad_query, axis=0), grad_key], axis=1) * SCALE
        both = turned(both, table_ref[0], -table_ref[1], -table_ref[2])
        qkv_ref[:, at : at + LANES] = both.astype(BF)
        qkv_ref[:, at + LANES : at + HEAD] = jnp.concatenate(
            [grad_value, jnp.zeros_like(grad_value)], axis=1
        ).astype(BF)

    def count_qkv(at, total):
        return total + by_eights(qkv_ref[at, :].astype(F32))

    total = over_rows(group, count_qkv, jnp.zeros((8, attn), F32))
    sums_ref[SUM_QKV : SUM_QKV + 1, :] = whole_sum(total)
    wide_ref[:group, :] = dot(qkv_ref[...], heads_ref[...], (1, 1))
    deep_ref[...] = dot(up_ref[...], w_ref[:, :hidden], (1, 1))

    def through_norms(with_first, part_ref, begin, to):
        def step(at, totals):
            there, at = moved(at, to), moved(at, begin)
            second, normed = deep_ref[at, :], state.normed[at, :]
            total, new = second * vec_ref[GAIN_B : GAIN_B + 1, :], (second * normed, second)
            if with_first:
                first = wide_ref[at, :]
                total = total + first * vec_ref[GAIN_A : GAIN_A + 1, :]
                new = (*new, first * normed, first)
            part_ref[there, :] = total.astype(BF)
            return tuple(old + by_eights(term) for old, term in zip(totals, new, strict=True))

        return step

    totals = (jnp.zeros((8, depth), F32),) * 4
    for begin, core, to in places(rows):
        count = 4 if begin < group else 2
        step = through_norms(begin < group, parts[core], begin, to)
        totals = (*over_rows(rows // 4, step, totals[:count]), *totals[count:])
    for row, total in zip((SUM_GAIN_B, SUM_SHIFT_B, SUM_GAIN_A, SUM_SHIFT_A), totals, strict=True):
        sums_ref[row : row + 1, :] = whole_sum(total)
    for ref, far_part_ref in zip(parts, far_parts, strict=True):
        put.start(ref, far_part_ref)
    heads_grad = dot(state.a[...], qkv_ref[...], (0, 0))
    heads_grad = heads_grad + dot(low_ref[:group, :], state.o[...], (0, 0))
    heads_ref[...] = heads_grad.astype(BF)
    w_ref[:, :hidden] = dot(state.m[...], up_ref[...], (0, 0)).astype(BF)
    w_ref[:, hidden : 2 * hidden] = dot(low, state.gl[...], (0, 0)).astype(BF)


def first_kernel(layers, *refs):
    inputs, (far_ref, place_ref, far_table_ref, far_mask_ref, *rest) = refs[:4], refs[4:]
    far_parts, vec_ref, far_state, rest = rest[:2], rest[2], rest[3:13], rest[13:]
    parts, (table_ref, mask_ref, get, put), rest = rest[:2], rest[2:6], rest[6:]
    wide_ref, small_ref, heads_ref, w_ref, arrived, *state = rest
    get, put = Copies(get), Copies(put)
    state = State(state, put, far_state)
    attn = state.o.shape[1]
    hidden = state.gl.shape[1]
    width = attn + 2 * hidden
    copy = pltpu.make_async_copy(far_ref.at[:, width:], small_ref, arrived.at[2])
    copy.start()
    slab = Slab(far_ref.at[:, :attn], far_ref.at[:, attn:width], heads_ref, w_ref, arrived)
    get.start(far_table_ref, table_ref)
    get.start(far_mask_ref, mask_ref)
    copy.wait()
    small = jnp.transpose(small_ref[...].astype(F32))
    at = 6 * layers
    biases = small[at : at + 4 * layers].astype(BF)
    bias_qkv = dot(biases[:layers], one_hot(place_ref, 0, attn), (1, 1)) + dot(
        biases[layers : 2 * layers], one_hot(place_ref, 1, attn), (1, 1)
    )
    bias_up = dot(biases[2 * layers : 3 * layers], one_hot(place_ref, 2, hidden), (1, 1)) + dot(
        biases[3 * layers :], one_hot(place_ref, 3, hidden), (1, 1)
    )
    for layer in range(layers):
        rows = small[6 * layer : 6 * layer + 6]
        vec_ref[layer, GAIN_A : SHIFT_B + 1, :] = rows[2:]
        vec_ref[layer, BIAS_QKV : BIAS_QKV + 1, :] = bias_qkv[layer : layer + 1]
        vec_ref[layer, BIAS_UP : BIAS_UP + 1, :hidden] = bias_up[layer : layer + 1]
        vec_ref[layer, BIAS_OUT : BIAS_OUT + 1, :] = rows[0:1] + rows[1:2]
        vec_ref[layer, BIAS_OUT + 1 : VECTORS, :] = rows[0:1]

    for quarter, ref in enumerate(inputs):

        def enter(at, _, ref=ref, begin=quarter * ref.shape[0]):
            normed, inv_std = row_norm(ref[at, :].astype(F32))
            state.normed[moved(at, begin), :] = normed
            state.inv_std[moved(at, begin), :] = inv_std

        over_rows(ref.shape[0], enter)
    forward(state, vec_ref.at[0], slab, get, table_ref, mask_ref, parts, wide_ref)
    for ref, far_part_ref in zip(parts, far_parts, strict=True):
        put.start(ref, far_part_ref)
    put.wait()


def summed_rows(parts, at, there):
    mine, half, near, near_half = parts
    first = mine[at, :].astype(F32) + half[at, :].astype(F32)
    return first + (near[there, :].astype(F32) + near_half[there, :].astype(F32))


def moved(at, by):
    return pl.ds(pl.multiple_of(at.start + by, CHUNK), CHUNK)


def over_totals(parts, other_ref, inputs, take):
    own = parts[0].shape[0] // 2

    def own_core(at, _):
        take(at, summed_rows(parts, at, moved(at, own)), inputs[0][at, :])

    def near_own_core(at, _):
        total = summed_rows(parts, moved(at, own), at)
        take(moved(at, 2 * own), total, inputs[2][at, :])

    def other(at, _):
        take(moved(at, own), other_ref[at, :].astype(F32), inputs[1][at, :])

    def near_other(at, _):
        total = other_ref[moved(at, own), :].astype(F32)
        take(moved(at, 3 * own), total, inputs[3][at, :])

    for step in (own_core, near_own_core, other, near_other):
        over_rows(own, step)


def last_kernel(*refs):
    inputs, far_ends, parts, refs = refs[:4], refs[4:8], refs[8:12], refs[12:]
    other_ref, vec_ref, far_ref, far_table_ref, far_mask_ref, *rest = refs
    far_parts, rest = rest[:4], rest[4:]
    slab_ref, sums_ref, far_hidden_ref, far_normed_ref, far_inv_std_ref, *rest = rest
    (table_ref, mask_ref, hidden_ref, get, put), rest = rest[:5], rest[5:]
    ahead, back, rest = rest[:2], rest[2:4], rest[4:]
    get, put = Copies(get), Copies(put)
    state, rest = State(rest[:10], put, (far_normed_ref, far_inv_std_ref)), rest[10:]
    grad_ref, heads_ref, w_ref, arrived, *scratch = rest
    attn, width = heads_ref.shape[1], heads_ref.shape[1] + w_ref.shape[1]
    slab = Slab(far_ref.at[:, :attn], far_ref.at[:, attn:width], heads_ref, w_ref, arrived)
    get.start(far_table_ref, table_ref)
    get.start(far_mask_ref, mask_ref)
    own = hidden_ref.shape[0]
    for quarter, ref in enumerate(far_ends):
        get.start(ref, grad_ref.at[quarter * own : (quarter + 1) * own, :])
    bias = vec_ref[0, BIAS_OUT : BIAS_OUT + 1, :]

    def enter(at, total, tokens):
        values = tokens.astype(F32) + total + bias
        scratch[3][at, :] = values
        normed, inv_std = row_norm(values)
        state.normed[at, :] = normed
        state.inv_std[at, :] = inv_std

    over_totals(parts, other_ref, inputs, enter)
    hidden_ref[...] = scratch[3][:own, :] + vec_ref[1, BIAS_OUT : BIAS_OUT + 1, :]
    put.start(hidden_ref, far_hidden_ref)
    forward(state, vec_ref.at[1], slab, get, table_ref, mask_ref, ahead, scratch[3])
    for ref, far_part_ref in zip(ahead, far_parts[:2], strict=True):
        put.start(ref, far_part_ref)
    backward(state, grad_ref, vec_ref.at[1], slab, table_ref, back, sums_ref, scratch, put, far_parts[2:])
    slab.give(slab_ref.at[:, :attn], slab_ref.at[:, attn:width], arrived)
    put.wait()


def back_kernel(layers, *refs):
    inputs, parts, refs = refs[:4], refs[4:8], refs[8:]
    other_ref, normed_ref, inv_std_ref, later_ref, vec_ref, far_ref, place_ref, far_table_ref, *rest = refs
    far_state, rest = rest[:10], rest[10:]
    far_back, (slab_ref, kept_ref, table_ref, get, put, *rest) = rest[:2], rest[2:]
    back, state, rest = rest[:2], State(rest[2:12]), rest[12:]
    sums_ref, below_ref, small_ref, heads_ref, w_ref, arrived, *scratch = rest
    get, put = Copies(get), Copies(put)
    attn, width = heads_ref.shape[1], heads_ref.shape[1] + w_ref.shape[1]
    slab = Slab(far_ref.at[:, :attn], far_ref.at[:, attn:width], heads_ref, w_ref, arrived)
    get.start(far_table_ref, table_ref)
    for name, ref in zip(State.names, far_state, strict=True):
        get.start(ref, getattr(state, name))
    attn, hidden = state.o.shape[1], state.gl.shape[1]

    def enter(at, total, cotangent):
        grad = row_norm_back(total, normed_ref[at, :], inv_std_ref[at, :])
        below_ref[at, :] = grad + cotangent.astype(F32)

    over_totals(parts, other_ref, inputs, enter)
    kept_ref[...] = below_ref[: kept_ref.shape[0], :]
    slab.wait()
    get.wait()
    backward(state, below_ref, vec_ref.at[0], slab, table_ref, back, sums_ref, scratch, put, far_back)
    both = [sums_ref, later_ref]
    pad = jnp.zeros((8 - layers, attn), F32)
    qkv = jnp.concatenate([ref[SUM_QKV : SUM_QKV + 1, :] for ref in both] + [pad], axis=0)
    up = [ref[SUM_UP : SUM_UP + 1, :hidden] for ref in both] + [pad[:, :hidden]]
    up = jnp.concatenate(up, axis=0)
    spread = [
        dot(values.astype(BF), one_hot(place_ref, at, values.shape[1]))[:layers]
        for values, at in ((qkv, 0), (qkv, 1), (up, 2), (up, 3))
    ]
    small = [ref[: SUM_SHIFT_B + 1, :] for ref in both] + spread
    used = 9 * layers
    small = jnp.concatenate(small + [jnp.zeros((LANES - used, attn), F32)], axis=0)
    small_ref[...] = jnp.transpose(small).astype(BF)
    copy = pltpu.make_async_copy(small_ref, slab_ref.at[:, width:], arrived.at[2])
    copy.start()
    slab.give(slab_ref.at[:, :attn], slab_ref.at[:, attn:width], arrived)
    copy.wait()
    put.wait()


def slabs_kernel(layers, core_ref, *refs):
    far, sends, refs = refs[:9], refs[9 : 9 + layers], refs[9 + layers :]
    local, (rows_ref, bias_ref, arrived) = refs[:9], refs[9:]
    copies = [
        pltpu.make_async_copy(src, dst, arrived.at[i])
        for i, (src, dst) in enumerate(zip(far, local, strict=True))
    ]
    for copy in copies:
        copy.start()
    for copy in copies:
        copy.wait()
    (qkv_ref, out_ref, up_ref, down_ref), vectors, biases = local[:4], local[4:7], local[7:9]
    depth, width_out = qkv_ref.shape[1], out_ref.shape[2] // 2
    hidden = up_ref.shape[2] // 4
    low = core_ref[0] == 0

    def half(values):
        width = values.shape[1] // 2
        return jnp.where(low, values[:, :width], values[:, width:])

    rows_ref[...] = jnp.zeros_like(rows_ref)
    at = 0
    for layer in range(layers):
        for ref in vectors:
            rows_ref[at : at + 2, :depth] = ref[layer].astype(F32)
            at += 2
    lanes = lax.broadcasted_iota(jnp.int32, bias_ref.shape, 1)
    for ref in biases:
        bias_ref[...] = jnp.zeros_like(bias_ref)
        bias_ref[:layers, : ref.shape[1]] = ref[...].astype(F32)
        for values in (bias_ref[...], pltpu.roll(bias_ref[...], LANES - depth, 1)):
            rows_ref[at : at + layers, :] = jnp.where(lanes < depth, values, 0.0)[:layers]
            at += layers
    small = jnp.transpose(rows_ref[...])[:depth].astype(BF)
    heads, wide = [], ([], [])
    for layer in range(layers):
        qkv, out = half(qkv_ref[layer]), half(out_ref[layer])
        up, down = half(up_ref[layer]), half(down_ref[layer])
        attn = []
        for head in range(width_out // HS):
            at = head * 3 * HS
            attn += [qkv[:, at : at + 3 * HS], out[:, head * HS : (head + 1) * HS]]
        heads.append(jnp.concatenate(attn, axis=1))
        for z in (0, 1):
            at = slice(z * hidden, (z + 1) * hidden)
            wide[z].append(jnp.concatenate([up[:, at], down[:, at]], axis=1))
    for z in (0, 1):
        for layer, send_ref in enumerate(sends):
            block = [heads[layer], wide[z][layer]] + ([small] if layer == 0 else [])
            block = jnp.concatenate(block, axis=1)
            for owner in range(send_ref.shape[0]):
                if owner // NEAR % 2 == z:
                    send_ref[owner] = block


def sums_of(got_ref, columns):
    sums = []
    for z in (0, 1):
        senders = [owner for owner in range(got_ref.shape[0]) if owner // NEAR % 2 == z]
        total = got_ref[senders[0], :, columns].astype(F32)
        for owner in senders[1:]:
            total = total + got_ref[owner, :, columns].astype(F32)
        sums.append(total)
    return sums


def put_sums(attn, got_ref, all_ref):
    hidden = (all_ref.shape[1] - attn) // 4
    first, second = sums_of(got_ref, slice(0, attn))
    all_ref[:, :attn] = (first + second).astype(BF)
    for kind in (0, 1):
        at = attn + kind * hidden
        for z, total in enumerate(sums_of(got_ref, slice(at, at + hidden))):
            at_z = attn + (2 * kind + z) * hidden
            all_ref[:, at_z : at_z + hidden] = total.astype(BF)


def total_of(refs):
    mine, half, near, near_half = (ref[...].astype(F32) for ref in refs)
    return (mine + half) + (near + near_half)


def gather_late_kernel(attn, got_ref, all_ref):
    put_sums(attn, got_ref, all_ref)


def gather_kernel(attn, got_ref, all_ref, small_ref, pad_ref):
    depth, width = got_ref.shape[1], got_ref.shape[2] - LANES
    put_sums(attn, got_ref, all_ref.at[:, : all_ref.shape[1] - LANES])
    first, second = sums_of(got_ref, slice(width, width + LANES))
    pad_ref[...] = jnp.zeros_like(pad_ref)
    pad_ref[:depth, :] = first + second
    small = jnp.transpose(pad_ref[...])[: small_ref.shape[0]].astype(BF)
    small_ref[...] = small
    all_ref[:, all_ref.shape[1] - LANES :] = small


def finish_kernel(layers, core_ref, *rest):
    pairs, (half_ref, core_half_ref), rest = (rest[:2], rest[2:4]), rest[4:6], rest[6:]
    parts, (below_ref, far_normed_ref, far_inv_std_ref, *rest) = rest[:4], rest[4:]
    ahead, hidden_ref, rest = rest[:4], rest[4], rest[5:]
    result_ref, grad_ref, qkv_ref, out_ref, up_ref, down_ref, *vectors = rest[:11]
    normed_ref, inv_std_ref, get = rest[11:]
    get = Copies(get)
    own = pl.ds(0, normed_ref.shape[0])
    get.start(far_normed_ref.at[own, :], normed_ref)
    get.start(far_inv_std_ref.at[own, :], inv_std_ref)
    bias_qkv_ref, bias_up_ref, bias_out_ref, gain_ref, shift_ref = vectors
    width_qkv, width_out, width_up = (r.shape[2] // 2 for r in (qkv_ref, out_ref, up_ref))
    depth, heads = qkv_ref.shape[1], width_out // HS
    attn = heads * HEAD
    width = attn + 2 * width_up
    low = core_ref[0] == 0
    for layer, pair in enumerate(pairs):
        mine, theirs = (ref[:, :width].astype(F32) for ref in pair)
        sides = (jnp.where(low, mine, theirs), jnp.where(low, theirs, mine))
        for side, values in enumerate(sides):
            at = side * width_up
            up_ref[layer, :, at : at + width_up] = values[:, attn : attn + width_up]
            down_ref[layer, :, at : at + width_up] = values[:, attn + width_up :]
        starts = [(values, head * HEAD) for values in sides for head in range(heads)]
        qkv_ref[layer] = jnp.concatenate([v[:, at : at + 3 * HS] for v, at in starts], axis=1)
        out_ref[layer] = jnp.concatenate([v[:, at + 3 * HS : at + HEAD] for v, at in starts], axis=1)
    mine, core = (ref[:, width:].astype(F32) for ref in pairs[0])
    half, core_half = half_ref[...].astype(F32), core_half_ref[...].astype(F32)
    vectors = (mine + half) + (core + core_half)
    for layer in range(layers):
        rows = vectors[5 * layer : 5 * layer + 5, :depth]
        bias_out_ref[layer, 0:1, :] = rows[:1]
        bias_out_ref[layer, 1:2, :] = rows[:1]
        gain_ref[layer] = rows[1:3]
        shift_ref[layer] = rows[3:5]
    biases = mine + core
    at = 5 * layers
    for ref in (bias_qkv_ref, bias_up_ref):
        first, second = biases[at : at + layers], biases[at + layers : at + 2 * layers]
        lanes = lax.broadcasted_iota(jnp.int32, first.shape, 1)
        both = jnp.where(lanes < depth, first, pltpu.roll(second, depth, 1))
        ref[...] = both[:, : ref.shape[1]]
        at += 2 * layers
    result_ref[...] = (hidden_ref[...] + total_of(ahead)).astype(BF)
    get.wait()
    total = row_norm_back(total_of(parts), normed_ref[...], inv_std_ref[...])
    grad_ref[...] = (below_ref[...] + total).astype(BF)


def call(kernel, outs, scratch, flops, *args, far=(), far_outs=(), limit=VMEM_BYTES, **more):
    def space(at, arg, far):
        if at in far:
            return pltpu.HBM
        return pltpu.SMEM if arg.shape == (1,) else pltpu.VMEM

    return pl.pallas_call(
        kernel,
        out_shape=outs,
        in_specs=[pl.BlockSpec(memory_space=space(at, arg, far)) for at, arg in enumerate(args)],
        out_specs=[
            pl.BlockSpec(memory_space=space(at, out, far_outs)) for at, out in enumerate(outs)
        ],
        scratch_shapes=scratch,
        compiler_params=pltpu.CompilerParams(vmem_limit_bytes=limit),
        cost_estimate=pl.CostEstimate(flops=flops, bytes_accessed=8_000_000, transcendentals=0),
        **more,
    )(*args)


def core_rows_summed(kept, sent):
    return (kept.astype(F32) + other_core(sent).astype(F32)).astype(BF)


def parts_of_sum(mine):
    return mine, other_half(mine), near_group(mine), near_other_half(mine)


def other_rows(parts):
    mine, half, near, near_half = (p.astype(F32).reshape(2, -1, p.shape[1]) for p in parts)
    total = (mine + half) + (near[::-1] + near_half[::-1])
    return other_core(total.astype(BF).reshape(parts[0].shape))


def own_parts(mine):
    own = mine.shape[0] // 2
    return mine[:own], other_half(mine[:own]), near_group(mine[own:]), near_other_half(mine[own:])


def rotation(positions):
    exponents = jnp.arange(ROT // 2, dtype=F32) * (2.0 / ROT)
    inverse = jnp.power(10000.0, -exponents)
    phase = positions.astype(F32)[:, None] * inverse[None, :]
    cos, sin = jnp.cos(phase), jnp.sin(phase)
    none = jnp.zeros_like(sin)
    rest = jnp.zeros((positions.shape[0], HS - ROT), F32)
    tables = [[cos, cos, rest + 1.0], [-sin, none, rest], [none, sin, rest]]
    return jnp.stack([jnp.concatenate(t + t, axis=1) for t in tables])


def bias_places(owners, depth, starts, widths, shards):
    owner = jnp.arange(owners * depth, dtype=jnp.int32) // depth
    inner = jnp.arange(owners * depth, dtype=jnp.int32) % depth
    rows = []
    for start, width, shard, head in zip(starts, widths, shards, (3 * HS, None), strict=True):
        for first in (0, depth):
            at = owner * shard + inner + first - start
            fits = (inner + first < shard) & (at >= 0) & (at < width)
            if head is not None:
                at = at // head * HEAD + at % head
            rows.append(jnp.where(fits, at, -1))
    return jnp.stack(rows + rows)


def per_device(
    tokens,
    cotangent,
    doc_lens,
    block_pos,
    w_qkv,
    w_out,
    w_up,
    w_down,
    b_qkv,
    b_up,
    out_bias,
    norm_gain,
    norm_bias,
):
    row_count = tokens.shape[0]
    block_rows = row_count // 2
    core = lax.axis_index("ctx")
    owners = lax.axis_size("fsdp")
    layers, depth, width_qkv = w_qkv.shape
    width_qkv, width_out, hidden = width_qkv // 2, w_out.shape[1] // 2, w_up.shape[2] // 4
    place_z = lax.axis_index("fsdp") // NEAR % 2
    heads = width_out // HS
    attn = heads * HEAD
    width = attn + 2 * hidden
    wide = owners * depth
    rows = 4 * row_count

    core_at = core.astype(jnp.int32).reshape(1)
    sds = jax.ShapeDtypeStruct
    raw = (
        w_qkv,
        w_out.transpose(0, 2, 1),
        w_up,
        w_down.transpose(0, 2, 1),
        out_bias,
        norm_gain,
        norm_bias,
        b_qkv,
        b_up,
    )
    sends = call(
        functools.partial(slabs_kernel, layers),
        (
            sds((owners, depth, width + LANES), BF),
            sds((owners, depth, width), BF),
        ),
        [pltpu.VMEM(a.shape, a.dtype) for a in raw]
        + [pltpu.VMEM((LANES, LANES), F32), pltpu.VMEM((8, LANES), F32)]
        + [pltpu.SemaphoreType.DMA((len(raw),))],
        1000,
        core_at,
        *raw,
        far=range(1, 1 + len(raw)),
    )
    first, second = (exchanged(blocks).reshape(wide, -1) for blocks in sends)
    starts, ends = ((own, near_other_half(own)) for own in (tokens, cotangent))
    starts, ends = ((o, other_core(o), n, other_core(n)) for o, n in (starts, ends))
    offsets = jnp.arange(block_rows, dtype=jnp.int32)
    positions = (block_pos[0][:, None] * block_rows + offsets[None, :]).reshape(2, row_count)
    positions = jnp.where(core == 0, positions, positions[::-1]).reshape(-1)
    doc_ends = jnp.cumsum(doc_lens[0])
    docs = jnp.sum((positions[:, None] >= doc_ends[None, :]).astype(jnp.int32), axis=1)
    allowed = (docs[:, None] == docs[None, :]) & (positions[None, :] <= positions[:, None])
    mask = jnp.where(allowed, 0.0, MASKED).astype(F32)
    table = rotation(positions)
    place = bias_places(
        owners,
        depth,
        (core * width_qkv, (2 * core + place_z) * hidden),
        (width_qkv, hidden),
        (b_qkv.shape[1], b_up.shape[1]),
    )

    flops = 2 * rows * wide * width
    part = sds((rows // 2, wide), BF)
    kept = State.shapes(rows, wide, heads, hidden)

    def vmem(*arrays):
        return [pltpu.VMEM(array.shape, array.dtype) for array in arrays]

    def copies(*counts):
        return [pltpu.SemaphoreType.DMA((count,)) for count in counts]

    slab_scratch = [
        pltpu.VMEM((wide, attn), BF),
        pltpu.VMEM((wide, 2 * hidden), BF),
        pltpu.SemaphoreType.DMA((3,)),
    ]
    kept_part, sent_part, vec, *state = call(
        functools.partial(first_kernel, layers),
        (part, part, sds((layers, VECTORS, wide), F32), *State.shapes(rows, wide, heads, hidden)),
        [
            *vmem(part, part, table, mask),
            *copies(2, 12),
            pltpu.VMEM((rows, wide), F32),
            pltpu.VMEM((wide, LANES), BF),
            *slab_scratch,
            *vmem(*kept),
        ],
        flops,
        *starts,
        first,
        place,
        table,
        mask,
        far=(4, 6, 7),
        far_outs=(0, 1, *range(3, 13)),
    )
    parts = parts_of_sum(core_rows_summed(kept_part, sent_part))
    scratch = [
        pltpu.VMEM((rows, wide), BF),
        pltpu.VMEM((rows, hidden), BF),
        pltpu.VMEM((rows // 2, attn), BF),
        pltpu.VMEM((rows, wide), F32),
        pltpu.VMEM((rows, wide), F32),
    ]
    *sums, slab, later_sums, result, normed, inv_std = call(
        last_kernel,
        (
            *(part,) * 4,
            sds((wide, width), BF),
            sds((8, wide), F32),
            sds((row_count, wide), F32),
            *kept[:2],
        ),
        [
            *vmem(table, mask, sds((row_count, wide), F32)),
            *copies(6, 7),
            *vmem(part, part, part, part, *kept, sds((rows, wide), BF)),
            *slab_scratch,
            *scratch,
        ],
        3 * flops,
        *starts,
        *ends,
        *parts,
        other_rows(parts),
        vec,
        second,
        table,
        mask,
        far=(4, 5, 6, 7, 14, 15, 16),
        far_outs=(0, 1, 2, 3, 4, 6, 7, 8),
    )
    parts = parts_of_sum(core_rows_summed(*sums[2:]))
    slab, *sums = lax.optimization_barrier((slab, *sums[:2], *parts))
    ahead, parts = own_parts(core_rows_summed(*sums[:2])), sums[2:]
    later = exchanged(slab.reshape(owners, depth, -1))
    kept_part, sent_part, slab, grad_below = call(
        functools.partial(back_kernel, layers),
        (part, part, sds((wide, width + LANES), BF), sds((row_count, wide), F32)),
        [
            *vmem(table),
            *copies(11, 2),
            *vmem(part, part, *kept, later_sums, sds((rows, wide), F32)),
            *vmem(sds((wide, LANES), BF)),
            *slab_scratch,
            *scratch,
        ],
        2 * flops,
        *ends,
        *parts,
        other_rows(parts),
        normed,
        inv_std,
        later_sums,
        vec,
        first,
        place,
        table,
        *state,
        far=(13, *range(15, 26)),
        far_outs=(0, 1, 2),
    )
    slab, later = lax.optimization_barrier((slab, later))
    earlier = exchanged(slab.reshape(owners, depth, -1))
    below = core_rows_summed(kept_part, sent_part)

    (late,) = call(
        functools.partial(gather_late_kernel, attn),
        (sds((depth, attn + 4 * hidden), BF),),
        [],
        flops // 8,
        later,
    )
    below, late = lax.optimization_barrier((below, late))
    below = own_parts(below)
    mine, small = call(
        functools.partial(gather_kernel, attn),
        (sds((depth, attn + 4 * hidden + LANES), BF), sds((depth, LANES), BF)),
        [pltpu.VMEM((LANES, LANES), F32)],
        1000,
        earlier,
    )
    result, grad_tokens, grad_qkv, grad_out, grad_up, grad_down, *vectors = call(
        functools.partial(finish_kernel, layers),
        (sds(tokens.shape, BF),) * 2
        + tuple(
            sds(shape, F32)
            for shape in (
                w_qkv.shape,
                (layers, depth, w_out.shape[1]),
                w_up.shape,
                (layers, depth, w_down.shape[1]),
                b_qkv.shape,
                b_up.shape,
                out_bias.shape,
                norm_gain.shape,
                norm_bias.shape,
            )
        ),
        [*vmem(sds((row_count, wide), F32), sds((row_count, 1), F32)), *copies(2)],
        1000,
        core_at,
        mine,
        other_core(mine),
        late,
        other_core(late),
        other_half(small),
        other_core_and_half(small),
        *below,
        grad_below,
        state[0],
        state[1],
        *ahead,
        result,
        far=(12, 13),
    )
    return (
        result,
        grad_tokens,
        grad_qkv,
        grad_out.transpose(0, 2, 1),
        grad_up,
        grad_down.transpose(0, 2, 1),
        *vectors,
    )


def solution(mesh):
    in_specs = (
        P(("fsdp", "ctx"), None),
        P(("fsdp", "ctx"), None),
        P("fsdp", None),
        P("fsdp", None),
        P(None, "fsdp", "tp"),
        P(None, "tp", "fsdp"),
        P(None, "fsdp", "tp"),
        P(None, "tp", "fsdp"),
        P(None, ("tp", "fsdp")),
        P(None, ("tp", "fsdp")),
        P(None, None, "fsdp"),
        P(None, None, "fsdp"),
        P(None, None, "fsdp"),
    )
    out_specs = (P(("fsdp", "ctx"), None), P(("fsdp", "ctx"), None), *in_specs[4:])
    return jax.shard_map(
        per_device, mesh=mesh, in_specs=in_specs, out_specs=out_specs, check_vma=False
    )
```

```python
import functools

import jax
import jax.numpy as jnp
from jax import lax
from jax.experimental import pallas as pl
from jax.experimental.pallas import tpu as pltpu
from jax.sharding import PartitionSpec as P

HS = 64
ROT = 16
EPSILON = 1e-05
MASKED = -1e30
F32 = jnp.float32
BF = jnp.bfloat16
SWAP = [(0, 1), (1, 0)]
NEAR = 4
LANES = 128
CHUNK = 128
HEAD = 4 * HS
SCALE = HS ** (-0.5)
VMEM_BYTES = 62 * 1024 * 1024
GAIN_A, GAIN_B, SHIFT_A, SHIFT_B, BIAS_QKV, BIAS_UP, BIAS_OUT = range(7)
VECTORS = 8
SUM_OUT, SUM_GAIN_A, SUM_GAIN_B, SUM_SHIFT_A, SUM_SHIFT_B, SUM_QKV, SUM_UP = range(7)


def other_core(values):
    return lax.ppermute(values, "ctx", SWAP)


def other_half(values):
    return lax.ppermute(values, "tp", SWAP)


def other_core_and_half(values):
    return lax.ppermute(values, ("ctx", "tp"), [(0, 3), (1, 2), (2, 1), (3, 0)])


def near_group(values):
    owners = lax.axis_size("fsdp")
    return lax.ppermute(values, "fsdp", [(f, f ^ NEAR) for f in range(owners)])


def near_other_half(values):
    owners = lax.axis_size("fsdp")
    pairs = [(2 * f + t, 2 * (f ^ NEAR) + 1 - t) for f in range(owners) for t in (0, 1)]
    return lax.ppermute(values, ("fsdp", "tp"), pairs)


def near_other_core(values):
    owners = lax.axis_size("fsdp")
    pairs = [(2 * f + c, 2 * (f ^ NEAR) + 1 - c) for f in range(owners) for c in (0, 1)]
    return lax.ppermute(values, ("fsdp", "ctx"), pairs)


def exchanged(blocks):
    return lax.all_to_all(blocks, "fsdp", 0, 0, tiled=True)


def exchanged_in_plane(blocks):
    owners = lax.axis_size("fsdp")
    planes = [[f for f in range(owners) if f // NEAR % 2 == z] for z in (0, 1)]
    return lax.all_to_all(blocks, "fsdp", 0, 0, axis_index_groups=planes, tiled=True)


def pairs_together(slab, owners):
    blocks = slab.reshape(owners // (2 * NEAR), 2, NEAR, -1, slab.shape[1])
    return blocks.transpose(0, 2, 1, 3, 4).reshape(owners // 2, -1, slab.shape[1])


def owners_in_order(blocks, owners):
    width = blocks.shape[2]
    blocks = blocks.reshape(owners // (2 * NEAR), NEAR, 2, -1, width)
    return blocks.transpose(0, 2, 1, 3, 4).reshape(-1, width)


def dot(left, right, along=(1, 0)):
    dims = (((along[0],), (along[1],)), ((), ()))
    return lax.dot_general(left, right, dims, preferred_element_type=F32)


def over_rows(rows, step, carry=None, start=0):
    def body(at, kept):
        return step(pl.ds(pl.multiple_of(at * CHUNK, CHUNK), CHUNK), kept)

    return lax.fori_loop(start // CHUNK, rows // CHUNK, body, carry)


def by_eights(values):
    return values.reshape(-1, 8, values.shape[-1]).sum(axis=0)


def whole_sum(eights):
    return jnp.sum(eights, axis=0, keepdims=True)


def turned(tile, cos, left, right):
    return (
        tile * cos
        + pltpu.roll(tile, LANES - ROT // 2, 1) * left
        + pltpu.roll(tile, ROT // 2, 1) * right
    )


def row_norm(values):
    centered = values - jnp.mean(values, axis=-1, keepdims=True)
    inv_std = lax.rsqrt(jnp.mean(centered * centered, axis=-1, keepdims=True) + EPSILON)
    return centered * inv_std, inv_std


def row_norm_back(total, normed, inv_std):
    return inv_std * (
        total
        - jnp.mean(total, axis=-1, keepdims=True)
        - normed * jnp.mean(total * normed, axis=-1, keepdims=True)
    )


def one_hot(place_ref, at, width):
    rows = lax.broadcasted_iota(jnp.int32, (width, place_ref.shape[1]), 0)
    return (rows == place_ref[at : at + 1, :]).astype(F32).astype(BF)


class Slab:
    def __init__(self, far_heads_ref, far_ref, heads_ref, w_ref, arrived):
        self.heads_ref, self.w_ref = heads_ref, w_ref
        self.copies = [
            pltpu.make_async_copy(far_heads_ref, heads_ref, arrived.at[0]),
            pltpu.make_async_copy(far_ref, w_ref, arrived.at[1]),
        ]
        for copy in self.copies:
            copy.start()

    def wait(self):
        for copy in self.copies:
            copy.wait()
        return self.heads_ref, self.w_ref

    def give(self, far_heads_ref, far_ref, sent):
        copies = [
            pltpu.make_async_copy(self.heads_ref, far_heads_ref, sent.at[0]),
            pltpu.make_async_copy(self.w_ref, far_ref, sent.at[1]),
        ]
        for copy in copies:
            copy.start()
        for copy in copies:
            copy.wait()


class Copies:
    def __init__(self, semaphores):
        self.semaphores, self.started = semaphores, []

    def start(self, src, dst):
        copy = pltpu.make_async_copy(src, dst, self.semaphores.at[len(self.started)])
        copy.start()
        self.started.append(copy)

    def wait(self, begin=0, end=None):
        for copy in self.started[begin:end]:
            copy.wait()


class State:
    names = ("normed", "inv_std", "a", "m", "qk", "v", "p", "o", "gl", "slope")

    def __init__(self, refs, copies=None, far=()):
        for name, ref in zip(self.names, refs, strict=True):
            setattr(self, name, ref)
        self.copies, self.far = copies, dict(zip(self.names, far))

    def ready(self, *names):
        for name in names:
            if name in self.far:
                self.copies.start(getattr(self, name), self.far[name])

    @staticmethod
    def shapes(rows, depth, heads, hidden):
        group = rows // 2
        return (
            jax.ShapeDtypeStruct((rows, depth), F32),
            jax.ShapeDtypeStruct((rows, 1), F32),
            jax.ShapeDtypeStruct((group, depth), BF),
            jax.ShapeDtypeStruct((rows, depth), BF),
            jax.ShapeDtypeStruct((group, heads * 2 * HS), BF),
            jax.ShapeDtypeStruct((group, heads * HS), BF),
            jax.ShapeDtypeStruct((heads, group, group), F32),
            jax.ShapeDtypeStruct((group, heads * HEAD), BF),
            jax.ShapeDtypeStruct((rows, hidden), BF),
            jax.ShapeDtypeStruct((rows, hidden), F32),
        )


def places(rows):
    quarter = rows // 4
    return [(0, 0, 0), (quarter, 1, 0), (2 * quarter, 0, quarter), (3 * quarter, 1, quarter)]


def forward(state, vec_ref, slab, near_copies, table_ref, mask_ref, parts, wide_ref):
    rows, depth = state.normed.shape
    group = rows // 2
    heads = state.v.shape[1] // HS
    hidden = state.gl.shape[1]

    def affine_a(at, _):
        state.a[at, :] = (
            state.normed[at, :] * vec_ref[GAIN_A : GAIN_A + 1, :]
            + vec_ref[SHIFT_A : SHIFT_A + 1, :]
        ).astype(BF)

    def affine_b(at, _):
        state.m[at, :] = (
            state.normed[at, :] * vec_ref[GAIN_B : GAIN_B + 1, :]
            + vec_ref[SHIFT_B : SHIFT_B + 1, :]
        ).astype(BF)

    state.ready("normed", "inv_std")
    over_rows(group, affine_a)
    over_rows(rows, affine_b)
    state.ready("a", "m")
    heads_ref, w_ref = slab.wait()
    near_copies.wait()
    wide_ref[:group, :] = dot(state.a[...], heads_ref[...])
    state.o[...] = jnp.zeros_like(state.o)
    for head in range(heads):
        at = head * HEAD
        bias = vec_ref[BIAS_QKV : BIAS_QKV + 1, at : at + HEAD]
        tile = wide_ref[:group, at : at + LANES] + bias[:, :LANES]
        tile = turned(tile, table_ref[0], table_ref[1], table_ref[2]).astype(BF)
        value = wide_ref[:group, at + 2 * HS : at + 3 * HS] + bias[:, 2 * HS : 3 * HS]
        value = value.astype(BF)
        state.qk[:, head * LANES : (head + 1) * LANES] = tile
        state.v[:, head * HS : (head + 1) * HS] = value
        half = group // 2
        for top in (0, half):
            scores = dot(tile[top : top + half, :HS], tile[:, HS:], (1, 1))
            scores = scores * SCALE + mask_ref[top : top + half, :]
            exponent = jnp.exp(scores - jnp.max(scores, axis=1, keepdims=True))
            share = exponent * (1.0 / jnp.sum(exponent, axis=1, keepdims=True))
            state.p[head, top : top + half, :] = share
            state.o[top : top + half, at + 3 * HS : at + HEAD] = dot(
                share.astype(BF), value
            ).astype(BF)
    state.ready("qk", "v", "p", "o")
    wide_ref[:, :hidden] = dot(state.m[...], w_ref[:, :hidden])

    def gelu(at, _):
        up = wide_ref[at, :hidden] + vec_ref[BIAS_UP : BIAS_UP + 1, :hidden]
        below = 0.5 + 0.5 * lax.erf(up * (0.5**0.5))
        state.gl[at, :] = (up * below).astype(BF)
        state.slope[at, :] = below + up * (jnp.exp(-0.5 * up * up) * 0.3989422804014327)

    over_rows(rows, gelu)
    state.ready("gl", "slope")
    down = w_ref[:, hidden : 2 * hidden]
    part = dot(state.o[...], heads_ref[...], (1, 1))
    half = group // 2
    part = (part + dot(state.gl[:group, :], down, (1, 1))).astype(BF)
    near = dot(state.gl[group:, :], down, (1, 1)).astype(BF)
    for core, part_ref in enumerate(parts):
        at = core * half
        part_ref[:half, :] = part[at : at + half]
        part_ref[half:, :] = near[at : at + half]


def backward(
    state, grad_ref, vec_ref, slab, table_ref, parts, sums_ref, scratch, put, far_parts
):
    low_ref, up_ref, qkv_ref, wide_ref, deep_ref = scratch
    heads_ref, w_ref = slab.heads_ref, slab.w_ref
    rows, depth = state.normed.shape
    group = rows // 2
    heads = state.v.shape[1] // HS
    attn, hidden = heads * HEAD, state.gl.shape[1]

    def lower(at, total):
        grad = grad_ref[at, :].astype(F32)
        low_ref[at, :] = grad.astype(BF)
        return total + by_eights(grad)

    total = over_rows(rows, lower, jnp.zeros((8, depth), F32))
    sums_ref[SUM_OUT : SUM_OUT + 1, :] = whole_sum(total) * 0.125
    low = low_ref[...]
    wide_ref[:, :hidden] = dot(low, w_ref[:, hidden : 2 * hidden])

    def through_gelu(at, total):
        up = (wide_ref[at, :hidden] * state.slope[at, :]).astype(BF)
        up_ref[at, :] = up
        return total + by_eights(up.astype(F32))

    total = over_rows(rows, through_gelu, jnp.zeros((8, hidden), F32))
    sums_ref[SUM_UP : SUM_UP + 1, :hidden] = whole_sum(total)
    wide_ref[:group, :] = dot(low_ref[:group, :], heads_ref[...])
    for head in range(heads):
        at = head * HEAD
        tile = state.qk[:, head * LANES : (head + 1) * LANES]
        query, key = tile[:, :HS], tile[:, HS:]
        value = state.v[:, head * HS : (head + 1) * HS]
        out = wide_ref[:group, at + 3 * HS : at + HEAD].astype(BF)
        half = group // 2
        grad_value, grad_key, grad_query = 0.0, 0.0, []
        for top in (0, half):
            share = state.p[head, top : top + half, :]
            grad = dot(out[top : top + half], value, (1, 1))
            delta = jnp.sum(share * grad, axis=1, keepdims=True)
            low_scores = (share * (grad - delta)).astype(BF)
            grad_value = grad_value + dot(share.astype(BF), out[top : top + half], (0, 0))
            grad_query.append(dot(low_scores, key))
            grad_key = grad_key + dot(low_scores, query[top : top + half], (0, 0))
        both = jnp.concatenate([jnp.concatenate(grad_query, axis=0), grad_key], axis=1) * SCALE
        both = turned(both, table_ref[0], -table_ref[1], -table_ref[2])
        qkv_ref[:, at : at + LANES] = both.astype(BF)
        qkv_ref[:, at + LANES : at + HEAD] = jnp.concatenate(
            [grad_value, jnp.zeros_like(grad_value)], axis=1
        ).astype(BF)

    def count_qkv(at, total):
        return total + by_eights(qkv_ref[at, :].astype(F32))

    total = over_rows(group, count_qkv, jnp.zeros((8, attn), F32))
    sums_ref[SUM_QKV : SUM_QKV + 1, :] = whole_sum(total)
    wide_ref[:group, :] = dot(qkv_ref[...], heads_ref[...], (1, 1))
    deep_ref[...] = dot(up_ref[...], w_ref[:, :hidden], (1, 1))

    def through_norms(with_first, part_ref, begin, to):
        def step(at, totals):
            there, at = moved(at, to), moved(at, begin)
            second, normed = deep_ref[at, :], state.normed[at, :]
            total, new = second * vec_ref[GAIN_B : GAIN_B + 1, :], (second * normed, second)
            if with_first:
                first = wide_ref[at, :]
                total = total + first * vec_ref[GAIN_A : GAIN_A + 1, :]
                new = (*new, first * normed, first)
            part_ref[there, :] = total.astype(BF)
            return tuple(old + by_eights(term) for old, term in zip(totals, new, strict=True))

        return step

    totals = (jnp.zeros((8, depth), F32),) * 4
    for begin, core, to in places(rows):
        count = 4 if begin < group else 2
        step = through_norms(begin < group, parts[core], begin, to)
        totals = (*over_rows(rows // 4, step, totals[:count]), *totals[count:])
    for row, total in zip((SUM_GAIN_B, SUM_SHIFT_B, SUM_GAIN_A, SUM_SHIFT_A), totals, strict=True):
        sums_ref[row : row + 1, :] = whole_sum(total)
    for ref, far_part_ref in zip(parts, far_parts, strict=True):
        put.start(ref, far_part_ref)
    heads_grad = dot(state.a[...], qkv_ref[...], (0, 0))
    heads_grad = heads_grad + dot(low_ref[:group, :], state.o[...], (0, 0))
    heads_ref[...] = heads_grad.astype(BF)
    w_ref[:, :hidden] = dot(state.m[...], up_ref[...], (0, 0)).astype(BF)
    w_ref[:, hidden : 2 * hidden] = dot(low, state.gl[...], (0, 0)).astype(BF)


def first_kernel(layers, *refs):
    inputs, (far_ref, place_ref, far_table_ref, far_mask_ref, *rest) = refs[:4], refs[4:]
    far_parts, vec_ref, far_state, rest = rest[:2], rest[2], rest[3:13], rest[13:]
    parts, (table_ref, mask_ref, get, put), rest = rest[:2], rest[2:6], rest[6:]
    wide_ref, small_ref, heads_ref, w_ref, arrived, *state = rest
    get, put = Copies(get), Copies(put)
    state = State(state, put, far_state)
    attn = state.o.shape[1]
    hidden = state.gl.shape[1]
    width = attn + 2 * hidden
    copy = pltpu.make_async_copy(far_ref.at[:, width:], small_ref, arrived.at[2])
    copy.start()
    slab = Slab(far_ref.at[:, :attn], far_ref.at[:, attn:width], heads_ref, w_ref, arrived)
    get.start(far_table_ref, table_ref)
    get.start(far_mask_ref, mask_ref)
    copy.wait()
    small = jnp.transpose(small_ref[...].astype(F32))
    at = 6 * layers
    biases = small[at : at + 4 * layers].astype(BF)
    bias_qkv = dot(biases[:layers], one_hot(place_ref, 0, attn), (1, 1)) + dot(
        biases[layers : 2 * layers], one_hot(place_ref, 1, attn), (1, 1)
    )
    bias_up = dot(biases[2 * layers : 3 * layers], one_hot(place_ref, 2, hidden), (1, 1)) + dot(
        biases[3 * layers :], one_hot(place_ref, 3, hidden), (1, 1)
    )
    for layer in range(layers):
        rows = small[6 * layer : 6 * layer + 6]
        vec_ref[layer, GAIN_A : SHIFT_B + 1, :] = rows[2:]
        vec_ref[layer, BIAS_QKV : BIAS_QKV + 1, :] = bias_qkv[layer : layer + 1]
        vec_ref[layer, BIAS_UP : BIAS_UP + 1, :hidden] = bias_up[layer : layer + 1]
        vec_ref[layer, BIAS_OUT : BIAS_OUT + 1, :] = rows[0:1] + rows[1:2]
        vec_ref[layer, BIAS_OUT + 1 : VECTORS, :] = rows[0:1]

    for quarter, ref in enumerate(inputs):

        def enter(at, _, ref=ref, begin=quarter * ref.shape[0]):
            normed, inv_std = row_norm(ref[at, :].astype(F32))
            state.normed[moved(at, begin), :] = normed
            state.inv_std[moved(at, begin), :] = inv_std

        over_rows(ref.shape[0], enter)
    forward(state, vec_ref.at[0], slab, get, table_ref, mask_ref, parts, wide_ref)
    for ref, far_part_ref in zip(parts, far_parts, strict=True):
        put.start(ref, far_part_ref)
    put.wait()


def summed_rows(parts, at, there):
    mine, near = parts
    return mine[at, :].astype(F32) + near[there, :].astype(F32)


def moved(at, by):
    return pl.ds(pl.multiple_of(at.start + by, CHUNK), CHUNK)


def over_totals(parts, other_ref, inputs, take):
    own = parts[0].shape[0] // 2

    def own_core(at, _):
        take(at, summed_rows(parts, at, moved(at, own)), inputs[0][at, :])

    def near_own_core(at, _):
        total = summed_rows(parts, moved(at, own), at)
        take(moved(at, 2 * own), total, inputs[2][at, :])

    def other(at, _):
        take(moved(at, own), other_ref[at, :].astype(F32), inputs[1][at, :])

    def near_other(at, _):
        total = other_ref[moved(at, own), :].astype(F32)
        take(moved(at, 3 * own), total, inputs[3][at, :])

    for step in (own_core, near_own_core, other, near_other):
        over_rows(own, step)


def last_kernel(*refs):
    inputs, far_ends, parts, refs = refs[:4], refs[4:8], refs[8:10], refs[10:]
    other_ref, vec_ref, far_ref, far_table_ref, far_mask_ref, *rest = refs
    far_parts, rest = rest[:4], rest[4:]
    slab_ref, sums_ref, far_hidden_ref, far_normed_ref, far_inv_std_ref, *rest = rest
    (table_ref, mask_ref, hidden_ref, get, put), rest = rest[:5], rest[5:]
    ahead, back, rest = rest[:2], rest[2:4], rest[4:]
    get, put = Copies(get), Copies(put)
    state, rest = State(rest[:10], put, (far_normed_ref, far_inv_std_ref)), rest[10:]
    grad_ref, heads_ref, w_ref, arrived, *scratch = rest
    attn, width = heads_ref.shape[1], heads_ref.shape[1] + w_ref.shape[1]
    slab = Slab(far_ref.at[:, :attn], far_ref.at[:, attn:width], heads_ref, w_ref, arrived)
    get.start(far_table_ref, table_ref)
    get.start(far_mask_ref, mask_ref)
    own = hidden_ref.shape[0]
    for quarter, ref in enumerate(far_ends):
        get.start(ref, grad_ref.at[quarter * own : (quarter + 1) * own, :])
    bias = vec_ref[0, BIAS_OUT : BIAS_OUT + 1, :]

    def enter(at, total, tokens):
        values = tokens.astype(F32) + total + bias
        scratch[3][at, :] = values
        normed, inv_std = row_norm(values)
        state.normed[at, :] = normed
        state.inv_std[at, :] = inv_std

    over_totals(parts, other_ref, inputs, enter)
    hidden_ref[...] = scratch[3][:own, :] + vec_ref[1, BIAS_OUT : BIAS_OUT + 1, :]
    put.start(hidden_ref, far_hidden_ref)
    forward(state, vec_ref.at[1], slab, get, table_ref, mask_ref, ahead, scratch[3])
    for ref, far_part_ref in zip(ahead, far_parts[:2], strict=True):
        put.start(ref, far_part_ref)
    backward(state, grad_ref, vec_ref.at[1], slab, table_ref, back, sums_ref, scratch, put, far_parts[2:])
    slab.give(slab_ref.at[:, :attn], slab_ref.at[:, attn:width], arrived)
    put.wait()


def back_kernel(layers, *refs):
    inputs, parts, refs = refs[:4], refs[4:6], refs[6:]
    other_ref, normed_ref, inv_std_ref, later_ref, vec_ref, far_ref, place_ref, far_table_ref, *rest = refs
    far_state, rest = rest[:10], rest[10:]
    far_back, (slab_ref, kept_ref, table_ref, get, put, *rest) = rest[:2], rest[2:]
    back, state, rest = rest[:2], State(rest[2:12]), rest[12:]
    sums_ref, below_ref, small_ref, heads_ref, w_ref, arrived, *scratch = rest
    get, put = Copies(get), Copies(put)
    attn, width = heads_ref.shape[1], heads_ref.shape[1] + w_ref.shape[1]
    slab = Slab(far_ref.at[:, :attn], far_ref.at[:, attn:width], heads_ref, w_ref, arrived)
    get.start(far_table_ref, table_ref)
    for name, ref in zip(State.names, far_state, strict=True):
        get.start(ref, getattr(state, name))
    attn, hidden = state.o.shape[1], state.gl.shape[1]

    def enter(at, total, cotangent):
        grad = row_norm_back(total, normed_ref[at, :], inv_std_ref[at, :])
        below_ref[at, :] = grad + cotangent.astype(F32)

    over_totals(parts, other_ref, inputs, enter)
    kept_ref[...] = below_ref[: kept_ref.shape[0], :]
    slab.wait()
    get.wait()
    backward(state, below_ref, vec_ref.at[0], slab, table_ref, back, sums_ref, scratch, put, far_back)
    both = [sums_ref, later_ref]
    pad = jnp.zeros((8 - layers, attn), F32)
    qkv = jnp.concatenate([ref[SUM_QKV : SUM_QKV + 1, :] for ref in both] + [pad], axis=0)
    up = [ref[SUM_UP : SUM_UP + 1, :hidden] for ref in both] + [pad[:, :hidden]]
    up = jnp.concatenate(up, axis=0)
    spread = [
        dot(values.astype(BF), one_hot(place_ref, at, values.shape[1]))[:layers]
        for values, at in ((qkv, 0), (qkv, 1), (up, 2), (up, 3))
    ]
    small = [ref[: SUM_SHIFT_B + 1, :] for ref in both] + spread
    used = 9 * layers
    small = jnp.concatenate(small + [jnp.zeros((LANES - used, attn), F32)], axis=0)
    small_ref[...] = jnp.transpose(small).astype(BF)
    copy = pltpu.make_async_copy(small_ref, slab_ref.at[:, width:], arrived.at[2])
    copy.start()
    slab.give(slab_ref.at[:, :attn], slab_ref.at[:, attn:width], arrived)
    copy.wait()
    put.wait()


def slabs_kernel(layers, core_ref, place_ref, *refs):
    far, (send_ref, own_ref, near_ref), refs = refs[:9], refs[9:12], refs[12:]
    local, (rows_ref, bias_ref, arrived) = refs[:9], refs[9:]
    copies = [
        pltpu.make_async_copy(src, dst, arrived.at[i])
        for i, (src, dst) in enumerate(zip(far, local, strict=True))
    ]
    for copy in copies:
        copy.start()
    for copy in copies:
        copy.wait()
    (qkv_ref, out_ref, up_ref, down_ref), vectors, biases = local[:4], local[4:7], local[7:9]
    depth, width_out = qkv_ref.shape[1], out_ref.shape[2] // 2
    hidden = up_ref.shape[2] // 4
    low = core_ref[0] == 0

    def half(values):
        width = values.shape[1] // 2
        return jnp.where(low, values[:, :width], values[:, width:])

    rows_ref[...] = jnp.zeros_like(rows_ref)
    at = 0
    for layer in range(layers):
        for ref in vectors:
            rows_ref[at : at + 2, :depth] = ref[layer].astype(F32)
            at += 2
    lanes = lax.broadcasted_iota(jnp.int32, bias_ref.shape, 1)
    for ref in biases:
        bias_ref[...] = jnp.zeros_like(bias_ref)
        bias_ref[:layers, : ref.shape[1]] = ref[...].astype(F32)
        for values in (bias_ref[...], pltpu.roll(bias_ref[...], LANES - depth, 1)):
            rows_ref[at : at + layers, :] = jnp.where(lanes < depth, values, 0.0)[:layers]
            at += layers
    small = jnp.transpose(rows_ref[...])[:depth].astype(BF)
    heads, wide = [], ([], [])
    for layer in range(layers):
        qkv, out = half(qkv_ref[layer]), half(out_ref[layer])
        up, down = half(up_ref[layer]), half(down_ref[layer])
        attn = []
        for head in range(width_out // HS):
            at = head * 3 * HS
            attn += [qkv[:, at : at + 3 * HS], out[:, head * HS : (head + 1) * HS]]
        heads.append(jnp.concatenate(attn, axis=1))
        for z in (0, 1):
            at = slice(z * hidden, (z + 1) * hidden)
            wide[z].append(jnp.concatenate([up[:, at], down[:, at]], axis=1))
    for z in (0, 1):
        block = jnp.concatenate([heads[0], wide[z][0], small], axis=1)
        for owner in range(send_ref.shape[0]):
            if owner // NEAR % 2 == z:
                send_ref[owner] = block
    first = place_ref[0] == 0
    own_ref[...] = jnp.concatenate([heads[1], jnp.where(first, *wide_of(wide, 0, 1))], axis=1)
    near_ref[...] = jnp.concatenate([heads[1], jnp.where(first, *wide_of(wide, 1, 0))], axis=1)


def wide_of(wide, *at):
    return [wide[z][1] for z in at]


def sum_of(got_ref, columns):
    total = got_ref[0, :, columns].astype(F32)
    for sender in range(1, got_ref.shape[0]):
        total = total + got_ref[sender, :, columns].astype(F32)
    return total


def put_sums(place_ref, got_ref, own_ref, near_ref):
    depth = own_ref.shape[0]
    step = 3 * LANES
    for begin in range(0, own_ref.shape[1], step):
        at = slice(begin, begin + step)
        total = sum_of(got_ref, at)
        low, high = total[:depth], total[depth:]
        own_ref[:, at] = jnp.where(place_ref[0] == 0, low, high).astype(BF)
        near_ref[:, at] = jnp.where(place_ref[0] == 0, high, low).astype(BF)


def total_of(refs):
    mine, near = refs
    return mine[...].astype(F32) + near[...].astype(F32)


def gather_late_kernel(place_ref, got_ref, own_ref, near_ref):
    put_sums(place_ref, got_ref, own_ref, near_ref)


def gather_kernel(place_ref, got_ref, own_ref, near_ref, pad_ref):
    depth, width = own_ref.shape[0], own_ref.shape[1] - LANES
    put_sums(place_ref, got_ref, own_ref.at[:, :width], near_ref.at[:, :width])
    pad_ref[...] = jnp.zeros_like(pad_ref)
    pad_ref[: 2 * depth, :] = sum_of(got_ref, slice(width, width + LANES))
    low = jnp.transpose(pad_ref[...])[:depth]
    high = pltpu.roll(low, LANES - depth, 1)
    own_ref[:, width:] = jnp.where(place_ref[0] == 0, low, high).astype(BF)
    near_ref[:, width:] = jnp.where(place_ref[0] == 0, high, low).astype(BF)


def finish_kernel(layers, core_ref, place_ref, *rest):
    groups, rest = (rest[:4], rest[4:8]), rest[8:]
    parts, (below_ref, far_normed_ref, far_inv_std_ref, *rest) = rest[:2], rest[2:]
    hidden_ref, *rest = rest
    result_ref, grad_ref, qkv_ref, out_ref, up_ref, down_ref, *biases = rest[:8]
    normed_ref, inv_std_ref, get = rest[8:]
    get = Copies(get)
    own = pl.ds(0, normed_ref.shape[0])
    get.start(far_normed_ref.at[own, :], normed_ref)
    get.start(far_inv_std_ref.at[own, :], inv_std_ref)
    width_qkv, width_out, width_up = (r.shape[2] // 2 for r in (qkv_ref, out_ref, up_ref))
    depth, heads = qkv_ref.shape[1], width_out // HS
    attn = heads * HEAD
    low, first = core_ref[0] == 0, place_ref[0] == 0

    def both_places(own, near):
        return jnp.where(first, own, near), jnp.where(first, near, own)

    hidden = width_up // 2
    for layer, group in enumerate(groups):
        mine, core, near, core_near = (ref[:, : attn + width_up].astype(F32) for ref in group)
        attention = (mine[:, :attn] + near[:, :attn], core[:, :attn] + core_near[:, :attn])
        sides = (jnp.where(low, *attention), jnp.where(low, *attention[::-1]))
        starts = [(values, head * HEAD) for values in sides for head in range(heads)]
        qkv_ref[layer] = jnp.concatenate([v[:, at : at + 3 * HS] for v, at in starts], axis=1)
        out_ref[layer] = jnp.concatenate([v[:, at + 3 * HS : at + HEAD] for v, at in starts], axis=1)
        for z, (ours, theirs) in enumerate(
            zip(both_places(mine, near), both_places(core, core_near), strict=True)
        ):
            for side, values in enumerate((jnp.where(low, ours, theirs), jnp.where(low, theirs, ours))):
                at = side * width_up + z * hidden
                up_ref[layer, :, at : at + hidden] = values[:, attn : attn + hidden]
                down_ref[layer, :, at : at + hidden] = values[:, attn + hidden : attn + 2 * hidden]
    rows = small_sum([ref[:, attn + width_up :] for ref in groups[0]])
    at = 5 * layers
    for ref in biases:
        low_rows, high_rows = rows[at : at + layers], rows[at + layers : at + 2 * layers]
        lanes = lax.broadcasted_iota(jnp.int32, low_rows.shape, 1)
        both = jnp.where(lanes < depth, low_rows, pltpu.roll(high_rows, depth, 1))
        ref[...] = both[:, : ref.shape[1]]
        at += 2 * layers
    totals = total_of(parts)
    count = hidden_ref.shape[0]
    result_ref[...] = (hidden_ref[...] + totals[:count]).astype(BF)
    get.wait()
    total = row_norm_back(totals[count:], normed_ref[...], inv_std_ref[...])
    grad_ref[...] = (below_ref[...] + total).astype(BF)


def small_sum(parts):
    mine, core, near, core_near = (part.astype(F32) for part in parts)
    return (mine + near) + (core + core_near)


def vectors_kernel(layers, mine_ref, half_ref, bias_out_ref, gain_ref, shift_ref):
    vectors = mine_ref[...] + half_ref[...]
    depth = gain_ref.shape[2]
    for layer in range(layers):
        rows = vectors[5 * layer : 5 * layer + 5, :depth]
        bias_out_ref[layer, 0:1, :] = rows[:1]
        bias_out_ref[layer, 1:2, :] = rows[:1]
        gain_ref[layer] = rows[1:3]
        shift_ref[layer] = rows[3:5]


def call(kernel, outs, scratch, flops, *args, far=(), far_outs=(), limit=VMEM_BYTES, **more):
    def space(at, arg, far):
        if at in far:
            return pltpu.HBM
        return pltpu.SMEM if arg.shape == (1,) else pltpu.VMEM

    return pl.pallas_call(
        kernel,
        out_shape=outs,
        in_specs=[pl.BlockSpec(memory_space=space(at, arg, far)) for at, arg in enumerate(args)],
        out_specs=[
            pl.BlockSpec(memory_space=space(at, out, far_outs)) for at, out in enumerate(outs)
        ],
        scratch_shapes=scratch,
        compiler_params=pltpu.CompilerParams(vmem_limit_bytes=limit),
        cost_estimate=pl.CostEstimate(flops=flops, bytes_accessed=8_000_000, transcendentals=0),
        **more,
    )(*args)


def core_rows_summed(kept, sent):
    return (kept.astype(F32) + other_core(sent).astype(F32)).astype(BF)


def turned_groups(values):
    return values.reshape(2, -1, values.shape[1])[::-1].reshape(values.shape)


def pair_sum(mine):
    theirs = turned_groups(near_other_half(mine))
    return (mine.astype(F32) + theirs.astype(F32)).astype(BF)


def other_rows(mine, near):
    return other_core((mine.astype(F32) + turned_groups(near).astype(F32)).astype(BF))


def own_parts(*mines):
    count = mines[0].shape[0] // 2
    own = jnp.concatenate([mine[:count] for mine in mines])
    return own, near_group(jnp.concatenate([mine[count:] for mine in mines]))


def rotation(positions):
    exponents = jnp.arange(ROT // 2, dtype=F32) * (2.0 / ROT)
    inverse = jnp.power(10000.0, -exponents)
    phase = positions.astype(F32)[:, None] * inverse[None, :]
    cos, sin = jnp.cos(phase), jnp.sin(phase)
    none = jnp.zeros_like(sin)
    rest = jnp.zeros((positions.shape[0], HS - ROT), F32)
    tables = [[cos, cos, rest + 1.0], [-sin, none, rest], [none, sin, rest]]
    return jnp.stack([jnp.concatenate(t + t, axis=1) for t in tables])


def bias_places(owners, depth, starts, widths, shards):
    owner = jnp.arange(owners * depth, dtype=jnp.int32) // depth
    inner = jnp.arange(owners * depth, dtype=jnp.int32) % depth
    rows = []
    for start, width, shard, head in zip(starts, widths, shards, (3 * HS, None), strict=True):
        for first in (0, depth):
            at = owner * shard + inner + first - start
            fits = (inner + first < shard) & (at >= 0) & (at < width)
            if head is not None:
                at = at // head * HEAD + at % head
            rows.append(jnp.where(fits, at, -1))
    return jnp.stack(rows + rows)


def per_device(
    tokens,
    cotangent,
    doc_lens,
    block_pos,
    w_qkv,
    w_out,
    w_up,
    w_down,
    b_qkv,
    b_up,
    out_bias,
    norm_gain,
    norm_bias,
):
    row_count = tokens.shape[0]
    block_rows = row_count // 2
    core = lax.axis_index("ctx")
    owners = lax.axis_size("fsdp")
    layers, depth, width_qkv = w_qkv.shape
    width_qkv, width_out, hidden = width_qkv // 2, w_out.shape[1] // 2, w_up.shape[2] // 4
    place_z = lax.axis_index("fsdp") // NEAR % 2
    heads = width_out // HS
    attn = heads * HEAD
    width = attn + 2 * hidden
    wide = owners * depth
    rows = 4 * row_count

    core_at = core.astype(jnp.int32).reshape(1)
    place_at = place_z.astype(jnp.int32).reshape(1)
    sds = jax.ShapeDtypeStruct
    raw = (
        w_qkv,
        w_out.transpose(0, 2, 1),
        w_up,
        w_down.transpose(0, 2, 1),
        out_bias,
        norm_gain,
        norm_bias,
        b_qkv,
        b_up,
    )
    send, own_block, near_block = call(
        functools.partial(slabs_kernel, layers),
        (
            sds((owners, depth, width + LANES), BF),
            sds((depth, width), BF),
            sds((depth, width), BF),
        ),
        [pltpu.VMEM(a.shape, a.dtype) for a in raw]
        + [pltpu.VMEM((LANES, LANES), F32), pltpu.VMEM((8, LANES), F32)]
        + [pltpu.SemaphoreType.DMA((len(raw),))],
        1000,
        core_at,
        place_at,
        *raw,
        far=range(2, 2 + len(raw)),
    )
    starts, ends = ((own, near_other_half(own)) for own in (tokens, cotangent))
    starts, ends = ((o, other_core(o), n, other_core(n)) for o, n in (starts, ends))
    first = exchanged(send).reshape(wide, -1)
    pair = [own_block, near_group(near_block)]
    pair = jnp.where(place_z == 0, jnp.concatenate(pair), jnp.concatenate(pair[::-1]))
    pair, starts, ends = lax.optimization_barrier((pair, starts, ends))
    second = jnp.broadcast_to(pair[None], (owners // 2, *pair.shape))
    second = owners_in_order(exchanged_in_plane(second), owners)
    offsets = jnp.arange(block_rows, dtype=jnp.int32)
    positions = (block_pos[0][:, None] * block_rows + offsets[None, :]).reshape(2, row_count)
    positions = jnp.where(core == 0, positions, positions[::-1]).reshape(-1)
    doc_ends = jnp.cumsum(doc_lens[0])
    docs = jnp.sum((positions[:, None] >= doc_ends[None, :]).astype(jnp.int32), axis=1)
    allowed = (docs[:, None] == docs[None, :]) & (positions[None, :] <= positions[:, None])
    mask = jnp.where(allowed, 0.0, MASKED).astype(F32)
    table = rotation(positions)
    place = bias_places(
        owners,
        depth,
        (core * width_qkv, (2 * core + place_z) * hidden),
        (width_qkv, hidden),
        (b_qkv.shape[1], b_up.shape[1]),
    )

    flops = 2 * rows * wide * width
    part = sds((rows // 2, wide), BF)
    kept = State.shapes(rows, wide, heads, hidden)

    def vmem(*arrays):
        return [pltpu.VMEM(array.shape, array.dtype) for array in arrays]

    def copies(*counts):
        return [pltpu.SemaphoreType.DMA((count,)) for count in counts]

    slab_scratch = [
        pltpu.VMEM((wide, attn), BF),
        pltpu.VMEM((wide, 2 * hidden), BF),
        pltpu.SemaphoreType.DMA((3,)),
    ]
    kept_part, sent_part, vec, *state = call(
        functools.partial(first_kernel, layers),
        (part, part, sds((layers, VECTORS, wide), F32), *State.shapes(rows, wide, heads, hidden)),
        [
            *vmem(part, part, table, mask),
            *copies(2, 12),
            pltpu.VMEM((rows, wide), F32),
            pltpu.VMEM((wide, LANES), BF),
            *slab_scratch,
            *vmem(*kept),
        ],
        flops,
        *starts,
        first,
        place,
        table,
        mask,
        far=(4, 6, 7),
        far_outs=(0, 1, *range(3, 13)),
    )
    mine = pair_sum(core_rows_summed(kept_part, sent_part))
    mine, near, second = lax.optimization_barrier((mine, near_group(mine), second))
    scratch = [
        pltpu.VMEM((rows, wide), BF),
        pltpu.VMEM((rows, hidden), BF),
        pltpu.VMEM((rows // 2, attn), BF),
        pltpu.VMEM((rows, wide), F32),
        pltpu.VMEM((rows, wide), F32),
    ]
    *sums, slab, later_sums, result, normed, inv_std = call(
        last_kernel,
        (
            *(part,) * 4,
            sds((wide, width), BF),
            sds((8, wide), F32),
            sds((row_count, wide), F32),
            *kept[:2],
        ),
        [
            *vmem(table, mask, sds((row_count, wide), F32)),
            *copies(6, 7),
            *vmem(part, part, part, part, *kept, sds((rows, wide), BF)),
            *slab_scratch,
            *scratch,
        ],
        3 * flops,
        *starts,
        *ends,
        mine,
        near,
        other_rows(mine, near),
        vec,
        second,
        table,
        mask,
        far=(4, 5, 6, 7, 12, 13, 14),
        far_outs=(0, 1, 2, 3, 4, 6, 7, 8),
    )
    mine = pair_sum(core_rows_summed(*sums[2:]))
    mine, slab = lax.optimization_barrier((mine, pairs_together(slab, owners)))
    later = exchanged_in_plane(slab)
    ahead, near = lax.optimization_barrier((sums[:2], near_group(mine)))
    ahead = pair_sum(core_rows_summed(*ahead))
    kept_part, sent_part, slab, grad_below = call(
        functools.partial(back_kernel, layers),
        (part, part, sds((wide, width + LANES), BF), sds((row_count, wide), F32)),
        [
            *vmem(table),
            *copies(11, 2),
            *vmem(part, part, *kept, later_sums, sds((rows, wide), F32)),
            *vmem(sds((wide, LANES), BF)),
            *slab_scratch,
            *scratch,
        ],
        2 * flops,
        *ends,
        mine,
        near,
        other_rows(mine, near),
        normed,
        inv_std,
        later_sums,
        vec,
        first,
        place,
        table,
        *state,
        far=(11, *range(13, 24)),
        far_outs=(0, 1, 2),
    )
    slab = pairs_together(slab, owners)
    slab, later, ahead = lax.optimization_barrier((slab, later, ahead))
    earlier = exchanged_in_plane(slab)
    below = pair_sum(core_rows_summed(kept_part, sent_part))

    piece = sds((depth, width), BF)
    late = call(gather_late_kernel, (piece, piece), [], flops // 8, place_at, later)
    ends = own_parts(ahead, below)

    def of_all(own, near):
        return own, other_core(own), near_group(near), near_other_core(near)

    late = of_all(*late)
    earlier, late, ends = lax.optimization_barrier((earlier, late, ends))
    piece = sds((depth, width + LANES), BF)
    early = of_all(
        *call(
            gather_kernel, (piece, piece), [pltpu.VMEM((LANES, LANES), F32)], 1000, place_at, earlier
        )
    )
    small = small_sum([part[:, width:] for part in early])
    half = other_half(small)
    result, grad_tokens, grad_qkv, grad_out, grad_up, grad_down, grad_b_qkv, grad_b_up = call(
        functools.partial(finish_kernel, layers),
        (sds(tokens.shape, BF),) * 2
        + tuple(
            sds(shape, F32)
            for shape in (
                w_qkv.shape,
                (layers, depth, w_out.shape[1]),
                w_up.shape,
                (layers, depth, w_down.shape[1]),
                b_qkv.shape,
                b_up.shape,
            )
        ),
        [*vmem(sds((row_count, wide), F32), sds((row_count, 1), F32)), *copies(2)],
        flops // 8,
        core_at,
        place_at,
        *early,
        *late,
        *ends,
        grad_below,
        state[0],
        state[1],
        result,
        far=(13, 14),
    )
    vectors = call(
        functools.partial(vectors_kernel, layers),
        tuple(sds(a.shape, F32) for a in (out_bias, norm_gain, norm_bias)),
        [],
        1000,
        small,
        half,
    )
    return (
        result,
        grad_tokens,
        grad_qkv,
        grad_out.transpose(0, 2, 1),
        grad_up,
        grad_down.transpose(0, 2, 1),
        grad_b_qkv,
        grad_b_up,
        *vectors,
    )


def solution(mesh):
    in_specs = (
        P(("fsdp", "ctx"), None),
        P(("fsdp", "ctx"), None),
        P("fsdp", None),
        P("fsdp", None),
        P(None, "fsdp", "tp"),
        P(None, "tp", "fsdp"),
        P(None, "fsdp", "tp"),
        P(None, "tp", "fsdp"),
        P(None, ("tp", "fsdp")),
        P(None, ("tp", "fsdp")),
        P(None, None, "fsdp"),
        P(None, None, "fsdp"),
        P(None, None, "fsdp"),
    )
    out_specs = (P(("fsdp", "ctx"), None), P(("fsdp", "ctx"), None), *in_specs[4:])
    return jax.shard_map(
        per_device, mesh=mesh, in_specs=in_specs, out_specs=out_specs, check_vma=False
    )
```

```python
import functools

import jax
import jax.numpy as jnp
from jax import lax
from jax.experimental import pallas as pl
from jax.experimental.pallas import tpu as pltpu
from jax.sharding import PartitionSpec as P

HS = 64
ROT = 16
EPSILON = 1e-05
MASKED = -1e30
F32 = jnp.float32
BF = jnp.bfloat16
SWAP = [(0, 1), (1, 0)]
NEAR = 4
LANES = 128
CHUNK = 128
HEAD = 4 * HS
SCALE = HS ** (-0.5)
VMEM_BYTES = 62 * 1024 * 1024
GAIN_A, GAIN_B, SHIFT_A, SHIFT_B, BIAS_QKV, BIAS_UP, BIAS_OUT = range(7)
VECTORS = 8
SUM_OUT, SUM_GAIN_A, SUM_GAIN_B, SUM_SHIFT_A, SUM_SHIFT_B, SUM_QKV, SUM_UP = range(7)


def other_core(values):
    return lax.ppermute(values, "ctx", SWAP)


def other_half(values):
    return lax.ppermute(values, "tp", SWAP)


def other_core_and_half(values):
    return lax.ppermute(values, ("ctx", "tp"), [(0, 3), (1, 2), (2, 1), (3, 0)])


def near_group(values):
    owners = lax.axis_size("fsdp")
    return lax.ppermute(values, "fsdp", [(f, f ^ NEAR) for f in range(owners)])


def near_other_half(values):
    owners = lax.axis_size("fsdp")
    pairs = [(2 * f + t, 2 * (f ^ NEAR) + 1 - t) for f in range(owners) for t in (0, 1)]
    return lax.ppermute(values, ("fsdp", "tp"), pairs)


def near_other_core(values):
    owners = lax.axis_size("fsdp")
    pairs = [(2 * f + c, 2 * (f ^ NEAR) + 1 - c) for f in range(owners) for c in (0, 1)]
    return lax.ppermute(values, ("fsdp", "ctx"), pairs)


def exchanged(blocks):
    return lax.all_to_all(blocks, "fsdp", 0, 0, tiled=True)


def exchanged_in_plane(blocks):
    owners = lax.axis_size("fsdp")
    planes = [[f for f in range(owners) if f // NEAR % 2 == z] for z in (0, 1)]
    return lax.all_to_all(blocks, "fsdp", 0, 0, axis_index_groups=planes, tiled=True)


def pairs_together(values, owners):
    depth = values.shape[0] // owners
    pairs = [y * 2 * NEAR + x for y in range(owners // (2 * NEAR)) for x in range(NEAR)]
    order = [first + z * NEAR for first in pairs for z in (0, 1)]
    return jnp.concatenate([values[owner * depth : (owner + 1) * depth] for owner in order])


def owners_in_order(blocks, owners):
    width = blocks.shape[2]
    blocks = blocks.reshape(owners // (2 * NEAR), NEAR, 2, -1, width)
    return blocks.transpose(0, 2, 1, 3, 4).reshape(-1, width)


def dot(left, right, along=(1, 0)):
    dims = (((along[0],), (along[1],)), ((), ()))
    return lax.dot_general(left, right, dims, preferred_element_type=F32)


def over_rows(rows, step, carry=None, start=0):
    def body(at, kept):
        return step(pl.ds(pl.multiple_of(at * CHUNK, CHUNK), CHUNK), kept)

    return lax.fori_loop(start // CHUNK, rows // CHUNK, body, carry)


def by_eights(values):
    return values.reshape(-1, 8, values.shape[-1]).sum(axis=0)


def whole_sum(eights):
    return jnp.sum(eights, axis=0, keepdims=True)


def turned(tile, cos, left, right):
    return (
        tile * cos
        + pltpu.roll(tile, LANES - ROT // 2, 1) * left
        + pltpu.roll(tile, ROT // 2, 1) * right
    )


def row_norm(values):
    centered = values - jnp.mean(values, axis=-1, keepdims=True)
    inv_std = lax.rsqrt(jnp.mean(centered * centered, axis=-1, keepdims=True) + EPSILON)
    return centered * inv_std, inv_std


def row_norm_back(total, normed, inv_std):
    return inv_std * (
        total
        - jnp.mean(total, axis=-1, keepdims=True)
        - normed * jnp.mean(total * normed, axis=-1, keepdims=True)
    )


def one_hot(place_ref, at, width):
    rows = lax.broadcasted_iota(jnp.int32, (width, place_ref.shape[1]), 0)
    return (rows == place_ref[at : at + 1, :]).astype(F32).astype(BF)


class Slab:
    def __init__(self, far_heads_ref, far_ref, heads_ref, w_ref, arrived):
        self.heads_ref, self.w_ref = heads_ref, w_ref
        self.copies = [
            pltpu.make_async_copy(far_heads_ref, heads_ref, arrived.at[0]),
            pltpu.make_async_copy(far_ref, w_ref, arrived.at[1]),
        ]
        for copy in self.copies:
            copy.start()

    def wait(self):
        for copy in self.copies:
            copy.wait()
        return self.heads_ref, self.w_ref

    def give(self, far_heads_ref, far_ref, sent):
        copies = [
            pltpu.make_async_copy(self.heads_ref, far_heads_ref, sent.at[0]),
            pltpu.make_async_copy(self.w_ref, far_ref, sent.at[1]),
        ]
        for copy in copies:
            copy.start()
        for copy in copies:
            copy.wait()


class Copies:
    def __init__(self, semaphores):
        self.semaphores, self.started = semaphores, []

    def start(self, src, dst):
        copy = pltpu.make_async_copy(src, dst, self.semaphores.at[len(self.started)])
        copy.start()
        self.started.append(copy)

    def wait(self, begin=0, end=None):
        for copy in self.started[begin:end]:
            copy.wait()


class State:
    names = ("normed", "inv_std", "a", "m", "qk", "v", "p", "o", "gl", "slope")

    def __init__(self, refs, copies=None, far=()):
        for name, ref in zip(self.names, refs, strict=True):
            setattr(self, name, ref)
        self.copies, self.far = copies, dict(zip(self.names, far))

    def ready(self, *names):
        for name in names:
            if name in self.far:
                self.copies.start(getattr(self, name), self.far[name])

    @staticmethod
    def shapes(rows, depth, heads, hidden):
        group = rows // 2
        return (
            jax.ShapeDtypeStruct((rows, depth), F32),
            jax.ShapeDtypeStruct((rows, 1), F32),
            jax.ShapeDtypeStruct((group, depth), BF),
            jax.ShapeDtypeStruct((rows, depth), BF),
            jax.ShapeDtypeStruct((group, heads * 2 * HS), BF),
            jax.ShapeDtypeStruct((group, heads * HS), BF),
            jax.ShapeDtypeStruct((heads, group, group), F32),
            jax.ShapeDtypeStruct((group, heads * HEAD), BF),
            jax.ShapeDtypeStruct((rows, hidden), BF),
            jax.ShapeDtypeStruct((rows, hidden), F32),
        )


def places(rows):
    quarter = rows // 4
    return [(0, 0, 0), (quarter, 1, 0), (2 * quarter, 0, quarter), (3 * quarter, 1, quarter)]


def forward(state, vec_ref, slab, near_copies, table_ref, mask_ref, parts, wide_ref):
    rows, depth = state.normed.shape
    group = rows // 2
    heads = state.v.shape[1] // HS
    hidden = state.gl.shape[1]

    def affine_a(at, _):
        state.a[at, :] = (
            state.normed[at, :] * vec_ref[GAIN_A : GAIN_A + 1, :]
            + vec_ref[SHIFT_A : SHIFT_A + 1, :]
        ).astype(BF)

    def affine_b(at, _):
        state.m[at, :] = (
            state.normed[at, :] * vec_ref[GAIN_B : GAIN_B + 1, :]
            + vec_ref[SHIFT_B : SHIFT_B + 1, :]
        ).astype(BF)

    state.ready("normed", "inv_std")
    over_rows(group, affine_a)
    over_rows(rows, affine_b)
    state.ready("a", "m")
    heads_ref, w_ref = slab.wait()
    near_copies.wait()
    wide_ref[:group, :] = dot(state.a[...], heads_ref[...])
    state.o[...] = jnp.zeros_like(state.o)
    for head in range(heads):
        at = head * HEAD
        bias = vec_ref[BIAS_QKV : BIAS_QKV + 1, at : at + HEAD]
        tile = wide_ref[:group, at : at + LANES] + bias[:, :LANES]
        tile = turned(tile, table_ref[0], table_ref[1], table_ref[2]).astype(BF)
        value = wide_ref[:group, at + 2 * HS : at + 3 * HS] + bias[:, 2 * HS : 3 * HS]
        value = value.astype(BF)
        state.qk[:, head * LANES : (head + 1) * LANES] = tile
        state.v[:, head * HS : (head + 1) * HS] = value
        half = group // 2
        for top in (0, half):
            scores = dot(tile[top : top + half, :HS], tile[:, HS:], (1, 1))
            scores = scores * SCALE + mask_ref[top : top + half, :]
            exponent = jnp.exp(scores - jnp.max(scores, axis=1, keepdims=True))
            share = exponent * (1.0 / jnp.sum(exponent, axis=1, keepdims=True))
            state.p[head, top : top + half, :] = share
            state.o[top : top + half, at + 3 * HS : at + HEAD] = dot(
                share.astype(BF), value
            ).astype(BF)
    state.ready("qk", "v", "p", "o")
    wide_ref[:, :hidden] = dot(state.m[...], w_ref[:, :hidden])

    def gelu(at, _):
        up = wide_ref[at, :hidden] + vec_ref[BIAS_UP : BIAS_UP + 1, :hidden]
        below = 0.5 + 0.5 * lax.erf(up * (0.5**0.5))
        state.gl[at, :] = (up * below).astype(BF)
        state.slope[at, :] = below + up * (jnp.exp(-0.5 * up * up) * 0.3989422804014327)

    over_rows(rows, gelu)
    state.ready("gl", "slope")
    down = w_ref[:, hidden : 2 * hidden]
    part = dot(state.o[...], heads_ref[...], (1, 1))
    half = group // 2
    part = (part + dot(state.gl[:group, :], down, (1, 1))).astype(BF)
    near = dot(state.gl[group:, :], down, (1, 1)).astype(BF)
    for core, part_ref in enumerate(parts):
        at = core * half
        part_ref[:half, :] = part[at : at + half]
        part_ref[half:, :] = near[at : at + half]


def backward(
    owners, state, grad_ref, vec_ref, slab, table_ref, parts, sums_ref, scratch, put, far_parts
):
    low_ref, up_ref, qkv_ref, wide_ref, deep_ref = scratch
    heads_ref, w_ref = slab.heads_ref, slab.w_ref
    rows, depth = state.normed.shape
    group = rows // 2
    heads = state.v.shape[1] // HS
    attn, hidden = heads * HEAD, state.gl.shape[1]

    def lower(at, total):
        grad = grad_ref[at, :].astype(F32)
        low_ref[at, :] = grad.astype(BF)
        return total + by_eights(grad)

    total = over_rows(rows, lower, jnp.zeros((8, depth), F32))
    sums_ref[SUM_OUT : SUM_OUT + 1, :] = whole_sum(total) * 0.125
    low = low_ref[...]
    wide_ref[:, :hidden] = dot(low, w_ref[:, hidden : 2 * hidden])

    def through_gelu(at, total):
        up = (wide_ref[at, :hidden] * state.slope[at, :]).astype(BF)
        up_ref[at, :] = up
        return total + by_eights(up.astype(F32))

    total = over_rows(rows, through_gelu, jnp.zeros((8, hidden), F32))
    sums_ref[SUM_UP : SUM_UP + 1, :hidden] = whole_sum(total)
    wide_ref[:group, :] = dot(low_ref[:group, :], heads_ref[...])
    for head in range(heads):
        at = head * HEAD
        tile = state.qk[:, head * LANES : (head + 1) * LANES]
        query, key = tile[:, :HS], tile[:, HS:]
        value = state.v[:, head * HS : (head + 1) * HS]
        out = wide_ref[:group, at + 3 * HS : at + HEAD].astype(BF)
        half = group // 2
        grad_value, grad_key, grad_query = 0.0, 0.0, []
        for top in (0, half):
            share = state.p[head, top : top + half, :]
            grad = dot(out[top : top + half], value, (1, 1))
            delta = jnp.sum(share * grad, axis=1, keepdims=True)
            low_scores = (share * (grad - delta)).astype(BF)
            grad_value = grad_value + dot(share.astype(BF), out[top : top + half], (0, 0))
            grad_query.append(dot(low_scores, key))
            grad_key = grad_key + dot(low_scores, query[top : top + half], (0, 0))
        both = jnp.concatenate([jnp.concatenate(grad_query, axis=0), grad_key], axis=1) * SCALE
        both = turned(both, table_ref[0], -table_ref[1], -table_ref[2])
        qkv_ref[:, at : at + LANES] = both.astype(BF)
        qkv_ref[:, at + LANES : at + HEAD] = jnp.concatenate(
            [grad_value, jnp.zeros_like(grad_value)], axis=1
        ).astype(BF)

    def count_qkv(at, total):
        return total + by_eights(qkv_ref[at, :].astype(F32))

    total = over_rows(group, count_qkv, jnp.zeros((8, attn), F32))
    sums_ref[SUM_QKV : SUM_QKV + 1, :] = whole_sum(total)
    wide_ref[:group, :] = dot(qkv_ref[...], heads_ref[...], (1, 1))
    deep_ref[...] = dot(up_ref[...], w_ref[:, :hidden], (1, 1))

    def through_norms(with_first, part_ref, begin, to):
        def step(at, totals):
            there, at = moved(at, to), moved(at, begin)
            second, normed = deep_ref[at, :], state.normed[at, :]
            total, new = second * vec_ref[GAIN_B : GAIN_B + 1, :], (second * normed, second)
            if with_first:
                first = wide_ref[at, :]
                total = total + first * vec_ref[GAIN_A : GAIN_A + 1, :]
                new = (*new, first * normed, first)
            part_ref[there, :] = total.astype(BF)
            return tuple(old + by_eights(term) for old, term in zip(totals, new, strict=True))

        return step

    totals = (jnp.zeros((8, depth), F32),) * 4
    for begin, core, to in places(rows):
        count = 4 if begin < group else 2
        step = through_norms(begin < group, parts[core], begin, to)
        totals = (*over_rows(rows // 4, step, totals[:count]), *totals[count:])
    for row, total in zip((SUM_GAIN_B, SUM_SHIFT_B, SUM_GAIN_A, SUM_SHIFT_A), totals, strict=True):
        sums_ref[row : row + 1, :] = whole_sum(total)
    for ref, far_part_ref in zip(parts, far_parts, strict=True):
        put.start(ref, far_part_ref)
    heads_grad = dot(state.a[...], qkv_ref[...], (0, 0))
    heads_grad = heads_grad + dot(low_ref[:group, :], state.o[...], (0, 0))
    heads_ref[...] = pairs_together(heads_grad, owners).astype(BF)
    up_grad = dot(state.m[...], up_ref[...], (0, 0))
    w_ref[:, :hidden] = pairs_together(up_grad, owners).astype(BF)
    down_grad = dot(low, state.gl[...], (0, 0))
    w_ref[:, hidden : 2 * hidden] = pairs_together(down_grad, owners).astype(BF)


def first_kernel(layers, *refs):
    inputs, (far_ref, place_ref, far_table_ref, far_mask_ref, *rest) = refs[:4], refs[4:]
    far_parts, vec_ref, far_state, rest = rest[:2], rest[2], rest[3:13], rest[13:]
    parts, (table_ref, mask_ref, get, put), rest = rest[:2], rest[2:6], rest[6:]
    wide_ref, small_ref, heads_ref, w_ref, arrived, *state = rest
    get, put = Copies(get), Copies(put)
    state = State(state, put, far_state)
    attn = state.o.shape[1]
    hidden = state.gl.shape[1]
    width = attn + 2 * hidden
    copy = pltpu.make_async_copy(far_ref.at[:, width:], small_ref, arrived.at[2])
    copy.start()
    slab = Slab(far_ref.at[:, :attn], far_ref.at[:, attn:width], heads_ref, w_ref, arrived)
    get.start(far_table_ref, table_ref)
    get.start(far_mask_ref, mask_ref)
    copy.wait()
    small = jnp.transpose(small_ref[...].astype(F32))
    at = 6 * layers
    biases = small[at : at + 4 * layers].astype(BF)
    bias_qkv = dot(biases[:layers], one_hot(place_ref, 0, attn), (1, 1)) + dot(
        biases[layers : 2 * layers], one_hot(place_ref, 1, attn), (1, 1)
    )
    bias_up = dot(biases[2 * layers : 3 * layers], one_hot(place_ref, 2, hidden), (1, 1)) + dot(
        biases[3 * layers :], one_hot(place_ref, 3, hidden), (1, 1)
    )
    for layer in range(layers):
        rows = small[6 * layer : 6 * layer + 6]
        vec_ref[layer, GAIN_A : SHIFT_B + 1, :] = rows[2:]
        vec_ref[layer, BIAS_QKV : BIAS_QKV + 1, :] = bias_qkv[layer : layer + 1]
        vec_ref[layer, BIAS_UP : BIAS_UP + 1, :hidden] = bias_up[layer : layer + 1]
        vec_ref[layer, BIAS_OUT : BIAS_OUT + 1, :] = rows[0:1] + rows[1:2]
        vec_ref[layer, BIAS_OUT + 1 : VECTORS, :] = rows[0:1]

    for quarter, ref in enumerate(inputs):

        def enter(at, _, ref=ref, begin=quarter * ref.shape[0]):
            normed, inv_std = row_norm(ref[at, :].astype(F32))
            state.normed[moved(at, begin), :] = normed
            state.inv_std[moved(at, begin), :] = inv_std

        over_rows(ref.shape[0], enter)
    forward(state, vec_ref.at[0], slab, get, table_ref, mask_ref, parts, wide_ref)
    for ref, far_part_ref in zip(parts, far_parts, strict=True):
        put.start(ref, far_part_ref)
    put.wait()


def summed_rows(parts, at, there):
    mine, near = parts
    return mine[at, :].astype(F32) + near[there, :].astype(F32)


def moved(at, by):
    return pl.ds(pl.multiple_of(at.start + by, CHUNK), CHUNK)


def over_totals(parts, other_ref, inputs, take):
    own = parts[0].shape[0] // 2

    def own_core(at, _):
        take(at, summed_rows(parts, at, moved(at, own)), inputs[0][at, :])

    def near_own_core(at, _):
        total = summed_rows(parts, moved(at, own), at)
        take(moved(at, 2 * own), total, inputs[2][at, :])

    def other(at, _):
        take(moved(at, own), other_ref[at, :].astype(F32), inputs[1][at, :])

    def near_other(at, _):
        total = other_ref[moved(at, own), :].astype(F32)
        take(moved(at, 3 * own), total, inputs[3][at, :])

    for step in (own_core, near_own_core, other, near_other):
        over_rows(own, step)


def last_kernel(owners, *refs):
    inputs, far_ends, parts, refs = refs[:4], refs[4:8], refs[8:10], refs[10:]
    other_ref, vec_ref, far_ref, far_table_ref, far_mask_ref, *rest = refs
    far_parts, rest = rest[:4], rest[4:]
    slab_ref, sums_ref, far_hidden_ref, far_normed_ref, far_inv_std_ref, *rest = rest
    (table_ref, mask_ref, hidden_ref, get, put), rest = rest[:5], rest[5:]
    ahead, back, rest = rest[:2], rest[2:4], rest[4:]
    get, put = Copies(get), Copies(put)
    state, rest = State(rest[:10], put, (far_normed_ref, far_inv_std_ref)), rest[10:]
    grad_ref, heads_ref, w_ref, arrived, *scratch = rest
    attn, width = heads_ref.shape[1], heads_ref.shape[1] + w_ref.shape[1]
    slab = Slab(far_ref.at[:, :attn], far_ref.at[:, attn:width], heads_ref, w_ref, arrived)
    get.start(far_table_ref, table_ref)
    get.start(far_mask_ref, mask_ref)
    own = hidden_ref.shape[0]
    for quarter, ref in enumerate(far_ends):
        get.start(ref, grad_ref.at[quarter * own : (quarter + 1) * own, :])
    bias = vec_ref[0, BIAS_OUT : BIAS_OUT + 1, :]

    def enter(at, total, tokens):
        values = tokens.astype(F32) + total + bias
        scratch[3][at, :] = values
        normed, inv_std = row_norm(values)
        state.normed[at, :] = normed
        state.inv_std[at, :] = inv_std

    over_totals(parts, other_ref, inputs, enter)
    hidden_ref[...] = scratch[3][:own, :] + vec_ref[1, BIAS_OUT : BIAS_OUT + 1, :]
    put.start(hidden_ref, far_hidden_ref)
    forward(state, vec_ref.at[1], slab, get, table_ref, mask_ref, ahead, scratch[3])
    for ref, far_part_ref in zip(ahead, far_parts[:2], strict=True):
        put.start(ref, far_part_ref)
    backward(owners, state, grad_ref, vec_ref.at[1], slab, table_ref, back, sums_ref, scratch, put, far_parts[2:])
    slab.give(slab_ref.at[:, :attn], slab_ref.at[:, attn:width], arrived)
    put.wait()


def back_kernel(layers, owners, *refs):
    inputs, parts, refs = refs[:4], refs[4:6], refs[6:]
    other_ref, normed_ref, inv_std_ref, later_ref, vec_ref, far_ref, place_ref, far_table_ref, *rest = refs
    far_state, rest = rest[:10], rest[10:]
    far_back, (slab_ref, kept_ref, table_ref, get, put, *rest) = rest[:2], rest[2:]
    back, state, rest = rest[:2], State(rest[2:12]), rest[12:]
    sums_ref, below_ref, small_ref, heads_ref, w_ref, arrived, *scratch = rest
    get, put = Copies(get), Copies(put)
    attn, width = heads_ref.shape[1], heads_ref.shape[1] + w_ref.shape[1]
    slab = Slab(far_ref.at[:, :attn], far_ref.at[:, attn:width], heads_ref, w_ref, arrived)
    get.start(far_table_ref, table_ref)
    for name, ref in zip(State.names, far_state, strict=True):
        get.start(ref, getattr(state, name))
    attn, hidden = state.o.shape[1], state.gl.shape[1]

    def enter(at, total, cotangent):
        grad = row_norm_back(total, normed_ref[at, :], inv_std_ref[at, :])
        below_ref[at, :] = grad + cotangent.astype(F32)

    over_totals(parts, other_ref, inputs, enter)
    kept_ref[...] = below_ref[: kept_ref.shape[0], :]
    slab.wait()
    get.wait()
    backward(owners, state, below_ref, vec_ref.at[0], slab, table_ref, back, sums_ref, scratch, put, far_back)
    both = [sums_ref, later_ref]
    pad = jnp.zeros((8 - layers, attn), F32)
    qkv = jnp.concatenate([ref[SUM_QKV : SUM_QKV + 1, :] for ref in both] + [pad], axis=0)
    up = [ref[SUM_UP : SUM_UP + 1, :hidden] for ref in both] + [pad[:, :hidden]]
    up = jnp.concatenate(up, axis=0)
    spread = [
        dot(values.astype(BF), one_hot(place_ref, at, values.shape[1]))[:layers]
        for values, at in ((qkv, 0), (qkv, 1), (up, 2), (up, 3))
    ]
    small = [ref[: SUM_SHIFT_B + 1, :] for ref in both] + spread
    used = 9 * layers
    small = jnp.concatenate(small + [jnp.zeros((LANES - used, attn), F32)], axis=0)
    small_ref[...] = pairs_together(jnp.transpose(small), owners).astype(BF)
    copy = pltpu.make_async_copy(small_ref, slab_ref.at[:, width:], arrived.at[2])
    copy.start()
    slab.give(slab_ref.at[:, :attn], slab_ref.at[:, attn:width], arrived)
    copy.wait()
    put.wait()


def slabs_kernel(layers, core_ref, place_ref, *refs):
    far, (send_ref, own_ref, near_ref), refs = refs[:9], refs[9:12], refs[12:]
    local, (rows_ref, bias_ref, arrived) = refs[:9], refs[9:]
    copies = [
        pltpu.make_async_copy(src, dst, arrived.at[i])
        for i, (src, dst) in enumerate(zip(far, local, strict=True))
    ]
    for copy in copies:
        copy.start()
    for copy in copies:
        copy.wait()
    (qkv_ref, out_ref, up_ref, down_ref), vectors, biases = local[:4], local[4:7], local[7:9]
    depth, width_out = qkv_ref.shape[1], out_ref.shape[2] // 2
    hidden = up_ref.shape[2] // 4
    low = core_ref[0] == 0

    def half(values):
        width = values.shape[1] // 2
        return jnp.where(low, values[:, :width], values[:, width:])

    rows_ref[...] = jnp.zeros_like(rows_ref)
    at = 0
    for layer in range(layers):
        for ref in vectors:
            rows_ref[at : at + 2, :depth] = ref[layer].astype(F32)
            at += 2
    lanes = lax.broadcasted_iota(jnp.int32, bias_ref.shape, 1)
    for ref in biases:
        bias_ref[...] = jnp.zeros_like(bias_ref)
        bias_ref[:layers, : ref.shape[1]] = ref[...].astype(F32)
        for values in (bias_ref[...], pltpu.roll(bias_ref[...], LANES - depth, 1)):
            rows_ref[at : at + layers, :] = jnp.where(lanes < depth, values, 0.0)[:layers]
            at += layers
    small = jnp.transpose(rows_ref[...])[:depth].astype(BF)
    heads, wide = [], ([], [])
    for layer in range(layers):
        qkv, out = half(qkv_ref[layer]), half(out_ref[layer])
        up, down = half(up_ref[layer]), half(down_ref[layer])
        attn = []
        for head in range(width_out // HS):
            at = head * 3 * HS
            attn += [qkv[:, at : at + 3 * HS], out[:, head * HS : (head + 1) * HS]]
        heads.append(jnp.concatenate(attn, axis=1))
        for z in (0, 1):
            at = slice(z * hidden, (z + 1) * hidden)
            wide[z].append(jnp.concatenate([up[:, at], down[:, at]], axis=1))
    for z in (0, 1):
        block = jnp.concatenate([heads[0], wide[z][0], small], axis=1)
        for owner in range(send_ref.shape[0]):
            if owner // NEAR % 2 == z:
                send_ref[owner] = block
    first = place_ref[0] == 0
    own_ref[...] = jnp.concatenate([heads[1], jnp.where(first, *wide_of(wide, 0, 1))], axis=1)
    near_ref[...] = jnp.concatenate([heads[1], jnp.where(first, *wide_of(wide, 1, 0))], axis=1)


def wide_of(wide, *at):
    return [wide[z][1] for z in at]


def sum_of(got_ref, columns):
    total = got_ref[0, :, columns].astype(F32)
    for sender in range(1, got_ref.shape[0]):
        total = total + got_ref[sender, :, columns].astype(F32)
    return total


def put_sums(place_ref, got_ref, own_ref, near_ref):
    depth = own_ref.shape[0]
    step = 3 * LANES
    for begin in range(0, own_ref.shape[1], step):
        at = slice(begin, begin + step)
        total = sum_of(got_ref, at)
        low, high = total[:depth], total[depth:]
        own_ref[:, at] = jnp.where(place_ref[0] == 0, low, high).astype(BF)
        near_ref[:, at] = jnp.where(place_ref[0] == 0, high, low).astype(BF)


def total_of(refs):
    mine, near = refs
    return mine[...].astype(F32) + near[...].astype(F32)


def gather_late_kernel(place_ref, got_ref, own_ref, near_ref):
    put_sums(place_ref, got_ref, own_ref, near_ref)


def gather_kernel(place_ref, got_ref, own_ref, near_ref, pad_ref):
    depth, width = own_ref.shape[0], own_ref.shape[1] - LANES
    put_sums(place_ref, got_ref, own_ref.at[:, :width], near_ref.at[:, :width])
    pad_ref[...] = jnp.zeros_like(pad_ref)
    pad_ref[: 2 * depth, :] = sum_of(got_ref, slice(width, width + LANES))
    low = jnp.transpose(pad_ref[...])[:depth]
    high = pltpu.roll(low, LANES - depth, 1)
    own_ref[:, width:] = jnp.where(place_ref[0] == 0, low, high).astype(BF)
    near_ref[:, width:] = jnp.where(place_ref[0] == 0, high, low).astype(BF)


def finish_kernel(layers, core_ref, place_ref, *rest):
    groups, rest = (rest[:4], rest[4:8]), rest[8:]
    parts, (below_ref, far_normed_ref, far_inv_std_ref, *rest) = rest[:2], rest[2:]
    hidden_ref, *rest = rest
    result_ref, grad_ref, qkv_ref, out_ref, up_ref, down_ref, *biases = rest[:8]
    normed_ref, inv_std_ref, get = rest[8:]
    get = Copies(get)
    own = pl.ds(0, normed_ref.shape[0])
    get.start(far_normed_ref.at[own, :], normed_ref)
    get.start(far_inv_std_ref.at[own, :], inv_std_ref)
    width_qkv, width_out, width_up = (r.shape[2] // 2 for r in (qkv_ref, out_ref, up_ref))
    depth, heads = qkv_ref.shape[1], width_out // HS
    attn = heads * HEAD
    low, first = core_ref[0] == 0, place_ref[0] == 0

    def both_places(own, near):
        return jnp.where(first, own, near), jnp.where(first, near, own)

    hidden = width_up // 2
    for layer, group in enumerate(groups):
        mine, core, near, core_near = (ref[:, : attn + width_up].astype(F32) for ref in group)
        attention = (mine[:, :attn] + near[:, :attn], core[:, :attn] + core_near[:, :attn])
        sides = (jnp.where(low, *attention), jnp.where(low, *attention[::-1]))
        starts = [(values, head * HEAD) for values in sides for head in range(heads)]
        qkv_ref[layer] = jnp.concatenate([v[:, at : at + 3 * HS] for v, at in starts], axis=1)
        out_ref[layer] = jnp.concatenate([v[:, at + 3 * HS : at + HEAD] for v, at in starts], axis=1)
        for z, (ours, theirs) in enumerate(
            zip(both_places(mine, near), both_places(core, core_near), strict=True)
        ):
            for side, values in enumerate((jnp.where(low, ours, theirs), jnp.where(low, theirs, ours))):
                at = side * width_up + z * hidden
                up_ref[layer, :, at : at + hidden] = values[:, attn : attn + hidden]
                down_ref[layer, :, at : at + hidden] = values[:, attn + hidden : attn + 2 * hidden]
    rows = small_sum([ref[:, attn + width_up :] for ref in groups[0]])
    at = 5 * layers
    for ref in biases:
        low_rows, high_rows = rows[at : at + layers], rows[at + layers : at + 2 * layers]
        lanes = lax.broadcasted_iota(jnp.int32, low_rows.shape, 1)
        both = jnp.where(lanes < depth, low_rows, pltpu.roll(high_rows, depth, 1))
        ref[...] = both[:, : ref.shape[1]]
        at += 2 * layers
    totals = total_of(parts)
    count = hidden_ref.shape[0]
    result_ref[...] = (hidden_ref[...] + totals[:count]).astype(BF)
    get.wait()
    total = row_norm_back(totals[count:], normed_ref[...], inv_std_ref[...])
    grad_ref[...] = (below_ref[...] + total).astype(BF)


def small_sum(parts):
    mine, core, near, core_near = (part.astype(F32) for part in parts)
    return (mine + near) + (core + core_near)


def vectors_kernel(layers, mine_ref, half_ref, bias_out_ref, gain_ref, shift_ref):
    vectors = mine_ref[...] + half_ref[...]
    depth = gain_ref.shape[2]
    for layer in range(layers):
        rows = vectors[5 * layer : 5 * layer + 5, :depth]
        bias_out_ref[layer, 0:1, :] = rows[:1]
        bias_out_ref[layer, 1:2, :] = rows[:1]
        gain_ref[layer] = rows[1:3]
        shift_ref[layer] = rows[3:5]


def call(kernel, outs, scratch, flops, *args, far=(), far_outs=(), limit=VMEM_BYTES, **more):
    def space(at, arg, far):
        if at in far:
            return pltpu.HBM
        return pltpu.SMEM if arg.shape == (1,) else pltpu.VMEM

    return pl.pallas_call(
        kernel,
        out_shape=outs,
        in_specs=[pl.BlockSpec(memory_space=space(at, arg, far)) for at, arg in enumerate(args)],
        out_specs=[
            pl.BlockSpec(memory_space=space(at, out, far_outs)) for at, out in enumerate(outs)
        ],
        scratch_shapes=scratch,
        compiler_params=pltpu.CompilerParams(vmem_limit_bytes=limit),
        cost_estimate=pl.CostEstimate(flops=flops, bytes_accessed=8_000_000, transcendentals=0),
        **more,
    )(*args)


def core_rows_summed(kept, sent):
    return (kept.astype(F32) + other_core(sent).astype(F32)).astype(BF)


def turned_groups(values):
    return values.reshape(2, -1, values.shape[1])[::-1].reshape(values.shape)


def pair_sum(mine):
    theirs = turned_groups(near_other_half(mine))
    return (mine.astype(F32) + theirs.astype(F32)).astype(BF)


def other_rows(mine, near):
    return other_core((mine.astype(F32) + turned_groups(near).astype(F32)).astype(BF))


def own_parts(*mines):
    count = mines[0].shape[0] // 2
    own = jnp.concatenate([mine[:count] for mine in mines])
    return own, near_group(jnp.concatenate([mine[count:] for mine in mines]))


def rotation(positions):
    exponents = jnp.arange(ROT // 2, dtype=F32) * (2.0 / ROT)
    inverse = jnp.power(10000.0, -exponents)
    phase = positions.astype(F32)[:, None] * inverse[None, :]
    cos, sin = jnp.cos(phase), jnp.sin(phase)
    none = jnp.zeros_like(sin)
    rest = jnp.zeros((positions.shape[0], HS - ROT), F32)
    tables = [[cos, cos, rest + 1.0], [-sin, none, rest], [none, sin, rest]]
    return jnp.stack([jnp.concatenate(t + t, axis=1) for t in tables])


def bias_places(owners, depth, starts, widths, shards):
    owner = jnp.arange(owners * depth, dtype=jnp.int32) // depth
    inner = jnp.arange(owners * depth, dtype=jnp.int32) % depth
    rows = []
    for start, width, shard, head in zip(starts, widths, shards, (3 * HS, None), strict=True):
        for first in (0, depth):
            at = owner * shard + inner + first - start
            fits = (inner + first < shard) & (at >= 0) & (at < width)
            if head is not None:
                at = at // head * HEAD + at % head
            rows.append(jnp.where(fits, at, -1))
    return jnp.stack(rows + rows)


def per_device(
    tokens,
    cotangent,
    doc_lens,
    block_pos,
    w_qkv,
    w_out,
    w_up,
    w_down,
    b_qkv,
    b_up,
    out_bias,
    norm_gain,
    norm_bias,
):
    row_count = tokens.shape[0]
    block_rows = row_count // 2
    core = lax.axis_index("ctx")
    owners = lax.axis_size("fsdp")
    layers, depth, width_qkv = w_qkv.shape
    width_qkv, width_out, hidden = width_qkv // 2, w_out.shape[1] // 2, w_up.shape[2] // 4
    place_z = lax.axis_index("fsdp") // NEAR % 2
    heads = width_out // HS
    attn = heads * HEAD
    width = attn + 2 * hidden
    wide = owners * depth
    rows = 4 * row_count

    core_at = core.astype(jnp.int32).reshape(1)
    place_at = place_z.astype(jnp.int32).reshape(1)
    sds = jax.ShapeDtypeStruct
    raw = (
        w_qkv,
        w_out.transpose(0, 2, 1),
        w_up,
        w_down.transpose(0, 2, 1),
        out_bias,
        norm_gain,
        norm_bias,
        b_qkv,
        b_up,
    )
    send, own_block, near_block = call(
        functools.partial(slabs_kernel, layers),
        (
            sds((owners, depth, width + LANES), BF),
            sds((depth, width), BF),
            sds((depth, width), BF),
        ),
        [pltpu.VMEM(a.shape, a.dtype) for a in raw]
        + [pltpu.VMEM((LANES, LANES), F32), pltpu.VMEM((8, LANES), F32)]
        + [pltpu.SemaphoreType.DMA((len(raw),))],
        1000,
        core_at,
        place_at,
        *raw,
        far=range(2, 2 + len(raw)),
    )
    starts, ends = ((own, near_other_half(own)) for own in (tokens, cotangent))
    starts, ends = ((o, other_core(o), n, other_core(n)) for o, n in (starts, ends))
    first = exchanged(send).reshape(wide, -1)
    pair = [own_block, near_group(near_block)]
    pair = jnp.where(place_z == 0, jnp.concatenate(pair), jnp.concatenate(pair[::-1]))
    pair, starts, ends = lax.optimization_barrier((pair, starts, ends))
    second = jnp.broadcast_to(pair[None], (owners // 2, *pair.shape))
    second = owners_in_order(exchanged_in_plane(second), owners)
    offsets = jnp.arange(block_rows, dtype=jnp.int32)
    positions = (block_pos[0][:, None] * block_rows + offsets[None, :]).reshape(2, row_count)
    positions = jnp.where(core == 0, positions, positions[::-1]).reshape(-1)
    doc_ends = jnp.cumsum(doc_lens[0])
    docs = jnp.sum((positions[:, None] >= doc_ends[None, :]).astype(jnp.int32), axis=1)
    allowed = (docs[:, None] == docs[None, :]) & (positions[None, :] <= positions[:, None])
    mask = jnp.where(allowed, 0.0, MASKED).astype(F32)
    table = rotation(positions)
    place = bias_places(
        owners,
        depth,
        (core * width_qkv, (2 * core + place_z) * hidden),
        (width_qkv, hidden),
        (b_qkv.shape[1], b_up.shape[1]),
    )

    flops = 2 * rows * wide * width
    part = sds((rows // 2, wide), BF)
    kept = State.shapes(rows, wide, heads, hidden)

    def vmem(*arrays):
        return [pltpu.VMEM(array.shape, array.dtype) for array in arrays]

    def copies(*counts):
        return [pltpu.SemaphoreType.DMA((count,)) for count in counts]

    slab_scratch = [
        pltpu.VMEM((wide, attn), BF),
        pltpu.VMEM((wide, 2 * hidden), BF),
        pltpu.SemaphoreType.DMA((3,)),
    ]
    kept_part, sent_part, vec, *state = call(
        functools.partial(first_kernel, layers),
        (part, part, sds((layers, VECTORS, wide), F32), *State.shapes(rows, wide, heads, hidden)),
        [
            *vmem(part, part, table, mask),
            *copies(2, 12),
            pltpu.VMEM((rows, wide), F32),
            pltpu.VMEM((wide, LANES), BF),
            *slab_scratch,
            *vmem(*kept),
        ],
        flops,
        *starts,
        first,
        place,
        table,
        mask,
        far=(4, 6, 7),
        far_outs=(0, 1, *range(3, 13)),
    )
    mine = pair_sum(core_rows_summed(kept_part, sent_part))
    mine, near, second = lax.optimization_barrier((mine, near_group(mine), second))
    scratch = [
        pltpu.VMEM((rows, wide), BF),
        pltpu.VMEM((rows, hidden), BF),
        pltpu.VMEM((rows // 2, attn), BF),
        pltpu.VMEM((rows, wide), F32),
        pltpu.VMEM((rows, wide), F32),
    ]
    *sums, slab, later_sums, result, normed, inv_std = call(
        functools.partial(last_kernel, owners),
        (
            *(part,) * 4,
            sds((wide, width), BF),
            sds((8, wide), F32),
            sds((row_count, wide), F32),
            *kept[:2],
        ),
        [
            *vmem(table, mask, sds((row_count, wide), F32)),
            *copies(6, 7),
            *vmem(part, part, part, part, *kept, sds((rows, wide), BF)),
            *slab_scratch,
            *scratch,
        ],
        3 * flops,
        *starts,
        *ends,
        mine,
        near,
        other_rows(mine, near),
        vec,
        second,
        table,
        mask,
        far=(4, 5, 6, 7, 12, 13, 14),
        far_outs=(0, 1, 2, 3, 4, 6, 7, 8),
    )
    mine, slab = lax.optimization_barrier((core_rows_summed(*sums[2:]), slab))
    later = exchanged_in_plane(slab.reshape(owners // 2, -1, width))
    ahead, mine = lax.optimization_barrier((sums[:2], pair_sum(mine)))
    near = near_group(mine)
    ahead = pair_sum(core_rows_summed(*ahead))
    kept_part, sent_part, slab, grad_below = call(
        functools.partial(back_kernel, layers, owners),
        (part, part, sds((wide, width + LANES), BF), sds((row_count, wide), F32)),
        [
            *vmem(table),
            *copies(11, 2),
            *vmem(part, part, *kept, later_sums, sds((rows, wide), F32)),
            *vmem(sds((wide, LANES), BF)),
            *slab_scratch,
            *scratch,
        ],
        2 * flops,
        *ends,
        mine,
        near,
        other_rows(mine, near),
        normed,
        inv_std,
        later_sums,
        vec,
        first,
        place,
        table,
        *state,
        far=(11, *range(13, 24)),
        far_outs=(0, 1, 2),
    )
    slab, later, ahead = lax.optimization_barrier((slab, later, ahead))
    earlier = exchanged_in_plane(slab.reshape(owners // 2, -1, width + LANES))
    below = pair_sum(core_rows_summed(kept_part, sent_part))

    piece = sds((depth, width), BF)
    late = call(gather_late_kernel, (piece, piece), [], flops // 8, place_at, later)
    ends = own_parts(ahead, below)

    def of_all(own, near):
        return own, other_core(own), near_group(near), near_other_core(near)

    late = of_all(*late)
    earlier, late, ends = lax.optimization_barrier((earlier, late, ends))
    piece = sds((depth, width + LANES), BF)
    early = of_all(
        *call(
            gather_kernel, (piece, piece), [pltpu.VMEM((LANES, LANES), F32)], 1000, place_at, earlier
        )
    )
    small = small_sum([part[:, width:] for part in early])
    half = other_half(small)
    result, grad_tokens, grad_qkv, grad_out, grad_up, grad_down, grad_b_qkv, grad_b_up = call(
        functools.partial(finish_kernel, layers),
        (sds(tokens.shape, BF),) * 2
        + tuple(
            sds(shape, F32)
            for shape in (
                w_qkv.shape,
                (layers, depth, w_out.shape[1]),
                w_up.shape,
                (layers, depth, w_down.shape[1]),
                b_qkv.shape,
                b_up.shape,
            )
        ),
        [*vmem(sds((row_count, wide), F32), sds((row_count, 1), F32)), *copies(2)],
        flops // 8,
        core_at,
        place_at,
        *early,
        *late,
        *ends,
        grad_below,
        state[0],
        state[1],
        result,
        far=(13, 14),
    )
    vectors = call(
        functools.partial(vectors_kernel, layers),
        tuple(sds(a.shape, F32) for a in (out_bias, norm_gain, norm_bias)),
        [],
        1000,
        small,
        half,
    )
    return (
        result,
        grad_tokens,
        grad_qkv,
        grad_out.transpose(0, 2, 1),
        grad_up,
        grad_down.transpose(0, 2, 1),
        grad_b_qkv,
        grad_b_up,
        *vectors,
    )


def solution(mesh):
    in_specs = (
        P(("fsdp", "ctx"), None),
        P(("fsdp", "ctx"), None),
        P("fsdp", None),
        P("fsdp", None),
        P(None, "fsdp", "tp"),
        P(None, "tp", "fsdp"),
        P(None, "fsdp", "tp"),
        P(None, "tp", "fsdp"),
        P(None, ("tp", "fsdp")),
        P(None, ("tp", "fsdp")),
        P(None, None, "fsdp"),
        P(None, None, "fsdp"),
        P(None, None, "fsdp"),
    )
    out_specs = (P(("fsdp", "ctx"), None), P(("fsdp", "ctx"), None), *in_specs[4:])
    return jax.shard_map(
        per_device, mesh=mesh, in_specs=in_specs, out_specs=out_specs, check_vma=False
    )
```

```python
import functools

import jax
import jax.numpy as jnp
from jax import lax
from jax.experimental import pallas as pl
from jax.experimental.pallas import tpu as pltpu
from jax.sharding import PartitionSpec as P

HS = 64
ROT = 16
EPSILON = 1e-05
MASKED = -1e30
F32 = jnp.float32
BF = jnp.bfloat16
SWAP = [(0, 1), (1, 0)]
NEAR = 4
LANES = 128
CHUNK = 128
HEAD = 4 * HS
SCALE = HS ** (-0.5)
VMEM_BYTES = 62 * 1024 * 1024
GAIN_A, GAIN_B, SHIFT_A, SHIFT_B, BIAS_QKV, BIAS_UP, BIAS_OUT = range(7)
VECTORS = 8
SUM_OUT, SUM_GAIN_A, SUM_GAIN_B, SUM_SHIFT_A, SUM_SHIFT_B, SUM_QKV, SUM_UP = range(7)


def other_core(values):
    return lax.ppermute(values, "ctx", SWAP)


def other_half(values):
    return lax.ppermute(values, "tp", SWAP)


def other_core_and_half(values):
    return lax.ppermute(values, ("ctx", "tp"), [(0, 3), (1, 2), (2, 1), (3, 0)])


def near_group(values):
    owners = lax.axis_size("fsdp")
    return lax.ppermute(values, "fsdp", [(f, f ^ NEAR) for f in range(owners)])


def near_other_half(values):
    owners = lax.axis_size("fsdp")
    pairs = [(2 * f + t, 2 * (f ^ NEAR) + 1 - t) for f in range(owners) for t in (0, 1)]
    return lax.ppermute(values, ("fsdp", "tp"), pairs)


def near_other_core(values):
    owners = lax.axis_size("fsdp")
    pairs = [(2 * f + c, 2 * (f ^ NEAR) + 1 - c) for f in range(owners) for c in (0, 1)]
    return lax.ppermute(values, ("fsdp", "ctx"), pairs)


def exchanged(blocks):
    return lax.all_to_all(blocks, "fsdp", 0, 0, tiled=True)


def exchanged_in_plane(blocks):
    owners = lax.axis_size("fsdp")
    planes = [[f for f in range(owners) if f // NEAR % 2 == z] for z in (0, 1)]
    return lax.all_to_all(blocks, "fsdp", 0, 0, axis_index_groups=planes, tiled=True)


def pairs_together(values, owners):
    depth = values.shape[0] // owners
    pairs = [y * 2 * NEAR + x for y in range(owners // (2 * NEAR)) for x in range(NEAR)]
    order = [first + z * NEAR for first in pairs for z in (0, 1)]
    return jnp.concatenate([values[owner * depth : (owner + 1) * depth] for owner in order])


def owners_in_order(blocks, owners):
    width = blocks.shape[2]
    blocks = blocks.reshape(owners // (2 * NEAR), NEAR, 2, -1, width)
    return blocks.transpose(0, 2, 1, 3, 4).reshape(-1, width)


def dot(left, right, along=(1, 0)):
    dims = (((along[0],), (along[1],)), ((), ()))
    return lax.dot_general(left, right, dims, preferred_element_type=F32)


def over_rows(rows, step, carry=None, start=0):
    def body(at, kept):
        return step(pl.ds(pl.multiple_of(at * CHUNK, CHUNK), CHUNK), kept)

    return lax.fori_loop(start // CHUNK, rows // CHUNK, body, carry, unroll=True)


def by_eights(values):
    return values.reshape(-1, 8, values.shape[-1]).sum(axis=0)


def whole_sum(eights):
    return jnp.sum(eights, axis=0, keepdims=True)


def turned(tile, cos, left, right):
    return (
        tile * cos
        + pltpu.roll(tile, LANES - ROT // 2, 1) * left
        + pltpu.roll(tile, ROT // 2, 1) * right
    )


def row_norm(values):
    centered = values - jnp.mean(values, axis=-1, keepdims=True)
    inv_std = lax.rsqrt(jnp.mean(centered * centered, axis=-1, keepdims=True) + EPSILON)
    return centered * inv_std, inv_std


def row_norm_back(total, normed, inv_std):
    return inv_std * (
        total
        - jnp.mean(total, axis=-1, keepdims=True)
        - normed * jnp.mean(total * normed, axis=-1, keepdims=True)
    )


def one_hot(place_ref, at, width):
    rows = lax.broadcasted_iota(jnp.int32, (width, place_ref.shape[1]), 0)
    return (rows == place_ref[at : at + 1, :]).astype(F32).astype(BF)


class Slab:
    def __init__(self, far_heads_ref, far_ref, heads_ref, w_ref, arrived):
        self.heads_ref, self.w_ref = heads_ref, w_ref
        self.copies = [
            pltpu.make_async_copy(far_heads_ref, heads_ref, arrived.at[0]),
            pltpu.make_async_copy(far_ref, w_ref, arrived.at[1]),
        ]
        for copy in self.copies:
            copy.start()

    def wait(self):
        for copy in self.copies:
            copy.wait()
        return self.heads_ref, self.w_ref

    def give(self, put, far_ref):
        attn, hidden = self.heads_ref.shape[1], self.w_ref.shape[1] // 2
        self.put = put
        self.pieces = [
            (self.heads_ref, far_ref.at[:, :attn]),
            (self.w_ref.at[:, :hidden], far_ref.at[:, attn : attn + hidden]),
            (self.w_ref.at[:, hidden:], far_ref.at[:, attn + hidden : attn + 2 * hidden]),
        ]

    def sent(self, piece):
        self.put.start(*self.pieces[piece])


class Copies:
    def __init__(self, semaphores):
        self.semaphores, self.started = semaphores, []

    def start(self, src, dst):
        copy = pltpu.make_async_copy(src, dst, self.semaphores.at[len(self.started)])
        copy.start()
        self.started.append(copy)

    def wait(self, begin=0, end=None):
        for copy in self.started[begin:end]:
            copy.wait()


class State:
    names = ("normed", "inv_std", "a", "m", "qk", "v", "p", "o", "gl", "slope")

    def __init__(self, refs, copies=None, far=()):
        for name, ref in zip(self.names, refs, strict=True):
            setattr(self, name, ref)
        self.copies, self.far = copies, dict(zip(self.names, far))

    def ready(self, *names):
        for name in names:
            if name in self.far:
                self.copies.start(getattr(self, name), self.far[name])

    @staticmethod
    def shapes(rows, depth, heads, hidden):
        group = rows // 2
        return (
            jax.ShapeDtypeStruct((rows, depth), F32),
            jax.ShapeDtypeStruct((rows, 1), F32),
            jax.ShapeDtypeStruct((group, depth), BF),
            jax.ShapeDtypeStruct((rows, depth), BF),
            jax.ShapeDtypeStruct((group, heads * 2 * HS), BF),
            jax.ShapeDtypeStruct((group, heads * HS), BF),
            jax.ShapeDtypeStruct((heads, group, group), F32),
            jax.ShapeDtypeStruct((group, heads * HEAD), BF),
            jax.ShapeDtypeStruct((rows, hidden), BF),
            jax.ShapeDtypeStruct((rows, hidden), F32),
        )


def places(rows):
    quarter = rows // 4
    return [(0, 0, 0), (quarter, 1, 0), (2 * quarter, 0, quarter), (3 * quarter, 1, quarter)]


def forward(state, vec_ref, slab, near_copies, table_ref, mask_ref, parts, wide_ref):
    rows, depth = state.normed.shape
    group = rows // 2
    heads = state.v.shape[1] // HS
    hidden = state.gl.shape[1]

    def affine_a(at, _):
        state.a[at, :] = (
            state.normed[at, :] * vec_ref[GAIN_A : GAIN_A + 1, :]
            + vec_ref[SHIFT_A : SHIFT_A + 1, :]
        ).astype(BF)

    def affine_b(at, _):
        state.m[at, :] = (
            state.normed[at, :] * vec_ref[GAIN_B : GAIN_B + 1, :]
            + vec_ref[SHIFT_B : SHIFT_B + 1, :]
        ).astype(BF)

    state.ready("normed", "inv_std")
    over_rows(group, affine_a)
    over_rows(rows, affine_b)
    state.ready("a", "m")
    heads_ref, w_ref = slab.wait()
    near_copies.wait()
    wide_ref[:group, :] = dot(state.a[...], heads_ref[...])
    state.o[...] = jnp.zeros_like(state.o)
    for head in range(heads):
        at = head * HEAD
        bias = vec_ref[BIAS_QKV : BIAS_QKV + 1, at : at + HEAD]
        tile = wide_ref[:group, at : at + LANES] + bias[:, :LANES]
        tile = turned(tile, table_ref[0], table_ref[1], table_ref[2]).astype(BF)
        value = wide_ref[:group, at + 2 * HS : at + 3 * HS] + bias[:, 2 * HS : 3 * HS]
        value = value.astype(BF)
        state.qk[:, head * LANES : (head + 1) * LANES] = tile
        state.v[:, head * HS : (head + 1) * HS] = value
        half = group // 2
        for top in (0, half):
            scores = dot(tile[top : top + half, :HS], tile[:, HS:], (1, 1))
            scores = scores * SCALE + mask_ref[top : top + half, :]
            exponent = jnp.exp(scores - jnp.max(scores, axis=1, keepdims=True))
            share = exponent * (1.0 / jnp.sum(exponent, axis=1, keepdims=True))
            state.p[head, top : top + half, :] = share
            state.o[top : top + half, at + 3 * HS : at + HEAD] = dot(
                share.astype(BF), value
            ).astype(BF)
    state.ready("qk", "v", "p", "o")
    wide_ref[:, :hidden] = dot(state.m[...], w_ref[:, :hidden])

    def gelu(at, _):
        up = wide_ref[at, :hidden] + vec_ref[BIAS_UP : BIAS_UP + 1, :hidden]
        below = 0.5 + 0.5 * lax.erf(up * (0.5**0.5))
        state.gl[at, :] = (up * below).astype(BF)
        state.slope[at, :] = below + up * (jnp.exp(-0.5 * up * up) * 0.3989422804014327)

    over_rows(rows, gelu)
    state.ready("gl", "slope")
    down = w_ref[:, hidden : 2 * hidden]
    part = dot(state.o[...], heads_ref[...], (1, 1))
    half = group // 2
    part = (part + dot(state.gl[:group, :], down, (1, 1))).astype(BF)
    near = dot(state.gl[group:, :], down, (1, 1)).astype(BF)
    for core, part_ref in enumerate(parts):
        at = core * half
        part_ref[:half, :] = part[at : at + half]
        part_ref[half:, :] = near[at : at + half]


def backward(
    owners, state, grad_ref, vec_ref, slab, table_ref, parts, sums_ref, scratch, put, far_parts
):
    low_ref, up_ref, qkv_ref, wide_ref, deep_ref = scratch
    heads_ref, w_ref = slab.heads_ref, slab.w_ref
    rows, depth = state.normed.shape
    group = rows // 2
    heads = state.v.shape[1] // HS
    attn, hidden = heads * HEAD, state.gl.shape[1]

    def lower(at, total):
        grad = grad_ref[at, :].astype(F32)
        low_ref[at, :] = grad.astype(BF)
        return total + by_eights(grad)

    total = over_rows(rows, lower, jnp.zeros((8, depth), F32))
    sums_ref[SUM_OUT : SUM_OUT + 1, :] = whole_sum(total) * 0.125
    low = low_ref[...]
    wide_ref[:, :hidden] = dot(low, w_ref[:, hidden : 2 * hidden])

    def through_gelu(at, total):
        up = (wide_ref[at, :hidden] * state.slope[at, :]).astype(BF)
        up_ref[at, :] = up
        return total + by_eights(up.astype(F32))

    total = over_rows(rows, through_gelu, jnp.zeros((8, hidden), F32))
    sums_ref[SUM_UP : SUM_UP + 1, :hidden] = whole_sum(total)
    wide_ref[:group, :] = dot(low_ref[:group, :], heads_ref[...])
    for head in range(heads):
        at = head * HEAD
        tile = state.qk[:, head * LANES : (head + 1) * LANES]
        query, key = tile[:, :HS], tile[:, HS:]
        value = state.v[:, head * HS : (head + 1) * HS]
        out = wide_ref[:group, at + 3 * HS : at + HEAD].astype(BF)
        half = group // 2
        grad_value, grad_key, grad_query = 0.0, 0.0, []
        for top in (0, half):
            share = state.p[head, top : top + half, :]
            grad = dot(out[top : top + half], value, (1, 1))
            delta = jnp.sum(share * grad, axis=1, keepdims=True)
            low_scores = (share * (grad - delta)).astype(BF)
            grad_value = grad_value + dot(share.astype(BF), out[top : top + half], (0, 0))
            grad_query.append(dot(low_scores, key))
            grad_key = grad_key + dot(low_scores, query[top : top + half], (0, 0))
        both = jnp.concatenate([jnp.concatenate(grad_query, axis=0), grad_key], axis=1) * SCALE
        both = turned(both, table_ref[0], -table_ref[1], -table_ref[2])
        qkv_ref[:, at : at + LANES] = both.astype(BF)
        qkv_ref[:, at + LANES : at + HEAD] = jnp.concatenate(
            [grad_value, jnp.zeros_like(grad_value)], axis=1
        ).astype(BF)

    def count_qkv(at, total):
        return total + by_eights(qkv_ref[at, :].astype(F32))

    total = over_rows(group, count_qkv, jnp.zeros((8, attn), F32))
    sums_ref[SUM_QKV : SUM_QKV + 1, :] = whole_sum(total)
    wide_ref[:group, :] = dot(qkv_ref[...], heads_ref[...], (1, 1))
    deep_ref[...] = dot(up_ref[...], w_ref[:, :hidden], (1, 1))

    def through_norms(with_first, part_ref, begin, to):
        def step(at, totals):
            there, at = moved(at, to), moved(at, begin)
            second, normed = deep_ref[at, :], state.normed[at, :]
            total, new = second * vec_ref[GAIN_B : GAIN_B + 1, :], (second * normed, second)
            if with_first:
                first = wide_ref[at, :]
                total = total + first * vec_ref[GAIN_A : GAIN_A + 1, :]
                new = (*new, first * normed, first)
            part_ref[there, :] = total.astype(BF)
            return tuple(old + by_eights(term) for old, term in zip(totals, new, strict=True))

        return step

    totals = (jnp.zeros((8, depth), F32),) * 4
    for begin, core, to in places(rows):
        count = 4 if begin < group else 2
        step = through_norms(begin < group, parts[core], begin, to)
        totals = (*over_rows(rows // 4, step, totals[:count]), *totals[count:])
    for row, total in zip((SUM_GAIN_B, SUM_SHIFT_B, SUM_GAIN_A, SUM_SHIFT_A), totals, strict=True):
        sums_ref[row : row + 1, :] = whole_sum(total)
    for ref, far_part_ref in zip(parts, far_parts, strict=True):
        put.start(ref, far_part_ref)
    heads_grad = dot(state.a[...], qkv_ref[...], (0, 0))
    heads_grad = heads_grad + dot(low_ref[:group, :], state.o[...], (0, 0))
    heads_ref[...] = pairs_together(heads_grad, owners).astype(BF)
    slab.sent(0)
    up_grad = dot(state.m[...], up_ref[...], (0, 0))
    w_ref[:, :hidden] = pairs_together(up_grad, owners).astype(BF)
    slab.sent(1)
    down_grad = dot(low, state.gl[...], (0, 0))
    w_ref[:, hidden : 2 * hidden] = pairs_together(down_grad, owners).astype(BF)
    slab.sent(2)


def first_kernel(layers, *refs):
    inputs, (far_ref, place_ref, far_table_ref, far_mask_ref, *rest) = refs[:4], refs[4:]
    far_parts, vec_ref, far_state, rest = rest[:2], rest[2], rest[3:13], rest[13:]
    parts, (table_ref, mask_ref, get, put), rest = rest[:2], rest[2:6], rest[6:]
    wide_ref, small_ref, heads_ref, w_ref, arrived, *state = rest
    get, put = Copies(get), Copies(put)
    state = State(state, put, far_state)
    attn = state.o.shape[1]
    hidden = state.gl.shape[1]
    width = attn + 2 * hidden
    copy = pltpu.make_async_copy(far_ref.at[:, width:], small_ref, arrived.at[2])
    copy.start()
    slab = Slab(far_ref.at[:, :attn], far_ref.at[:, attn:width], heads_ref, w_ref, arrived)
    get.start(far_table_ref, table_ref)
    get.start(far_mask_ref, mask_ref)
    copy.wait()
    small = jnp.transpose(small_ref[...].astype(F32))
    at = 6 * layers
    biases = small[at : at + 4 * layers].astype(BF)
    bias_qkv = dot(biases[:layers], one_hot(place_ref, 0, attn), (1, 1)) + dot(
        biases[layers : 2 * layers], one_hot(place_ref, 1, attn), (1, 1)
    )
    bias_up = dot(biases[2 * layers : 3 * layers], one_hot(place_ref, 2, hidden), (1, 1)) + dot(
        biases[3 * layers :], one_hot(place_ref, 3, hidden), (1, 1)
    )
    for layer in range(layers):
        rows = small[6 * layer : 6 * layer + 6]
        vec_ref[layer, GAIN_A : SHIFT_B + 1, :] = rows[2:]
        vec_ref[layer, BIAS_QKV : BIAS_QKV + 1, :] = bias_qkv[layer : layer + 1]
        vec_ref[layer, BIAS_UP : BIAS_UP + 1, :hidden] = bias_up[layer : layer + 1]
        vec_ref[layer, BIAS_OUT : BIAS_OUT + 1, :] = rows[0:1] + rows[1:2]
        vec_ref[layer, BIAS_OUT + 1 : VECTORS, :] = rows[0:1]

    for quarter, ref in enumerate(inputs):

        def enter(at, _, ref=ref, begin=quarter * ref.shape[0]):
            normed, inv_std = row_norm(ref[at, :].astype(F32))
            state.normed[moved(at, begin), :] = normed
            state.inv_std[moved(at, begin), :] = inv_std

        over_rows(ref.shape[0], enter)
    forward(state, vec_ref.at[0], slab, get, table_ref, mask_ref, parts, wide_ref)
    for ref, far_part_ref in zip(parts, far_parts, strict=True):
        put.start(ref, far_part_ref)
    put.wait()


def summed_rows(parts, at, there):
    mine, near = parts
    return mine[at, :].astype(F32) + near[there, :].astype(F32)


def moved(at, by):
    return pl.ds(pl.multiple_of(at.start + by, CHUNK), CHUNK)


def over_totals(parts, other_ref, inputs, take):
    own = parts[0].shape[0] // 2

    def own_core(at, _):
        take(at, summed_rows(parts, at, moved(at, own)), inputs[0][at, :])

    def near_own_core(at, _):
        total = summed_rows(parts, moved(at, own), at)
        take(moved(at, 2 * own), total, inputs[2][at, :])

    def other(at, _):
        take(moved(at, own), other_ref[at, :].astype(F32), inputs[1][at, :])

    def near_other(at, _):
        total = other_ref[moved(at, own), :].astype(F32)
        take(moved(at, 3 * own), total, inputs[3][at, :])

    for step in (own_core, near_own_core, other, near_other):
        over_rows(own, step)


def last_kernel(owners, *refs):
    inputs, far_ends, parts, refs = refs[:4], refs[4:8], refs[8:10], refs[10:]
    other_ref, vec_ref, far_ref, far_table_ref, far_mask_ref, *rest = refs
    far_parts, rest = rest[:4], rest[4:]
    slab_ref, sums_ref, far_hidden_ref, far_normed_ref, far_inv_std_ref, *rest = rest
    (table_ref, mask_ref, hidden_ref, get, put), rest = rest[:5], rest[5:]
    ahead, back, rest = rest[:2], rest[2:4], rest[4:]
    get, put = Copies(get), Copies(put)
    state, rest = State(rest[:10], put, (far_normed_ref, far_inv_std_ref)), rest[10:]
    grad_ref, heads_ref, w_ref, arrived, *scratch = rest
    attn, width = heads_ref.shape[1], heads_ref.shape[1] + w_ref.shape[1]
    slab = Slab(far_ref.at[:, :attn], far_ref.at[:, attn:width], heads_ref, w_ref, arrived)
    get.start(far_table_ref, table_ref)
    get.start(far_mask_ref, mask_ref)
    own = hidden_ref.shape[0]
    for quarter, ref in enumerate(far_ends):
        get.start(ref, grad_ref.at[quarter * own : (quarter + 1) * own, :])
    bias = vec_ref[0, BIAS_OUT : BIAS_OUT + 1, :]

    def enter(at, total, tokens):
        values = tokens.astype(F32) + total + bias
        scratch[3][at, :] = values
        normed, inv_std = row_norm(values)
        state.normed[at, :] = normed
        state.inv_std[at, :] = inv_std

    over_totals(parts, other_ref, inputs, enter)
    hidden_ref[...] = scratch[3][:own, :] + vec_ref[1, BIAS_OUT : BIAS_OUT + 1, :]
    put.start(hidden_ref, far_hidden_ref)
    forward(state, vec_ref.at[1], slab, get, table_ref, mask_ref, ahead, scratch[3])
    for ref, far_part_ref in zip(ahead, far_parts[:2], strict=True):
        put.start(ref, far_part_ref)
    slab.give(put, slab_ref)
    backward(owners, state, grad_ref, vec_ref.at[1], slab, table_ref, back, sums_ref, scratch, put, far_parts[2:])
    put.wait()


def back_kernel(layers, owners, *refs):
    inputs, parts, refs = refs[:4], refs[4:6], refs[6:]
    other_ref, normed_ref, inv_std_ref, later_ref, vec_ref, far_ref, place_ref, far_table_ref, *rest = refs
    far_state, rest = rest[:10], rest[10:]
    far_back, (slab_ref, kept_ref, table_ref, get, put, *rest) = rest[:2], rest[2:]
    back, state, rest = rest[:2], State(rest[2:12]), rest[12:]
    sums_ref, below_ref, small_ref, heads_ref, w_ref, arrived, *scratch = rest
    get, put = Copies(get), Copies(put)
    attn, width = heads_ref.shape[1], heads_ref.shape[1] + w_ref.shape[1]
    slab = Slab(far_ref.at[:, :attn], far_ref.at[:, attn:width], heads_ref, w_ref, arrived)
    get.start(far_table_ref, table_ref)
    for name, ref in zip(State.names, far_state, strict=True):
        get.start(ref, getattr(state, name))
    attn, hidden = state.o.shape[1], state.gl.shape[1]

    def enter(at, total, cotangent):
        grad = row_norm_back(total, normed_ref[at, :], inv_std_ref[at, :])
        below_ref[at, :] = grad + cotangent.astype(F32)

    over_totals(parts, other_ref, inputs, enter)
    kept_ref[...] = below_ref[: kept_ref.shape[0], :]
    slab.wait()
    get.wait()
    slab.give(put, slab_ref)
    backward(owners, state, below_ref, vec_ref.at[0], slab, table_ref, back, sums_ref, scratch, put, far_back)
    both = [sums_ref, later_ref]
    pad = jnp.zeros((8 - layers, attn), F32)
    qkv = jnp.concatenate([ref[SUM_QKV : SUM_QKV + 1, :] for ref in both] + [pad], axis=0)
    up = [ref[SUM_UP : SUM_UP + 1, :hidden] for ref in both] + [pad[:, :hidden]]
    up = jnp.concatenate(up, axis=0)
    spread = [
        dot(values.astype(BF), one_hot(place_ref, at, values.shape[1]))[:layers]
        for values, at in ((qkv, 0), (qkv, 1), (up, 2), (up, 3))
    ]
    small = [ref[: SUM_SHIFT_B + 1, :] for ref in both] + spread
    used = 9 * layers
    small = jnp.concatenate(small + [jnp.zeros((LANES - used, attn), F32)], axis=0)
    small_ref[...] = pairs_together(jnp.transpose(small), owners).astype(BF)
    copy = pltpu.make_async_copy(small_ref, slab_ref.at[:, width:], arrived.at[2])
    copy.start()
    copy.wait()
    put.wait()


def slabs_kernel(layers, core_ref, place_ref, *refs):
    far, (send_ref, own_ref, near_ref), refs = refs[:9], refs[9:12], refs[12:]
    local, (rows_ref, bias_ref, arrived) = refs[:9], refs[9:]
    copies = [
        pltpu.make_async_copy(src, dst, arrived.at[i])
        for i, (src, dst) in enumerate(zip(far, local, strict=True))
    ]
    for copy in copies:
        copy.start()
    for copy in copies:
        copy.wait()
    (qkv_ref, out_ref, up_ref, down_ref), vectors, biases = local[:4], local[4:7], local[7:9]
    depth, width_out = qkv_ref.shape[1], out_ref.shape[2] // 2
    hidden = up_ref.shape[2] // 4
    low = core_ref[0] == 0

    def half(values):
        width = values.shape[1] // 2
        return jnp.where(low, values[:, :width], values[:, width:])

    rows_ref[...] = jnp.zeros_like(rows_ref)
    at = 0
    for layer in range(layers):
        for ref in vectors:
            rows_ref[at : at + 2, :depth] = ref[layer].astype(F32)
            at += 2
    lanes = lax.broadcasted_iota(jnp.int32, bias_ref.shape, 1)
    for ref in biases:
        bias_ref[...] = jnp.zeros_like(bias_ref)
        bias_ref[:layers, : ref.shape[1]] = ref[...].astype(F32)
        for values in (bias_ref[...], pltpu.roll(bias_ref[...], LANES - depth, 1)):
            rows_ref[at : at + layers, :] = jnp.where(lanes < depth, values, 0.0)[:layers]
            at += layers
    small = jnp.transpose(rows_ref[...])[:depth].astype(BF)
    heads, wide = [], ([], [])
    for layer in range(layers):
        qkv, out = half(qkv_ref[layer]), half(out_ref[layer])
        up, down = half(up_ref[layer]), half(down_ref[layer])
        attn = []
        for head in range(width_out // HS):
            at = head * 3 * HS
            attn += [qkv[:, at : at + 3 * HS], out[:, head * HS : (head + 1) * HS]]
        heads.append(jnp.concatenate(attn, axis=1))
        for z in (0, 1):
            at = slice(z * hidden, (z + 1) * hidden)
            wide[z].append(jnp.concatenate([up[:, at], down[:, at]], axis=1))
    for z in (0, 1):
        block = jnp.concatenate([heads[0], wide[z][0], small], axis=1)
        for owner in range(send_ref.shape[0]):
            if owner // NEAR % 2 == z:
                send_ref[owner] = block
    first = place_ref[0] == 0
    own_ref[...] = jnp.concatenate([heads[1], jnp.where(first, *wide_of(wide, 0, 1))], axis=1)
    near_ref[...] = jnp.concatenate([heads[1], jnp.where(first, *wide_of(wide, 1, 0))], axis=1)


def wide_of(wide, *at):
    return [wide[z][1] for z in at]


def sum_of(got_ref, columns):
    total = got_ref[0, :, columns].astype(F32)
    for sender in range(1, got_ref.shape[0]):
        total = total + got_ref[sender, :, columns].astype(F32)
    return total


def put_sums(place_ref, got_ref, own_ref, near_ref):
    depth = own_ref.shape[0]
    step = 3 * LANES
    for begin in range(0, own_ref.shape[1], step):
        at = slice(begin, begin + step)
        total = sum_of(got_ref, at)
        low, high = total[:depth], total[depth:]
        own_ref[:, at] = jnp.where(place_ref[0] == 0, low, high).astype(BF)
        near_ref[:, at] = jnp.where(place_ref[0] == 0, high, low).astype(BF)


def total_of(refs):
    mine, near = refs
    return mine[...].astype(F32) + near[...].astype(F32)


def gather_late_kernel(place_ref, got_ref, own_ref, near_ref):
    put_sums(place_ref, got_ref, own_ref, near_ref)


def gather_kernel(place_ref, got_ref, own_ref, near_ref, pad_ref):
    depth, width = own_ref.shape[0], own_ref.shape[1] - LANES
    put_sums(place_ref, got_ref, own_ref.at[:, :width], near_ref.at[:, :width])
    pad_ref[...] = jnp.zeros_like(pad_ref)
    pad_ref[: 2 * depth, :] = sum_of(got_ref, slice(width, width + LANES))
    low = jnp.transpose(pad_ref[...])[:depth]
    high = pltpu.roll(low, LANES - depth, 1)
    own_ref[:, width:] = jnp.where(place_ref[0] == 0, low, high).astype(BF)
    near_ref[:, width:] = jnp.where(place_ref[0] == 0, high, low).astype(BF)


def finish_kernel(layers, core_ref, place_ref, *rest):
    groups, rest = (rest[:4], rest[4:8]), rest[8:]
    parts, (below_ref, far_normed_ref, far_inv_std_ref, *rest) = rest[:2], rest[2:]
    hidden_ref, *rest = rest
    result_ref, grad_ref, qkv_ref, out_ref, up_ref, down_ref, *biases = rest[:8]
    normed_ref, inv_std_ref, get = rest[8:]
    get = Copies(get)
    own = pl.ds(0, normed_ref.shape[0])
    get.start(far_normed_ref.at[own, :], normed_ref)
    get.start(far_inv_std_ref.at[own, :], inv_std_ref)
    width_qkv, width_out, width_up = (r.shape[2] // 2 for r in (qkv_ref, out_ref, up_ref))
    depth, heads = qkv_ref.shape[1], width_out // HS
    attn = heads * HEAD
    low, first = core_ref[0] == 0, place_ref[0] == 0

    def both_places(own, near):
        return jnp.where(first, own, near), jnp.where(first, near, own)

    hidden = width_up // 2
    for layer, group in enumerate(groups):
        mine, core, near, core_near = (ref[:, : attn + width_up].astype(F32) for ref in group)
        attention = (mine[:, :attn] + near[:, :attn], core[:, :attn] + core_near[:, :attn])
        sides = (jnp.where(low, *attention), jnp.where(low, *attention[::-1]))
        starts = [(values, head * HEAD) for values in sides for head in range(heads)]
        qkv_ref[layer] = jnp.concatenate([v[:, at : at + 3 * HS] for v, at in starts], axis=1)
        out_ref[layer] = jnp.concatenate([v[:, at + 3 * HS : at + HEAD] for v, at in starts], axis=1)
        for z, (ours, theirs) in enumerate(
            zip(both_places(mine, near), both_places(core, core_near), strict=True)
        ):
            for side, values in enumerate((jnp.where(low, ours, theirs), jnp.where(low, theirs, ours))):
                at = side * width_up + z * hidden
                up_ref[layer, :, at : at + hidden] = values[:, attn : attn + hidden]
                down_ref[layer, :, at : at + hidden] = values[:, attn + hidden : attn + 2 * hidden]
    rows = small_sum([ref[:, attn + width_up :] for ref in groups[0]])
    at = 5 * layers
    for ref in biases:
        low_rows, high_rows = rows[at : at + layers], rows[at + layers : at + 2 * layers]
        lanes = lax.broadcasted_iota(jnp.int32, low_rows.shape, 1)
        both = jnp.where(lanes < depth, low_rows, pltpu.roll(high_rows, depth, 1))
        ref[...] = both[:, : ref.shape[1]]
        at += 2 * layers
    totals = total_of(parts)
    count = hidden_ref.shape[0]
    result_ref[...] = (hidden_ref[...] + totals[:count]).astype(BF)
    get.wait()
    total = row_norm_back(totals[count:], normed_ref[...], inv_std_ref[...])
    grad_ref[...] = (below_ref[...] + total).astype(BF)


def small_sum(parts):
    mine, core, near, core_near = (part.astype(F32) for part in parts)
    return (mine + near) + (core + core_near)


def vectors_kernel(layers, mine_ref, half_ref, bias_out_ref, gain_ref, shift_ref):
    vectors = mine_ref[...] + half_ref[...]
    depth = gain_ref.shape[2]
    for layer in range(layers):
        rows = vectors[5 * layer : 5 * layer + 5, :depth]
        bias_out_ref[layer, 0:1, :] = rows[:1]
        bias_out_ref[layer, 1:2, :] = rows[:1]
        gain_ref[layer] = rows[1:3]
        shift_ref[layer] = rows[3:5]


def call(kernel, outs, scratch, flops, *args, far=(), far_outs=(), limit=VMEM_BYTES, **more):
    def space(at, arg, far):
        if at in far:
            return pltpu.HBM
        return pltpu.SMEM if arg.shape == (1,) else pltpu.VMEM

    return pl.pallas_call(
        kernel,
        out_shape=outs,
        in_specs=[pl.BlockSpec(memory_space=space(at, arg, far)) for at, arg in enumerate(args)],
        out_specs=[
            pl.BlockSpec(memory_space=space(at, out, far_outs)) for at, out in enumerate(outs)
        ],
        scratch_shapes=scratch,
        compiler_params=pltpu.CompilerParams(vmem_limit_bytes=limit),
        cost_estimate=pl.CostEstimate(flops=flops, bytes_accessed=8_000_000, transcendentals=0),
        **more,
    )(*args)


def core_rows_summed(kept, sent):
    return (kept.astype(F32) + other_core(sent).astype(F32)).astype(BF)


def turned_groups(values):
    return values.reshape(2, -1, values.shape[1])[::-1].reshape(values.shape)


def pair_sum(mine):
    theirs = turned_groups(near_other_half(mine))
    return (mine.astype(F32) + theirs.astype(F32)).astype(BF)


def other_rows(mine, near):
    return other_core((mine.astype(F32) + turned_groups(near).astype(F32)).astype(BF))


def own_parts(*mines):
    count = mines[0].shape[0] // 2
    own = jnp.concatenate([mine[:count] for mine in mines])
    return own, near_group(jnp.concatenate([mine[count:] for mine in mines]))


def rotation(positions):
    exponents = jnp.arange(ROT // 2, dtype=F32) * (2.0 / ROT)
    inverse = jnp.power(10000.0, -exponents)
    phase = positions.astype(F32)[:, None] * inverse[None, :]
    cos, sin = jnp.cos(phase), jnp.sin(phase)
    none = jnp.zeros_like(sin)
    rest = jnp.zeros((positions.shape[0], HS - ROT), F32)
    tables = [[cos, cos, rest + 1.0], [-sin, none, rest], [none, sin, rest]]
    return jnp.stack([jnp.concatenate(t + t, axis=1) for t in tables])


def bias_places(owners, depth, starts, widths, shards):
    owner = jnp.arange(owners * depth, dtype=jnp.int32) // depth
    inner = jnp.arange(owners * depth, dtype=jnp.int32) % depth
    rows = []
    for start, width, shard, head in zip(starts, widths, shards, (3 * HS, None), strict=True):
        for first in (0, depth):
            at = owner * shard + inner + first - start
            fits = (inner + first < shard) & (at >= 0) & (at < width)
            if head is not None:
                at = at // head * HEAD + at % head
            rows.append(jnp.where(fits, at, -1))
    return jnp.stack(rows + rows)


def per_device(
    tokens,
    cotangent,
    doc_lens,
    block_pos,
    w_qkv,
    w_out,
    w_up,
    w_down,
    b_qkv,
    b_up,
    out_bias,
    norm_gain,
    norm_bias,
):
    row_count = tokens.shape[0]
    block_rows = row_count // 2
    core = lax.axis_index("ctx")
    owners = lax.axis_size("fsdp")
    layers, depth, width_qkv = w_qkv.shape
    width_qkv, width_out, hidden = width_qkv // 2, w_out.shape[1] // 2, w_up.shape[2] // 4
    place_z = lax.axis_index("fsdp") // NEAR % 2
    heads = width_out // HS
    attn = heads * HEAD
    width = attn + 2 * hidden
    wide = owners * depth
    rows = 4 * row_count

    core_at = core.astype(jnp.int32).reshape(1)
    place_at = place_z.astype(jnp.int32).reshape(1)
    sds = jax.ShapeDtypeStruct
    raw = (
        w_qkv,
        w_out.transpose(0, 2, 1),
        w_up,
        w_down.transpose(0, 2, 1),
        out_bias,
        norm_gain,
        norm_bias,
        b_qkv,
        b_up,
    )
    send, own_block, near_block = call(
        functools.partial(slabs_kernel, layers),
        (
            sds((owners, depth, width + LANES), BF),
            sds((depth, width), BF),
            sds((depth, width), BF),
        ),
        [pltpu.VMEM(a.shape, a.dtype) for a in raw]
        + [pltpu.VMEM((LANES, LANES), F32), pltpu.VMEM((8, LANES), F32)]
        + [pltpu.SemaphoreType.DMA((len(raw),))],
        1000,
        core_at,
        place_at,
        *raw,
        far=range(2, 2 + len(raw)),
    )
    starts, ends = ((own, near_other_half(own)) for own in (tokens, cotangent))
    starts, ends = ((o, other_core(o), n, other_core(n)) for o, n in (starts, ends))
    first = exchanged(send).reshape(wide, -1)
    pair = [own_block, near_group(near_block)]
    pair = jnp.where(place_z == 0, jnp.concatenate(pair), jnp.concatenate(pair[::-1]))
    pair, starts, ends = lax.optimization_barrier((pair, starts, ends))
    second = jnp.broadcast_to(pair[None], (owners // 2, *pair.shape))
    second = owners_in_order(exchanged_in_plane(second), owners)
    offsets = jnp.arange(block_rows, dtype=jnp.int32)
    positions = (block_pos[0][:, None] * block_rows + offsets[None, :]).reshape(2, row_count)
    positions = jnp.where(core == 0, positions, positions[::-1]).reshape(-1)
    doc_ends = jnp.cumsum(doc_lens[0])
    docs = jnp.sum((positions[:, None] >= doc_ends[None, :]).astype(jnp.int32), axis=1)
    allowed = (docs[:, None] == docs[None, :]) & (positions[None, :] <= positions[:, None])
    mask = jnp.where(allowed, 0.0, MASKED).astype(F32)
    table = rotation(positions)
    place = bias_places(
        owners,
        depth,
        (core * width_qkv, (2 * core + place_z) * hidden),
        (width_qkv, hidden),
        (b_qkv.shape[1], b_up.shape[1]),
    )

    flops = 2 * rows * wide * width
    part = sds((rows // 2, wide), BF)
    kept = State.shapes(rows, wide, heads, hidden)

    def vmem(*arrays):
        return [pltpu.VMEM(array.shape, array.dtype) for array in arrays]

    def copies(*counts):
        return [pltpu.SemaphoreType.DMA((count,)) for count in counts]

    slab_scratch = [
        pltpu.VMEM((wide, attn), BF),
        pltpu.VMEM((wide, 2 * hidden), BF),
        pltpu.SemaphoreType.DMA((3,)),
    ]
    kept_part, sent_part, vec, *state = call(
        functools.partial(first_kernel, layers),
        (part, part, sds((layers, VECTORS, wide), F32), *State.shapes(rows, wide, heads, hidden)),
        [
            *vmem(part, part, table, mask),
            *copies(2, 12),
            pltpu.VMEM((rows, wide), F32),
            pltpu.VMEM((wide, LANES), BF),
            *slab_scratch,
            *vmem(*kept),
        ],
        flops,
        *starts,
        first,
        place,
        table,
        mask,
        far=(4, 6, 7),
        far_outs=(0, 1, *range(3, 13)),
    )
    mine = pair_sum(core_rows_summed(kept_part, sent_part))
    mine, near, second = lax.optimization_barrier((mine, near_group(mine), second))
    scratch = [
        pltpu.VMEM((rows, wide), BF),
        pltpu.VMEM((rows, hidden), BF),
        pltpu.VMEM((rows // 2, attn), BF),
        pltpu.VMEM((rows, wide), F32),
        pltpu.VMEM((rows, wide), F32),
    ]
    *sums, slab, later_sums, result, normed, inv_std = call(
        functools.partial(last_kernel, owners),
        (
            *(part,) * 4,
            sds((wide, width), BF),
            sds((8, wide), F32),
            sds((row_count, wide), F32),
            *kept[:2],
        ),
        [
            *vmem(table, mask, sds((row_count, wide), F32)),
            *copies(6, 10),
            *vmem(part, part, part, part, *kept, sds((rows, wide), BF)),
            *slab_scratch,
            *scratch,
        ],
        3 * flops,
        *starts,
        *ends,
        mine,
        near,
        other_rows(mine, near),
        vec,
        second,
        table,
        mask,
        far=(4, 5, 6, 7, 12, 13, 14),
        far_outs=(0, 1, 2, 3, 4, 6, 7, 8),
    )
    mine, slab = lax.optimization_barrier((core_rows_summed(*sums[2:]), slab))
    later = exchanged_in_plane(slab.reshape(owners // 2, -1, width))
    ahead, mine = lax.optimization_barrier((sums[:2], pair_sum(mine)))
    near = near_group(mine)
    ahead = pair_sum(core_rows_summed(*ahead))
    kept_part, sent_part, slab, grad_below = call(
        functools.partial(back_kernel, layers, owners),
        (part, part, sds((wide, width + LANES), BF), sds((row_count, wide), F32)),
        [
            *vmem(table),
            *copies(11, 5),
            *vmem(part, part, *kept, later_sums, sds((rows, wide), F32)),
            *vmem(sds((wide, LANES), BF)),
            *slab_scratch,
            *scratch,
        ],
        2 * flops,
        *ends,
        mine,
        near,
        other_rows(mine, near),
        normed,
        inv_std,
        later_sums,
        vec,
        first,
        place,
        table,
        *state,
        far=(11, *range(13, 24)),
        far_outs=(0, 1, 2),
    )
    slab, later, ahead = lax.optimization_barrier((slab, later, ahead))
    earlier = exchanged_in_plane(slab.reshape(owners // 2, -1, width + LANES))
    below = pair_sum(core_rows_summed(kept_part, sent_part))

    piece = sds((depth, width), BF)
    late = call(gather_late_kernel, (piece, piece), [], flops // 8, place_at, later)
    ends = own_parts(ahead, below)

    def of_all(own, near):
        return own, other_core(own), near_group(near), near_other_core(near)

    late = of_all(*late)
    earlier, late, ends = lax.optimization_barrier((earlier, late, ends))
    piece = sds((depth, width + LANES), BF)
    early = of_all(
        *call(
            gather_kernel, (piece, piece), [pltpu.VMEM((LANES, LANES), F32)], 1000, place_at, earlier
        )
    )
    small = small_sum([part[:, width:] for part in early])
    half = other_half(small)
    result, grad_tokens, grad_qkv, grad_out, grad_up, grad_down, grad_b_qkv, grad_b_up = call(
        functools.partial(finish_kernel, layers),
        (sds(tokens.shape, BF),) * 2
        + tuple(
            sds(shape, F32)
            for shape in (
                w_qkv.shape,
                (layers, depth, w_out.shape[1]),
                w_up.shape,
                (layers, depth, w_down.shape[1]),
                b_qkv.shape,
                b_up.shape,
            )
        ),
        [*vmem(sds((row_count, wide), F32), sds((row_count, 1), F32)), *copies(2)],
        flops // 8,
        core_at,
        place_at,
        *early,
        *late,
        *ends,
        grad_below,
        state[0],
        state[1],
        result,
        far=(13, 14),
    )
    vectors = call(
        functools.partial(vectors_kernel, layers),
        tuple(sds(a.shape, F32) for a in (out_bias, norm_gain, norm_bias)),
        [],
        1000,
        small,
        half,
    )
    return (
        result,
        grad_tokens,
        grad_qkv,
        grad_out.transpose(0, 2, 1),
        grad_up,
        grad_down.transpose(0, 2, 1),
        grad_b_qkv,
        grad_b_up,
        *vectors,
    )


def solution(mesh):
    in_specs = (
        P(("fsdp", "ctx"), None),
        P(("fsdp", "ctx"), None),
        P("fsdp", None),
        P("fsdp", None),
        P(None, "fsdp", "tp"),
        P(None, "tp", "fsdp"),
        P(None, "fsdp", "tp"),
        P(None, "tp", "fsdp"),
        P(None, ("tp", "fsdp")),
        P(None, ("tp", "fsdp")),
        P(None, None, "fsdp"),
        P(None, None, "fsdp"),
        P(None, None, "fsdp"),
    )
    out_specs = (P(("fsdp", "ctx"), None), P(("fsdp", "ctx"), None), *in_specs[4:])
    return jax.shard_map(
        per_device, mesh=mesh, in_specs=in_specs, out_specs=out_specs, check_vma=False
    )
```

```python
import functools

import jax
import jax.numpy as jnp
from jax import lax
from jax.experimental import pallas as pl
from jax.experimental.pallas import tpu as pltpu
from jax.sharding import PartitionSpec as P

HS = 64
ROT = 16
EPSILON = 1e-05
MASKED = -1e30
F32 = jnp.float32
BF = jnp.bfloat16
SWAP = [(0, 1), (1, 0)]
NEAR = 4
LANES = 128
CHUNK = 128
HEAD = 4 * HS
SCALE = HS ** (-0.5)
VMEM_BYTES = 62 * 1024 * 1024
GAIN_A, GAIN_B, SHIFT_A, SHIFT_B, BIAS_QKV, BIAS_UP, BIAS_OUT = range(7)
VECTORS = 8
SUM_OUT, SUM_GAIN_A, SUM_GAIN_B, SUM_SHIFT_A, SUM_SHIFT_B, SUM_QKV, SUM_UP = range(7)


def other_core(values):
    return lax.ppermute(values, "ctx", SWAP)


def other_half(values):
    return lax.ppermute(values, "tp", SWAP)


def other_core_and_half(values):
    return lax.ppermute(values, ("ctx", "tp"), [(0, 3), (1, 2), (2, 1), (3, 0)])


def near_group(values):
    owners = lax.axis_size("fsdp")
    return lax.ppermute(values, "fsdp", [(f, f ^ NEAR) for f in range(owners)])


def near_other_half(values):
    owners = lax.axis_size("fsdp")
    pairs = [(2 * f + t, 2 * (f ^ NEAR) + 1 - t) for f in range(owners) for t in (0, 1)]
    return lax.ppermute(values, ("fsdp", "tp"), pairs)


def near_other_core(values):
    owners = lax.axis_size("fsdp")
    pairs = [(2 * f + c, 2 * (f ^ NEAR) + 1 - c) for f in range(owners) for c in (0, 1)]
    return lax.ppermute(values, ("fsdp", "ctx"), pairs)


def exchanged(blocks):
    return lax.all_to_all(blocks, "fsdp", 0, 0, tiled=True)


def exchanged_in_plane(blocks):
    owners = lax.axis_size("fsdp")
    planes = [[f for f in range(owners) if f // NEAR % 2 == z] for z in (0, 1)]
    return lax.all_to_all(blocks, "fsdp", 0, 0, axis_index_groups=planes, tiled=True)


def pairs_together(values, owners):
    depth = values.shape[0] // owners
    pairs = [y * 2 * NEAR + x for y in range(owners // (2 * NEAR)) for x in range(NEAR)]
    order = [first + z * NEAR for first in pairs for z in (0, 1)]
    return jnp.concatenate([values[owner * depth : (owner + 1) * depth] for owner in order])


def owners_in_order(blocks, owners):
    width = blocks.shape[2]
    blocks = blocks.reshape(owners // (2 * NEAR), NEAR, 2, -1, width)
    return blocks.transpose(0, 2, 1, 3, 4).reshape(-1, width)


def dot(left, right, along=(1, 0)):
    dims = (((along[0],), (along[1],)), ((), ()))
    return lax.dot_general(left, right, dims, preferred_element_type=F32)


def over_rows(rows, step, carry=None, start=0):
    def body(at, kept):
        return step(pl.ds(pl.multiple_of(at * CHUNK, CHUNK), CHUNK), kept)

    return lax.fori_loop(start // CHUNK, rows // CHUNK, body, carry, unroll=True)


def by_eights(values):
    return values.reshape(-1, 8, values.shape[-1]).sum(axis=0)


def whole_sum(eights):
    return jnp.sum(eights, axis=0, keepdims=True)


def turned(tile, cos, left, right):
    return (
        tile * cos
        + pltpu.roll(tile, LANES - ROT // 2, 1) * left
        + pltpu.roll(tile, ROT // 2, 1) * right
    )


def row_norm(values):
    centered = values - jnp.mean(values, axis=-1, keepdims=True)
    inv_std = lax.rsqrt(jnp.mean(centered * centered, axis=-1, keepdims=True) + EPSILON)
    return centered * inv_std, inv_std


def row_norm_back(total, normed, inv_std):
    return inv_std * (
        total
        - jnp.mean(total, axis=-1, keepdims=True)
        - normed * jnp.mean(total * normed, axis=-1, keepdims=True)
    )


def one_hot(place_ref, at, width):
    rows = lax.broadcasted_iota(jnp.int32, (width, place_ref.shape[1]), 0)
    return (rows == place_ref[at : at + 1, :]).astype(F32).astype(BF)


class Slab:
    def __init__(self, far_heads_ref, far_ref, heads_ref, w_ref, arrived):
        self.heads_ref, self.w_ref = heads_ref, w_ref
        self.copies = [
            pltpu.make_async_copy(far_heads_ref, heads_ref, arrived.at[0]),
            pltpu.make_async_copy(far_ref, w_ref, arrived.at[1]),
        ]
        for copy in self.copies:
            copy.start()

    def wait(self):
        for copy in self.copies:
            copy.wait()
        return self.heads_ref, self.w_ref

    def give(self, put, far_ref):
        attn, hidden = self.heads_ref.shape[1], self.w_ref.shape[1] // 2
        self.put = put
        self.pieces = [
            (self.heads_ref, far_ref.at[:, :attn]),
            (self.w_ref.at[:, :hidden], far_ref.at[:, attn : attn + hidden]),
            (self.w_ref.at[:, hidden:], far_ref.at[:, attn + hidden : attn + 2 * hidden]),
        ]

    def sent(self, piece):
        self.put.start(*self.pieces[piece])


class Copies:
    def __init__(self, semaphores):
        self.semaphores, self.started = semaphores, []

    def start(self, src, dst):
        copy = pltpu.make_async_copy(src, dst, self.semaphores.at[len(self.started)])
        copy.start()
        self.started.append(copy)

    def wait(self, begin=0, end=None):
        for copy in self.started[begin:end]:
            copy.wait()


class State:
    names = ("normed", "inv_std", "a", "m", "qk", "v", "p", "o", "gl", "slope")

    def __init__(self, refs, copies=None, far=()):
        for name, ref in zip(self.names, refs, strict=True):
            setattr(self, name, ref)
        self.copies, self.far = copies, dict(zip(self.names, far))

    def ready(self, *names):
        for name in names:
            if name in self.far:
                self.copies.start(getattr(self, name), self.far[name])

    @staticmethod
    def shapes(rows, depth, heads, hidden):
        group = rows // 2
        return (
            jax.ShapeDtypeStruct((rows, depth), F32),
            jax.ShapeDtypeStruct((rows, 1), F32),
            jax.ShapeDtypeStruct((group, depth), BF),
            jax.ShapeDtypeStruct((rows, depth), BF),
            jax.ShapeDtypeStruct((group, heads * 2 * HS), BF),
            jax.ShapeDtypeStruct((group, heads * HS), BF),
            jax.ShapeDtypeStruct((heads, group, group), F32),
            jax.ShapeDtypeStruct((group, heads * HEAD), BF),
            jax.ShapeDtypeStruct((rows, hidden), BF),
            jax.ShapeDtypeStruct((rows, hidden), F32),
        )


def places(rows):
    quarter = rows // 4
    return [(0, 0, 0), (quarter, 1, 0), (2 * quarter, 0, quarter), (3 * quarter, 1, quarter)]


def forward(state, vec_ref, slab, near_copies, table_ref, mask_ref, parts, wide_ref):
    rows, depth = state.normed.shape
    group = rows // 2
    heads = state.v.shape[1] // HS
    hidden = state.gl.shape[1]

    def affine_a(at, _):
        state.a[at, :] = (
            state.normed[at, :] * vec_ref[GAIN_A : GAIN_A + 1, :]
            + vec_ref[SHIFT_A : SHIFT_A + 1, :]
        ).astype(BF)

    def affine_b(at, _):
        state.m[at, :] = (
            state.normed[at, :] * vec_ref[GAIN_B : GAIN_B + 1, :]
            + vec_ref[SHIFT_B : SHIFT_B + 1, :]
        ).astype(BF)

    state.ready("normed", "inv_std")
    over_rows(group, affine_a)
    over_rows(rows, affine_b)
    state.ready("a", "m")
    heads_ref, w_ref = slab.wait()
    near_copies.wait()
    wide_ref[:group, :] = dot(state.a[...], heads_ref[...])
    state.o[...] = jnp.zeros_like(state.o)
    for head in range(heads):
        at = head * HEAD
        bias = vec_ref[BIAS_QKV : BIAS_QKV + 1, at : at + HEAD]
        tile = wide_ref[:group, at : at + LANES] + bias[:, :LANES]
        tile = turned(tile, table_ref[0], table_ref[1], table_ref[2]).astype(BF)
        value = wide_ref[:group, at + 2 * HS : at + 3 * HS] + bias[:, 2 * HS : 3 * HS]
        value = value.astype(BF)
        state.qk[:, head * LANES : (head + 1) * LANES] = tile
        state.v[:, head * HS : (head + 1) * HS] = value
        half = group // 2
        for top in (0, half):
            scores = dot(tile[top : top + half, :HS], tile[:, HS:], (1, 1))
            scores = scores * SCALE + mask_ref[top : top + half, :]
            exponent = jnp.exp(scores - jnp.max(scores, axis=1, keepdims=True))
            share = exponent * (1.0 / jnp.sum(exponent, axis=1, keepdims=True))
            state.p[head, top : top + half, :] = share
            state.o[top : top + half, at + 3 * HS : at + HEAD] = dot(
                share.astype(BF), value
            ).astype(BF)
    state.ready("qk", "v", "p", "o")
    wide_ref[:, :hidden] = dot(state.m[...], w_ref[:, :hidden])

    def gelu(at, _):
        up = wide_ref[at, :hidden] + vec_ref[BIAS_UP : BIAS_UP + 1, :hidden]
        below = 0.5 + 0.5 * lax.erf(up * (0.5**0.5))
        state.gl[at, :] = (up * below).astype(BF)
        state.slope[at, :] = below + up * (jnp.exp(-0.5 * up * up) * 0.3989422804014327)

    over_rows(rows, gelu)
    state.ready("gl", "slope")
    down = w_ref[:, hidden : 2 * hidden]
    part = dot(state.o[...], heads_ref[...], (1, 1))
    half = group // 2
    part = (part + dot(state.gl[:group, :], down, (1, 1))).astype(BF)
    near = dot(state.gl[group:, :], down, (1, 1)).astype(BF)
    for core, part_ref in enumerate(parts):
        at = core * half
        part_ref[:half, :] = part[at : at + half]
        part_ref[half:, :] = near[at : at + half]


def backward(
    owners, state, grad_ref, vec_ref, slab, table_ref, parts, sums_ref, scratch, put, far_parts
):
    low_ref, up_ref, qkv_ref, wide_ref, deep_ref = scratch
    heads_ref, w_ref = slab.heads_ref, slab.w_ref
    rows, depth = state.normed.shape
    group = rows // 2
    heads = state.v.shape[1] // HS
    attn, hidden = heads * HEAD, state.gl.shape[1]

    def lower(at, total):
        grad = grad_ref[at, :].astype(F32)
        low_ref[at, :] = grad.astype(BF)
        return total + by_eights(grad)

    total = over_rows(rows, lower, jnp.zeros((8, depth), F32))
    sums_ref[SUM_OUT : SUM_OUT + 1, :] = whole_sum(total) * 0.125
    low = low_ref[...]
    wide_ref[:, :hidden] = dot(low, w_ref[:, hidden : 2 * hidden])

    def through_gelu(at, total):
        up = (wide_ref[at, :hidden] * state.slope[at, :]).astype(BF)
        up_ref[at, :] = up
        return total + by_eights(up.astype(F32))

    total = over_rows(rows, through_gelu, jnp.zeros((8, hidden), F32))
    sums_ref[SUM_UP : SUM_UP + 1, :hidden] = whole_sum(total)
    wide_ref[:group, :] = dot(low_ref[:group, :], heads_ref[...])
    for head in range(heads):
        at = head * HEAD
        tile = state.qk[:, head * LANES : (head + 1) * LANES]
        query, key = tile[:, :HS], tile[:, HS:]
        value = state.v[:, head * HS : (head + 1) * HS]
        out = wide_ref[:group, at + 3 * HS : at + HEAD].astype(BF)
        half = group // 2
        grad_value, grad_key, grad_query = 0.0, 0.0, []
        for top in (0, half):
            share = state.p[head, top : top + half, :]
            grad = dot(out[top : top + half], value, (1, 1))
            delta = jnp.sum(share * grad, axis=1, keepdims=True)
            low_scores = (share * (grad - delta)).astype(BF)
            grad_value = grad_value + dot(share.astype(BF), out[top : top + half], (0, 0))
            grad_query.append(dot(low_scores, key))
            grad_key = grad_key + dot(low_scores, query[top : top + half], (0, 0))
        both = jnp.concatenate([jnp.concatenate(grad_query, axis=0), grad_key], axis=1) * SCALE
        both = turned(both, table_ref[0], -table_ref[1], -table_ref[2])
        qkv_ref[:, at : at + LANES] = both.astype(BF)
        qkv_ref[:, at + LANES : at + HEAD] = jnp.concatenate(
            [grad_value, jnp.zeros_like(grad_value)], axis=1
        ).astype(BF)

    def count_qkv(at, total):
        return total + by_eights(qkv_ref[at, :].astype(F32))

    total = over_rows(group, count_qkv, jnp.zeros((8, attn), F32))
    sums_ref[SUM_QKV : SUM_QKV + 1, :] = whole_sum(total)
    wide_ref[:group, :] = dot(qkv_ref[...], heads_ref[...], (1, 1))
    deep_ref[...] = dot(up_ref[...], w_ref[:, :hidden], (1, 1))

    def through_norms(with_first, part_ref, begin, to):
        def step(at, totals):
            there, at = moved(at, to), moved(at, begin)
            second, normed = deep_ref[at, :], state.normed[at, :]
            total, new = second * vec_ref[GAIN_B : GAIN_B + 1, :], (second * normed, second)
            if with_first:
                first = wide_ref[at, :]
                total = total + first * vec_ref[GAIN_A : GAIN_A + 1, :]
                new = (*new, first * normed, first)
            part_ref[there, :] = total.astype(BF)
            return tuple(old + by_eights(term) for old, term in zip(totals, new, strict=True))

        return step

    totals = (jnp.zeros((8, depth), F32),) * 4
    for begin, core, to in places(rows):
        count = 4 if begin < group else 2
        step = through_norms(begin < group, parts[core], begin, to)
        totals = (*over_rows(rows // 4, step, totals[:count]), *totals[count:])
    for row, total in zip((SUM_GAIN_B, SUM_SHIFT_B, SUM_GAIN_A, SUM_SHIFT_A), totals, strict=True):
        sums_ref[row : row + 1, :] = whole_sum(total)
    for ref, far_part_ref in zip(parts, far_parts, strict=True):
        put.start(ref, far_part_ref)
    heads_grad = dot(state.a[...], qkv_ref[...], (0, 0))
    heads_grad = heads_grad + dot(low_ref[:group, :], state.o[...], (0, 0))
    heads_ref[...] = pairs_together(heads_grad, owners).astype(BF)
    slab.sent(0)
    up_grad = dot(state.m[...], up_ref[...], (0, 0))
    w_ref[:, :hidden] = pairs_together(up_grad, owners).astype(BF)
    slab.sent(1)
    down_grad = dot(low, state.gl[...], (0, 0))
    w_ref[:, hidden : 2 * hidden] = pairs_together(down_grad, owners).astype(BF)
    slab.sent(2)


def first_kernel(layers, *refs):
    inputs, (far_ref, place_ref, far_table_ref, far_mask_ref, *rest) = refs[:4], refs[4:]
    far_parts, vec_ref, far_state, rest = rest[:2], rest[2], rest[3:13], rest[13:]
    parts, (table_ref, mask_ref, get, put), rest = rest[:2], rest[2:6], rest[6:]
    wide_ref, small_ref, heads_ref, w_ref, arrived, *state = rest
    get, put = Copies(get), Copies(put)
    state = State(state, put, far_state)
    attn = state.o.shape[1]
    hidden = state.gl.shape[1]
    width = attn + 2 * hidden
    copy = pltpu.make_async_copy(far_ref.at[:, width:], small_ref, arrived.at[2])
    copy.start()
    slab = Slab(far_ref.at[:, :attn], far_ref.at[:, attn:width], heads_ref, w_ref, arrived)
    get.start(far_table_ref, table_ref)
    get.start(far_mask_ref, mask_ref)
    copy.wait()
    small = jnp.transpose(small_ref[...].astype(F32))
    at = 6 * layers
    biases = small[at : at + 4 * layers].astype(BF)
    bias_qkv = dot(biases[:layers], one_hot(place_ref, 0, attn), (1, 1)) + dot(
        biases[layers : 2 * layers], one_hot(place_ref, 1, attn), (1, 1)
    )
    bias_up = dot(biases[2 * layers : 3 * layers], one_hot(place_ref, 2, hidden), (1, 1)) + dot(
        biases[3 * layers :], one_hot(place_ref, 3, hidden), (1, 1)
    )
    for layer in range(layers):
        rows = small[6 * layer : 6 * layer + 6]
        vec_ref[layer, GAIN_A : SHIFT_B + 1, :] = rows[2:]
        vec_ref[layer, BIAS_QKV : BIAS_QKV + 1, :] = bias_qkv[layer : layer + 1]
        vec_ref[layer, BIAS_UP : BIAS_UP + 1, :hidden] = bias_up[layer : layer + 1]
        vec_ref[layer, BIAS_OUT : BIAS_OUT + 1, :] = rows[0:1] + rows[1:2]
        vec_ref[layer, BIAS_OUT + 1 : VECTORS, :] = rows[0:1]

    for quarter, ref in enumerate(inputs):

        def enter(at, _, ref=ref, begin=quarter * ref.shape[0]):
            normed, inv_std = row_norm(ref[at, :].astype(F32))
            state.normed[moved(at, begin), :] = normed
            state.inv_std[moved(at, begin), :] = inv_std

        over_rows(ref.shape[0], enter)
    forward(state, vec_ref.at[0], slab, get, table_ref, mask_ref, parts, wide_ref)
    for ref, far_part_ref in zip(parts, far_parts, strict=True):
        put.start(ref, far_part_ref)
    put.wait()


def summed_rows(parts, at, there):
    mine, near = parts
    return mine[at, :].astype(F32) + near[there, :].astype(F32)


def moved(at, by):
    return pl.ds(pl.multiple_of(at.start + by, CHUNK), CHUNK)


def over_totals(parts, other_ref, inputs, take):
    own = parts[0].shape[0] // 2

    def own_core(at, _):
        take(at, summed_rows(parts, at, moved(at, own)), inputs[0][at, :])

    def near_own_core(at, _):
        total = summed_rows(parts, moved(at, own), at)
        take(moved(at, 2 * own), total, inputs[2][at, :])

    def other(at, _):
        take(moved(at, own), other_ref[at, :].astype(F32), inputs[1][at, :])

    def near_other(at, _):
        total = other_ref[moved(at, own), :].astype(F32)
        take(moved(at, 3 * own), total, inputs[3][at, :])

    for step in (own_core, near_own_core, other, near_other):
        over_rows(own, step)


def last_kernel(owners, *refs):
    inputs, far_ends, parts, refs = refs[:4], refs[4:8], refs[8:10], refs[10:]
    other_ref, vec_ref, far_ref, far_table_ref, far_mask_ref, *rest = refs
    far_parts, rest = rest[:4], rest[4:]
    slab_ref, sums_ref, far_hidden_ref, far_normed_ref, far_inv_std_ref, *rest = rest
    (table_ref, mask_ref, hidden_ref, get, put), rest = rest[:5], rest[5:]
    ahead, back, rest = rest[:2], rest[2:4], rest[4:]
    get, put = Copies(get), Copies(put)
    state, rest = State(rest[:10], put, (far_normed_ref, far_inv_std_ref)), rest[10:]
    grad_ref, heads_ref, w_ref, arrived, *scratch = rest
    attn, width = heads_ref.shape[1], heads_ref.shape[1] + w_ref.shape[1]
    slab = Slab(far_ref.at[:, :attn], far_ref.at[:, attn:width], heads_ref, w_ref, arrived)
    get.start(far_table_ref, table_ref)
    get.start(far_mask_ref, mask_ref)
    own = hidden_ref.shape[0]
    for quarter, ref in enumerate(far_ends):
        get.start(ref, grad_ref.at[quarter * own : (quarter + 1) * own, :])
    bias = vec_ref[0, BIAS_OUT : BIAS_OUT + 1, :]

    def enter(at, total, tokens):
        values = tokens.astype(F32) + total + bias
        scratch[3][at, :] = values
        normed, inv_std = row_norm(values)
        state.normed[at, :] = normed
        state.inv_std[at, :] = inv_std

    over_totals(parts, other_ref, inputs, enter)
    hidden_ref[...] = scratch[3][:own, :] + vec_ref[1, BIAS_OUT : BIAS_OUT + 1, :]
    put.start(hidden_ref, far_hidden_ref)
    forward(state, vec_ref.at[1], slab, get, table_ref, mask_ref, ahead, scratch[3])
    for ref, far_part_ref in zip(ahead, far_parts[:2], strict=True):
        put.start(ref, far_part_ref)
    slab.give(put, slab_ref)
    backward(owners, state, grad_ref, vec_ref.at[1], slab, table_ref, back, sums_ref, scratch, put, far_parts[2:])
    put.wait()


def back_kernel(layers, owners, *refs):
    inputs, parts, refs = refs[:4], refs[4:6], refs[6:]
    other_ref, normed_ref, inv_std_ref, later_ref, vec_ref, far_ref, place_ref, far_table_ref, *rest = refs
    far_state, rest = rest[:10], rest[10:]
    far_back, (slab_ref, kept_ref, table_ref, get, put, *rest) = rest[:2], rest[2:]
    back, state, rest = rest[:2], State(rest[2:12]), rest[12:]
    sums_ref, below_ref, small_ref, heads_ref, w_ref, arrived, *scratch = rest
    get, put = Copies(get), Copies(put)
    attn, width = heads_ref.shape[1], heads_ref.shape[1] + w_ref.shape[1]
    slab = Slab(far_ref.at[:, :attn], far_ref.at[:, attn:width], heads_ref, w_ref, arrived)
    get.start(far_table_ref, table_ref)
    for name, ref in zip(State.names, far_state, strict=True):
        get.start(ref, getattr(state, name))
    attn, hidden = state.o.shape[1], state.gl.shape[1]

    def enter(at, total, cotangent):
        grad = row_norm_back(total, normed_ref[at, :], inv_std_ref[at, :])
        below_ref[at, :] = grad + cotangent.astype(F32)

    over_totals(parts, other_ref, inputs, enter)
    kept_ref[...] = below_ref[: kept_ref.shape[0], :]
    slab.wait()
    get.wait()
    slab.give(put, slab_ref)
    backward(owners, state, below_ref, vec_ref.at[0], slab, table_ref, back, sums_ref, scratch, put, far_back)
    both = [sums_ref, later_ref]
    pad = jnp.zeros((8 - layers, attn), F32)
    qkv = jnp.concatenate([ref[SUM_QKV : SUM_QKV + 1, :] for ref in both] + [pad], axis=0)
    up = [ref[SUM_UP : SUM_UP + 1, :hidden] for ref in both] + [pad[:, :hidden]]
    up = jnp.concatenate(up, axis=0)
    spread = [
        dot(values.astype(BF), one_hot(place_ref, at, values.shape[1]))[:layers]
        for values, at in ((qkv, 0), (qkv, 1), (up, 2), (up, 3))
    ]
    small = [ref[: SUM_SHIFT_B + 1, :] for ref in both] + spread
    used = 9 * layers
    small = jnp.concatenate(small + [jnp.zeros((LANES - used, attn), F32)], axis=0)
    small_ref[...] = pairs_together(jnp.transpose(small), owners).astype(BF)
    copy = pltpu.make_async_copy(small_ref, slab_ref.at[:, width:], arrived.at[2])
    copy.start()
    copy.wait()
    put.wait()


def slabs_kernel(layers, core_ref, place_ref, *refs):
    far, (send_ref, own_ref, near_ref), refs = refs[:9], refs[9:12], refs[12:]
    local, (rows_ref, bias_ref, arrived) = refs[:9], refs[9:]
    copies = [
        pltpu.make_async_copy(src, dst, arrived.at[i])
        for i, (src, dst) in enumerate(zip(far, local, strict=True))
    ]
    for copy in copies:
        copy.start()
    for copy in copies:
        copy.wait()
    (qkv_ref, out_ref, up_ref, down_ref), vectors, biases = local[:4], local[4:7], local[7:9]
    depth, width_out = qkv_ref.shape[1], out_ref.shape[2] // 2
    hidden = up_ref.shape[2] // 4
    low = core_ref[0] == 0

    def half(values):
        width = values.shape[1] // 2
        return jnp.where(low, values[:, :width], values[:, width:])

    rows_ref[...] = jnp.zeros_like(rows_ref)
    at = 0
    for layer in range(layers):
        for ref in vectors:
            rows_ref[at : at + 2, :depth] = ref[layer].astype(F32)
            at += 2
    lanes = lax.broadcasted_iota(jnp.int32, bias_ref.shape, 1)
    for ref in biases:
        bias_ref[...] = jnp.zeros_like(bias_ref)
        bias_ref[:layers, : ref.shape[1]] = ref[...].astype(F32)
        for values in (bias_ref[...], pltpu.roll(bias_ref[...], LANES - depth, 1)):
            rows_ref[at : at + layers, :] = jnp.where(lanes < depth, values, 0.0)[:layers]
            at += layers
    small = jnp.transpose(rows_ref[...])[:depth].astype(BF)
    heads, wide = [], ([], [])
    for layer in range(layers):
        qkv, out = half(qkv_ref[layer]), half(out_ref[layer])
        up, down = half(up_ref[layer]), half(down_ref[layer])
        attn = []
        for head in range(width_out // HS):
            at = head * 3 * HS
            attn += [qkv[:, at : at + 3 * HS], out[:, head * HS : (head + 1) * HS]]
        heads.append(jnp.concatenate(attn, axis=1))
        for z in (0, 1):
            at = slice(z * hidden, (z + 1) * hidden)
            wide[z].append(jnp.concatenate([up[:, at], down[:, at]], axis=1))
    for z in (0, 1):
        block = jnp.concatenate([heads[0], wide[z][0], small], axis=1)
        for owner in range(send_ref.shape[0]):
            if owner // NEAR % 2 == z:
                send_ref[owner] = block
    first = place_ref[0] == 0
    own_ref[...] = jnp.concatenate([heads[1], jnp.where(first, *wide_of(wide, 0, 1))], axis=1)
    near_ref[...] = jnp.concatenate([heads[1], jnp.where(first, *wide_of(wide, 1, 0))], axis=1)


def wide_of(wide, *at):
    return [wide[z][1] for z in at]


def spread_kernel(place_ref, own_ref, near_ref, send_ref):
    own, near = own_ref[...].astype(F32), near_ref[...].astype(F32)
    first = place_ref[0] == 0
    rows = [jnp.where(first, own, near), jnp.where(first, near, own)]
    rows = jnp.concatenate(rows, axis=0).astype(BF)
    for pair in range(send_ref.shape[0]):
        send_ref[pair] = rows


def sum_of(got_ref, columns):
    total = got_ref[0, :, columns].astype(F32)
    for sender in range(1, got_ref.shape[0]):
        total = total + got_ref[sender, :, columns].astype(F32)
    return total


def put_sums(place_ref, got_ref, own_ref, near_ref):
    depth = own_ref.shape[0]
    step = 3 * LANES
    for begin in range(0, own_ref.shape[1], step):
        at = slice(begin, begin + step)
        total = sum_of(got_ref, at)
        low, high = total[:depth], total[depth:]
        own_ref[:, at] = jnp.where(place_ref[0] == 0, low, high).astype(BF)
        near_ref[:, at] = jnp.where(place_ref[0] == 0, high, low).astype(BF)


def total_of(refs):
    mine, near = refs
    return mine[...].astype(F32) + near[...].astype(F32)


def gather_late_kernel(place_ref, got_ref, own_ref, near_ref):
    put_sums(place_ref, got_ref, own_ref, near_ref)


def gather_kernel(place_ref, got_ref, own_ref, near_ref, pad_ref):
    depth, width = own_ref.shape[0], own_ref.shape[1] - LANES
    put_sums(place_ref, got_ref, own_ref.at[:, :width], near_ref.at[:, :width])
    pad_ref[...] = jnp.zeros_like(pad_ref)
    pad_ref[: 2 * depth, :] = sum_of(got_ref, slice(width, width + LANES))
    low = jnp.transpose(pad_ref[...])[:depth]
    high = pltpu.roll(low, LANES - depth, 1)
    own_ref[:, width:] = jnp.where(place_ref[0] == 0, low, high).astype(BF)
    near_ref[:, width:] = jnp.where(place_ref[0] == 0, high, low).astype(BF)


def finish_kernel(layers, core_ref, place_ref, *rest):
    groups, rest = (rest[:4], rest[4:8]), rest[8:]
    parts, (below_ref, far_normed_ref, far_inv_std_ref, *rest) = rest[:2], rest[2:]
    hidden_ref, *rest = rest
    result_ref, grad_ref, qkv_ref, out_ref, up_ref, down_ref, *biases = rest[:8]
    normed_ref, inv_std_ref, get = rest[8:]
    get = Copies(get)
    own = pl.ds(0, normed_ref.shape[0])
    get.start(far_normed_ref.at[own, :], normed_ref)
    get.start(far_inv_std_ref.at[own, :], inv_std_ref)
    width_qkv, width_out, width_up = (r.shape[2] // 2 for r in (qkv_ref, out_ref, up_ref))
    depth, heads = qkv_ref.shape[1], width_out // HS
    attn = heads * HEAD
    low, first = core_ref[0] == 0, place_ref[0] == 0

    def both_places(own, near):
        return jnp.where(first, own, near), jnp.where(first, near, own)

    hidden = width_up // 2
    for layer, group in enumerate(groups):
        mine, core, near, core_near = (ref[:, : attn + width_up].astype(F32) for ref in group)
        attention = (mine[:, :attn] + near[:, :attn], core[:, :attn] + core_near[:, :attn])
        sides = (jnp.where(low, *attention), jnp.where(low, *attention[::-1]))
        starts = [(values, head * HEAD) for values in sides for head in range(heads)]
        qkv_ref[layer] = jnp.concatenate([v[:, at : at + 3 * HS] for v, at in starts], axis=1)
        out_ref[layer] = jnp.concatenate([v[:, at + 3 * HS : at + HEAD] for v, at in starts], axis=1)
        for z, (ours, theirs) in enumerate(
            zip(both_places(mine, near), both_places(core, core_near), strict=True)
        ):
            for side, values in enumerate((jnp.where(low, ours, theirs), jnp.where(low, theirs, ours))):
                at = side * width_up + z * hidden
                up_ref[layer, :, at : at + hidden] = values[:, attn : attn + hidden]
                down_ref[layer, :, at : at + hidden] = values[:, attn + hidden : attn + 2 * hidden]
    rows = small_sum([ref[:, attn + width_up :] for ref in groups[0]])
    at = 5 * layers
    for ref in biases:
        low_rows, high_rows = rows[at : at + layers], rows[at + layers : at + 2 * layers]
        lanes = lax.broadcasted_iota(jnp.int32, low_rows.shape, 1)
        both = jnp.where(lanes < depth, low_rows, pltpu.roll(high_rows, depth, 1))
        ref[...] = both[:, : ref.shape[1]]
        at += 2 * layers
    totals = total_of(parts)
    count = hidden_ref.shape[0]
    result_ref[...] = (hidden_ref[...] + totals[:count]).astype(BF)
    get.wait()
    total = row_norm_back(totals[count:], normed_ref[...], inv_std_ref[...])
    grad_ref[...] = (below_ref[...] + total).astype(BF)


def small_sum(parts):
    mine, core, near, core_near = (part.astype(F32) for part in parts)
    return (mine + near) + (core + core_near)


def vectors_kernel(layers, mine_ref, half_ref, bias_out_ref, gain_ref, shift_ref):
    vectors = mine_ref[...] + half_ref[...]
    depth = gain_ref.shape[2]
    for layer in range(layers):
        rows = vectors[5 * layer : 5 * layer + 5, :depth]
        bias_out_ref[layer, 0:1, :] = rows[:1]
        bias_out_ref[layer, 1:2, :] = rows[:1]
        gain_ref[layer] = rows[1:3]
        shift_ref[layer] = rows[3:5]


def call(kernel, outs, scratch, flops, *args, far=(), far_outs=(), limit=VMEM_BYTES, **more):
    def space(at, arg, far):
        if at in far:
            return pltpu.HBM
        return pltpu.SMEM if arg.shape == (1,) else pltpu.VMEM

    return pl.pallas_call(
        kernel,
        out_shape=outs,
        in_specs=[pl.BlockSpec(memory_space=space(at, arg, far)) for at, arg in enumerate(args)],
        out_specs=[
            pl.BlockSpec(memory_space=space(at, out, far_outs)) for at, out in enumerate(outs)
        ],
        scratch_shapes=scratch,
        compiler_params=pltpu.CompilerParams(vmem_limit_bytes=limit),
        cost_estimate=pl.CostEstimate(flops=flops, bytes_accessed=8_000_000, transcendentals=0),
        **more,
    )(*args)


def core_rows_summed(kept, sent):
    return (kept.astype(F32) + other_core(sent).astype(F32)).astype(BF)


def turned_groups(values):
    return values.reshape(2, -1, values.shape[1])[::-1].reshape(values.shape)


def pair_sum(mine):
    theirs = turned_groups(near_other_half(mine))
    return (mine.astype(F32) + theirs.astype(F32)).astype(BF)


def other_rows(mine, near):
    return other_core((mine.astype(F32) + turned_groups(near).astype(F32)).astype(BF))


def own_parts(*mines):
    count = mines[0].shape[0] // 2
    own = jnp.concatenate([mine[:count] for mine in mines])
    return own, near_group(jnp.concatenate([mine[count:] for mine in mines]))


def rotation(positions):
    exponents = jnp.arange(ROT // 2, dtype=F32) * (2.0 / ROT)
    inverse = jnp.power(10000.0, -exponents)
    phase = positions.astype(F32)[:, None] * inverse[None, :]
    cos, sin = jnp.cos(phase), jnp.sin(phase)
    none = jnp.zeros_like(sin)
    rest = jnp.zeros((positions.shape[0], HS - ROT), F32)
    tables = [[cos, cos, rest + 1.0], [-sin, none, rest], [none, sin, rest]]
    return jnp.stack([jnp.concatenate(t + t, axis=1) for t in tables])


def bias_places(owners, depth, starts, widths, shards):
    owner = jnp.arange(owners * depth, dtype=jnp.int32) // depth
    inner = jnp.arange(owners * depth, dtype=jnp.int32) % depth
    rows = []
    for start, width, shard, head in zip(starts, widths, shards, (3 * HS, None), strict=True):
        for first in (0, depth):
            at = owner * shard + inner + first - start
            fits = (inner + first < shard) & (at >= 0) & (at < width)
            if head is not None:
                at = at // head * HEAD + at % head
            rows.append(jnp.where(fits, at, -1))
    return jnp.stack(rows + rows)


def per_device(
    tokens,
    cotangent,
    doc_lens,
    block_pos,
    w_qkv,
    w_out,
    w_up,
    w_down,
    b_qkv,
    b_up,
    out_bias,
    norm_gain,
    norm_bias,
):
    row_count = tokens.shape[0]
    block_rows = row_count // 2
    core = lax.axis_index("ctx")
    owners = lax.axis_size("fsdp")
    layers, depth, width_qkv = w_qkv.shape
    width_qkv, width_out, hidden = width_qkv // 2, w_out.shape[1] // 2, w_up.shape[2] // 4
    place_z = lax.axis_index("fsdp") // NEAR % 2
    heads = width_out // HS
    attn = heads * HEAD
    width = attn + 2 * hidden
    wide = owners * depth
    rows = 4 * row_count

    core_at = core.astype(jnp.int32).reshape(1)
    place_at = place_z.astype(jnp.int32).reshape(1)
    sds = jax.ShapeDtypeStruct
    raw = (
        w_qkv,
        w_out.transpose(0, 2, 1),
        w_up,
        w_down.transpose(0, 2, 1),
        out_bias,
        norm_gain,
        norm_bias,
        b_qkv,
        b_up,
    )
    send, own_block, near_block = call(
        functools.partial(slabs_kernel, layers),
        (
            sds((owners, depth, width + LANES), BF),
            sds((depth, width), BF),
            sds((depth, width), BF),
        ),
        [pltpu.VMEM(a.shape, a.dtype) for a in raw]
        + [pltpu.VMEM((LANES, LANES), F32), pltpu.VMEM((8, LANES), F32)]
        + [pltpu.SemaphoreType.DMA((len(raw),))],
        1000,
        core_at,
        place_at,
        *raw,
        far=range(2, 2 + len(raw)),
    )
    starts, ends = ((own, near_other_half(own)) for own in (tokens, cotangent))
    starts, ends = ((o, other_core(o), n, other_core(n)) for o, n in (starts, ends))
    first = exchanged(send).reshape(wide, -1)
    near_rows, starts, ends = lax.optimization_barrier((near_group(near_block), starts, ends))
    (second,) = call(
        spread_kernel,
        (sds((owners // 2, 2 * depth, width), BF),),
        [],
        100_000_000,
        place_at,
        own_block,
        near_rows,
    )
    second = owners_in_order(exchanged_in_plane(second), owners)
    offsets = jnp.arange(block_rows, dtype=jnp.int32)
    positions = (block_pos[0][:, None] * block_rows + offsets[None, :]).reshape(2, row_count)
    positions = jnp.where(core == 0, positions, positions[::-1]).reshape(-1)
    doc_ends = jnp.cumsum(doc_lens[0])
    docs = jnp.sum((positions[:, None] >= doc_ends[None, :]).astype(jnp.int32), axis=1)
    allowed = (docs[:, None] == docs[None, :]) & (positions[None, :] <= positions[:, None])
    mask = jnp.where(allowed, 0.0, MASKED).astype(F32)
    table = rotation(positions)
    place = bias_places(
        owners,
        depth,
        (core * width_qkv, (2 * core + place_z) * hidden),
        (width_qkv, hidden),
        (b_qkv.shape[1], b_up.shape[1]),
    )

    flops = 2 * rows * wide * width
    part = sds((rows // 2, wide), BF)
    kept = State.shapes(rows, wide, heads, hidden)

    def vmem(*arrays):
        return [pltpu.VMEM(array.shape, array.dtype) for array in arrays]

    def copies(*counts):
        return [pltpu.SemaphoreType.DMA((count,)) for count in counts]

    slab_scratch = [
        pltpu.VMEM((wide, attn), BF),
        pltpu.VMEM((wide, 2 * hidden), BF),
        pltpu.SemaphoreType.DMA((3,)),
    ]
    kept_part, sent_part, vec, *state = call(
        functools.partial(first_kernel, layers),
        (part, part, sds((layers, VECTORS, wide), F32), *State.shapes(rows, wide, heads, hidden)),
        [
            *vmem(part, part, table, mask),
            *copies(2, 12),
            pltpu.VMEM((rows, wide), F32),
            pltpu.VMEM((wide, LANES), BF),
            *slab_scratch,
            *vmem(*kept),
        ],
        flops,
        *starts,
        first,
        place,
        table,
        mask,
        far=(4, 6, 7),
        far_outs=(0, 1, *range(3, 13)),
    )
    mine = pair_sum(core_rows_summed(kept_part, sent_part))
    mine, near, second = lax.optimization_barrier((mine, near_group(mine), second))
    scratch = [
        pltpu.VMEM((rows, wide), BF),
        pltpu.VMEM((rows, hidden), BF),
        pltpu.VMEM((rows // 2, attn), BF),
        pltpu.VMEM((rows, wide), F32),
        pltpu.VMEM((rows, wide), F32),
    ]
    *sums, slab, later_sums, result, normed, inv_std = call(
        functools.partial(last_kernel, owners),
        (
            *(part,) * 4,
            sds((wide, width), BF),
            sds((8, wide), F32),
            sds((row_count, wide), F32),
            *kept[:2],
        ),
        [
            *vmem(table, mask, sds((row_count, wide), F32)),
            *copies(6, 10),
            *vmem(part, part, part, part, *kept, sds((rows, wide), BF)),
            *slab_scratch,
            *scratch,
        ],
        3 * flops,
        *starts,
        *ends,
        mine,
        near,
        other_rows(mine, near),
        vec,
        second,
        table,
        mask,
        far=(4, 5, 6, 7, 12, 13, 14),
        far_outs=(0, 1, 2, 3, 4, 6, 7, 8),
    )
    mine, slab = lax.optimization_barrier((core_rows_summed(*sums[2:]), slab))
    later = exchanged_in_plane(slab.reshape(owners // 2, -1, width))
    ahead, mine = lax.optimization_barrier((sums[:2], pair_sum(mine)))
    near = near_group(mine)
    ahead = pair_sum(core_rows_summed(*ahead))
    kept_part, sent_part, slab, grad_below = call(
        functools.partial(back_kernel, layers, owners),
        (part, part, sds((wide, width + LANES), BF), sds((row_count, wide), F32)),
        [
            *vmem(table),
            *copies(11, 5),
            *vmem(part, part, *kept, later_sums, sds((rows, wide), F32)),
            *vmem(sds((wide, LANES), BF)),
            *slab_scratch,
            *scratch,
        ],
        2 * flops,
        *ends,
        mine,
        near,
        other_rows(mine, near),
        normed,
        inv_std,
        later_sums,
        vec,
        first,
        place,
        table,
        *state,
        far=(11, *range(13, 24)),
        far_outs=(0, 1, 2),
    )
    slab, later, ahead = lax.optimization_barrier((slab, later, ahead))
    earlier = exchanged_in_plane(slab.reshape(owners // 2, -1, width + LANES))
    below = pair_sum(core_rows_summed(kept_part, sent_part))

    piece = sds((depth, width), BF)
    late = call(gather_late_kernel, (piece, piece), [], flops // 8, place_at, later)
    ends = own_parts(ahead, below)

    def of_all(own, near):
        return own, other_core(own), near_group(near), near_other_core(near)

    late = of_all(*late)
    earlier, late, ends = lax.optimization_barrier((earlier, late, ends))
    piece = sds((depth, width + LANES), BF)
    early = of_all(
        *call(
            gather_kernel, (piece, piece), [pltpu.VMEM((LANES, LANES), F32)], 1000, place_at, earlier
        )
    )
    small = small_sum([part[:, width:] for part in early])
    half = other_half(small)
    result, grad_tokens, grad_qkv, grad_out, grad_up, grad_down, grad_b_qkv, grad_b_up = call(
        functools.partial(finish_kernel, layers),
        (sds(tokens.shape, BF),) * 2
        + tuple(
            sds(shape, F32)
            for shape in (
                w_qkv.shape,
                (layers, depth, w_out.shape[1]),
                w_up.shape,
                (layers, depth, w_down.shape[1]),
                b_qkv.shape,
                b_up.shape,
            )
        ),
        [*vmem(sds((row_count, wide), F32), sds((row_count, 1), F32)), *copies(2)],
        flops // 8,
        core_at,
        place_at,
        *early,
        *late,
        *ends,
        grad_below,
        state[0],
        state[1],
        result,
        far=(13, 14),
    )
    vectors = call(
        functools.partial(vectors_kernel, layers),
        tuple(sds(a.shape, F32) for a in (out_bias, norm_gain, norm_bias)),
        [],
        1000,
        small,
        half,
    )
    return (
        result,
        grad_tokens,
        grad_qkv,
        grad_out.transpose(0, 2, 1),
        grad_up,
        grad_down.transpose(0, 2, 1),
        grad_b_qkv,
        grad_b_up,
        *vectors,
    )


def solution(mesh):
    in_specs = (
        P(("fsdp", "ctx"), None),
        P(("fsdp", "ctx"), None),
        P("fsdp", None),
        P("fsdp", None),
        P(None, "fsdp", "tp"),
        P(None, "tp", "fsdp"),
        P(None, "fsdp", "tp"),
        P(None, "tp", "fsdp"),
        P(None, ("tp", "fsdp")),
        P(None, ("tp", "fsdp")),
        P(None, None, "fsdp"),
        P(None, None, "fsdp"),
        P(None, None, "fsdp"),
    )
    out_specs = (P(("fsdp", "ctx"), None), P(("fsdp", "ctx"), None), *in_specs[4:])
    return jax.shard_map(
        per_device, mesh=mesh, in_specs=in_specs, out_specs=out_specs, check_vma=False
    )
```
